128 devices in a mesh: sub: 32 (over y, x, core), grp: 4 (over z).
Axes of the slice: x: 4, y: 4, z: 4, core: 2. Of those that a mesh axis runs over, the one named last changes fastest.
Arguments:
- inverse_blocks: bfloat16 [128, 2304, 2304], P(('sub', 'grp'))
- primal_loads: bfloat16 [128, 2304, 128], P(('sub', 'grp'))
- mortar_values: bfloat16 [128, 768, 768], P(('sub', 'grp')), may hold values from -1.5 to 1.5
- segment_ids: int32 [128, 768], P(('sub', 'grp')), may hold values from 0 to 47, never falling along the last dimension, each value on 1 to 32 neighbouring positions
- slave_weights: float32 [128, 768], P(('sub', 'grp')), may hold values from 0.5 to 2
- rigid_modes: float32 [128, 6, 1536], P(('sub', 'grp')), may hold values from -6 to 6
- coarse_inverse: float32 [768, 768], P(('sub', 'grp')), as said below
- candidates: int32 [128, 384], P(('sub', 'grp')), may hold values from 0 to 767, as said below
- start_multipliers: float32 [128, 768, 128], P(('sub', 'grp')), may hold values from -6 to 6
Outputs:
- multipliers: float32 [128, 768, 128], P(('sub', 'grp'))
- gradient: float32 [128, 768, 128], P(('sub', 'grp'))
The draws below stay inside these ranges and needn't reach their ends.
Inputs may be any that keep to these rules, and one draw needn't show every extreme that they name: `segment_ids`: along each row the block numbers never fall, and each block has 1 to 32 multipliers. The candidates of one subdomain are distinct. coarse_inverse is symmetric.
All inputs are finite; a program needn't handle non-finite values.
Results may differ from the reference program's by a relative error of at most 0.0075.
Values may be sent and summed in bfloat16 or wider, within the bound.
No kernel may reach another device: no remote copies, remote signals or barrier semaphores. Data moves between devices by JAX's collectives and lax.ppermute only.
A program may use at most 64 MiB of HBM per device.

```python
import math
import jax
import jax.numpy as jnp
import numpy as np
from jax import lax

NB = 2304
MS = 768
LC = 128
NR = 6
STEPS = 3
SEG_MOST = 32
SEG_COUNT = 48
CAND = 384
SUBS = 128
NC = 768
N_SUB = 32
N_GRP = 4


def draw_inverse_blocks(key, part):
    key = jax.random.fold_in(key, 11)
    key_off, key_diag, key_pair = jax.random.split(key, 3)
    noise = jax.random.normal(key_off, (SUBS, NB, NB), jnp.float32) * (0.25 / NB ** 0.5)
    diag_vals = jax.random.uniform(key_diag, (SUBS, NB, 1), jnp.float32, 2.2, 3.0)
    pair_vals = jax.random.uniform(key_pair, (SUBS, MS), jnp.float32, 1.0, 1.5)
    pair_full = jnp.concatenate([pair_vals, pair_vals * 0.0, pair_vals], axis=1)[:, :, None]
    rows = jnp.arange(NB)[:, None]
    cols = jnp.arange(NB)[None, :]
    ident = (rows == cols).astype(jnp.float32)
    coupled = (jnp.abs(rows - cols) == 2 * MS).astype(jnp.float32)
    drawn = 1.0 - ident - coupled
    return (noise * drawn + ident * diag_vals + coupled * pair_full).astype(jnp.bfloat16)


def draw_primal_loads(key, part):
    key = jax.random.fold_in(key, 12)
    key_noise, key_rows = jax.random.split(key, 2)
    ramp = 1.0 + 2.0 * jnp.arange(SUBS, dtype=jnp.float32) / (SUBS - 1)
    row_scale = 10.0 ** jax.random.uniform(key_rows, (SUBS, NB, 1), jnp.float32, -0.5, 0.5)
    noise = jax.random.normal(key_noise, (SUBS, NB, LC), jnp.float32)
    return (noise * row_scale * ramp[:, None, None]).astype(jnp.bfloat16)


def draw_mortar_values(key, part):
    key = jax.random.fold_in(key, 15)
    key_off, key_diag = jax.random.split(key)
    noise = jax.random.normal(key_off, (SUBS, MS, MS), jnp.float32) * 0.15
    diag_vals = jax.random.uniform(key_diag, (SUBS, MS, 1), jnp.float32, 0.7, 1.3)
    ident = (jnp.arange(MS)[:, None] == jnp.arange(MS)[None, :]).astype(jnp.float32)
    return jnp.clip(noise * (1.0 - ident) + ident * diag_vals, -1.5, 1.5).astype(jnp.bfloat16)


def draw_start_multipliers(key, part):
    key = jax.random.fold_in(key, 16)
    key_base, key_common = jax.random.split(key)
    base = jax.random.normal(key_base, (SUBS, MS, LC), jnp.float32)
    common = jax.random.normal(key_common, (MS, LC), jnp.float32)
    parity = 1.0 - 2.0 * (jnp.arange(SUBS) // N_GRP % 2).astype(jnp.float32)
    return jnp.clip(base + 1.2 * parity[:, None, None] * common[None], -6.0, 6.0)


def draw_coarse_inverse(key, part):
    key = jax.random.fold_in(key, 13)
    key_off, key_diag = jax.random.split(key)
    noise = jax.random.normal(key_off, (NC, NC), jnp.float32)
    sym = (noise + noise.T) * (1.5 / (2.0 * NC) ** 0.5)
    diag_vals = jax.random.uniform(key_diag, (NC,), jnp.float32, 2.0, 6.0)
    ident = (jnp.arange(NC)[:, None] == jnp.arange(NC)[None, :]).astype(jnp.float32)
    return (sym * (1.0 - ident) + ident * diag_vals[None, :]) / (2.0 * MS)


def pick_some(one_key):
    return jax.random.permutation(one_key, MS)[:CAND]


def draw_candidates(key, part):
    key = jax.random.fold_in(key, 14)
    keys = jax.random.split(key, SUBS)
    return jax.vmap(pick_some)(keys).astype(jnp.int32)


def levels(key, extent, cuts, least, largest):
    factor_of = 1.0
    for position, blocks in cuts:
        steps = jax.random.uniform(jax.random.fold_in(jax.random.fold_in(key, 6), position), (blocks,), jnp.float32, least / len(cuts), largest / len(cuts))
        factor_of = factor_of * jnp.repeat(jnp.exp(steps), extent[position] // blocks).reshape((-1,) + (1,) * (len(extent) - 1 - position))
    return factor_of


def profile(count, total, reach, slope):
    weights = [(1 << 20) // math.isqrt(rank ** slope) + 1 for rank in range(2, count + 1)]
    rest, holding = total - reach - (count - 1), [1] * (count - 1)
    while rest > 0:
        free = [i for i in range(count - 1) if holding[i] < reach]
        whole, remaining = sum([weights[i] for i in free]), rest
        for i in free:
            extra = min(reach - holding[i], max(1, remaining * weights[i] // whole), rest)
            holding[i] = holding[i] + extra
            rest = rest - extra
    return np.array([reach] + holding)


def ragged(rng, amount, total, most, lean):
    if amount == 2:
        one = jax.random.randint(rng, (), max(1, total - most), min(most, total - 1) + 1)
        return jnp.stack([one, total - one])
    tallies = jnp.asarray(profile(amount, total, most, lean), jnp.int32)
    twos = (amount - 1) // 2
    giver, sink = tallies[1:1 + 2 * twos:2], tallies[2:2 + 2 * twos:2]
    slack = jnp.minimum(giver - 1, most - sink)
    passed = jax.random.randint(jax.random.fold_in(rng, 1), (twos,), 0, 1 << 20) % (slack + 1)
    tallies = tallies.at[1:1 + 2 * twos:2].set(giver - passed).at[2:2 + 2 * twos:2].set(sink + passed)
    return tallies[jax.random.permutation(jax.random.fold_in(rng, 2), amount)]


def normal_values(key, extent, width, bound, cuts=(), held_as=jnp.bfloat16):
    level = levels(key, extent, cuts, -0.22, 0.18) if cuts else 1.0
    drawn = jax.random.normal(key, extent, jnp.float32) * width * level
    return jnp.minimum(jnp.maximum(drawn, -bound), bound).astype(held_as)


def setup_inputs(seed: int = 0) -> dict:
    key_list = jax.random.split(jax.random.key(seed), 10)
    return {
        "inverse_blocks": draw_inverse_blocks(jax.random.fold_in(key_list[9], 71), 0),
        "primal_loads": draw_primal_loads(jax.random.fold_in(key_list[9], 71), 0),
        "mortar_values": draw_mortar_values(jax.random.fold_in(key_list[9], 71), 0),
        "segment_ids": jax.vmap(lambda own: jnp.searchsorted(jnp.cumsum(ragged(own, SEG_COUNT, MS, SEG_MOST, 2)), jnp.arange(MS), side="right"))(jax.random.split(key_list[3], SUBS)).reshape((SUBS, MS)).astype(jnp.int32),
        "slave_weights": jnp.clip(jnp.exp(math.log(2.0) - 1.3862944 * jax.random.uniform(key_list[4], (SUBS, MS), jnp.float32) ** levels(key_list[4], (SUBS, MS), ((0, 128),), -0.2, 0.2)), 0.5, 2.0),
        "rigid_modes": normal_values(key_list[5], (SUBS, NR, 2 * MS), 1.0, 6.0, ((0, 128),), jnp.float32),
        "coarse_inverse": draw_coarse_inverse(jax.random.fold_in(key_list[9], 71), 0),
        "candidates": draw_candidates(jax.random.fold_in(key_list[9], 71), 0),
        "start_multipliers": draw_start_multipliers(jax.random.fold_in(key_list[9], 71), 0),
    }


def cycle_next(values):
    shaped = values.reshape((N_SUB, N_GRP) + values.shape[1:])
    return jnp.roll(shaped, -1, axis=0).reshape(values.shape)

def cycle_prev(values):
    shaped = values.reshape((N_SUB, N_GRP) + values.shape[1:])
    return jnp.roll(shaped, 1, axis=0).reshape(values.shape)

def reference(inverse_blocks, primal_loads, mortar_values, segment_ids, slave_weights, rigid_modes, coarse_inverse, candidates, start_multipliers):
    width_m = MS
    same_block = segment_ids[:, :, None] == segment_ids[:, None, :]
    mortar = jnp.where(same_block, mortar_values, jnp.zeros((), jnp.bfloat16))
    mortar_wide = mortar.astype(jnp.float32)
    weights = slave_weights[:, :, None]
    positions = jnp.arange(width_m, dtype=jnp.int32)
    clip_mask = jnp.any(candidates[:, :, None] == positions[None, None, :], axis=1)[:, :, None]

    def incoming_push(field):
        field_bf = field.astype(jnp.bfloat16).astype(jnp.float32)
        pushed = jnp.einsum('sij,sic->sjc', mortar_wide, field_bf).astype(jnp.bfloat16)
        return cycle_prev(pushed)

    def jump(master, slave):
        following = cycle_next(master).astype(jnp.float32)
        return weights * slave.astype(jnp.float32) - jnp.einsum('sij,sjc->sic', mortar_wide, following)

    def solve_blocks(loads):

        def one_block(pair):
            return jnp.dot(pair[0], pair[1], preferred_element_type=jnp.float32).astype(jnp.bfloat16)
        return lax.map(one_block, (inverse_blocks, loads))

    def dual_grad(field):
        incoming = incoming_push(field).astype(jnp.float32)
        loads_wide = primal_loads.astype(jnp.float32)
        master = (-incoming - loads_wide[:, :width_m]).astype(jnp.bfloat16)
        middle = -primal_loads[:, width_m:2 * width_m]
        slave = (weights * field - loads_wide[:, 2 * width_m:]).astype(jnp.bfloat16)
        traces = solve_blocks(jnp.concatenate([master, middle, slave], axis=1))
        return jump(traces[:, :width_m], traces[:, 2 * width_m:])

    def dual_apply(field):
        incoming = incoming_push(field)
        middle = jnp.zeros_like(incoming)
        slave = (weights * field).astype(jnp.bfloat16)
        traces = solve_blocks(jnp.concatenate([-incoming, middle, slave], axis=1))
        return jump(traces[:, :width_m], traces[:, 2 * width_m:])

    def project(field):
        incoming = incoming_push(field).astype(jnp.float32)
        high = lax.Precision.HIGHEST
        resid = jnp.einsum('skm,smc->skc', rigid_modes[:, :, :width_m], -incoming, precision=high)
        resid = resid + jnp.einsum('skm,smc->skc', rigid_modes[:, :, width_m:], weights * field, precision=high)
        coeffs = jnp.dot(coarse_inverse, resid.reshape(NC, LC), precision=high).reshape(SUBS, NR, LC)
        modes = jnp.einsum('skm,skc->smc', rigid_modes, coeffs, precision=high).astype(jnp.bfloat16)
        return field - jump(modes[:, :width_m], modes[:, width_m:])
    multipliers = start_multipliers
    gradient = dual_grad(multipliers)
    for iteration in range(STEPS):
        direction = project(gradient)
        curved = dual_apply(direction)
        norm_sq = lax.optimization_barrier(jnp.sum(direction * direction, axis=(0, 1)))
        curve_sq = lax.optimization_barrier(jnp.sum(direction * curved, axis=(0, 1)))
        moved = multipliers - (norm_sq / curve_sq)[None, None, :] * direction
        multipliers = jnp.where(clip_mask, jnp.maximum(moved, 0.0), moved)
        gradient = dual_grad(multipliers)
    return (multipliers, gradient)
```

```python
import jax
import jax.numpy as jnp
from jax import lax
from jax.sharding import PartitionSpec as P

STEPS = 3
HIGH = lax.Precision.HIGHEST
AXES = ("sub", "grp")


def shifted(block, distance):
    size = lax.axis_size("sub")
    return lax.ppermute(block, "sub", [((i - distance) % size, i) for i in range(size)])


def gathered(block):
    count = lax.axis_size("sub") * lax.axis_size("grp")
    copies = jnp.broadcast_to(block[None], (count,) + block.shape)
    return lax.all_to_all(copies, AXES, 0, 0, tiled=True)


def across(left, right, dims, **kw):
    return lax.dot_general(left, right, ((dims[:1], dims[1:]), ((), ())), **kw)


def on_device(
    inverse_blocks,
    primal_loads,
    mortar_values,
    segment_ids,
    slave_weights,
    rigid_modes,
    coarse_inverse,
    candidates,
    start_multipliers,
):
    f32, bf16 = jnp.float32, jnp.bfloat16
    ms = mortar_values.shape[1]
    nr = rigid_modes.shape[1]
    kinv = inverse_blocks[0]
    loads = primal_loads[0]
    seg = segment_ids[0]
    same_block = seg[:, None] == seg[None, :]
    mortar = jnp.where(same_block, mortar_values[0], jnp.zeros((), bf16))
    weights = slave_weights[0][:, None]
    rigid = rigid_modes[0]
    positions = jnp.arange(ms, dtype=jnp.int32)
    clipped = jnp.any(candidates[0][:, None] == positions[None, :], axis=0)[:, None]
    field = start_multipliers[0]

    def mul(matrix, values):
        return jnp.dot(matrix, values.astype(bf16), preferred_element_type=f32)

    def mul_t(matrix, values):
        return across(matrix, values.astype(bf16), (0, 0), preferred_element_type=f32)

    push = shifted(mul_t(mortar, field).astype(bf16), 1)
    mortar_p = shifted(mortar, 1)
    side = jnp.concatenate([weights.T, clipped.T.astype(f32), rigid[:, ms:]], axis=0)
    side_p = shifted(side, 1)
    weights_p = side_p[0][:, None]
    clipped_p = side_p[1][:, None] > 0
    field_p = shifted(field, 1)
    rigid_n = shifted(rigid[:, :ms], -1)
    coarse = jnp.concatenate(
        [shifted(coarse_inverse, 1), coarse_inverse, shifted(coarse_inverse, -1)], axis=0
    )

    slave_p = weights_p * side_p[2:].T
    slave_s = weights * rigid[:, ms:].T
    wide, wide_p = mortar.astype(f32), mortar_p.astype(f32)
    master_s = jnp.dot(wide_p, rigid[:, :ms].T, precision=HIGH)
    master_n = jnp.dot(wide, rigid_n.T, precision=HIGH)
    none = jnp.zeros((ms, nr), f32)
    modes = jnp.concatenate([none, slave_s, -master_n], axis=1)
    modes_p = jnp.concatenate([slave_p, -master_s, none], axis=1)
    from_master = -across(modes_p, wide_p, (0, 0), precision=HIGH)
    from_slave = (modes * weights).T
    resid_of = jnp.concatenate([from_master, from_slave], axis=1)

    sub, grp = lax.axis_size("sub"), lax.axis_size("grp")
    blocks = coarse.reshape(3 * nr, sub, grp, nr)
    pieces = jnp.stack(
        [jnp.roll(blocks, 1, axis=1), blocks, jnp.roll(blocks, -1, axis=1)], axis=3
    )
    coarse_of = pieces.reshape(3 * nr, sub * grp * 3 * nr)

    kff = jnp.concatenate(
        [
            jnp.concatenate([kinv[:ms, :ms], kinv[:ms, 2 * ms :]], axis=1),
            jnp.concatenate([kinv[2 * ms :, :ms], kinv[2 * ms :, 2 * ms :]], axis=1),
        ],
        axis=0,
    )
    middle = jnp.concatenate([kinv[:ms, ms : 2 * ms], kinv[2 * ms :, ms : 2 * ms]], axis=0)
    fixed = -jnp.dot(middle, loads[ms : 2 * ms], preferred_element_type=f32)
    loads_m = loads[:ms].astype(f32)
    loads_s = loads[2 * ms :].astype(f32)

    def solve(push, field):
        load = jnp.concatenate(
            [
                (-push.astype(f32) - loads_m).astype(bf16),
                (weights * field - loads_s).astype(bf16),
            ],
            axis=0,
        )
        return (jnp.dot(kff, load, preferred_element_type=f32) + fixed).astype(bf16)

    traces = solve(push, field)
    for _ in range(STEPS):
        from_n = shifted(traces[:ms], -1)
        from_p = shifted(traces[ms:], 1)
        resid = jnp.dot(resid_of, traces.astype(f32), precision=HIGH).astype(bf16)
        every = gathered(resid).reshape(-1, resid.shape[1]).astype(f32)
        gradient = weights * traces[ms:].astype(f32) - mul(mortar, from_n)
        gradient_p = weights_p * from_p.astype(f32) - mul(mortar_p, traces[:ms])
        coeffs = jnp.dot(coarse_of, every, precision=HIGH)
        direction = gradient - jnp.dot(modes, coeffs, precision=HIGH)
        direction_p = gradient_p - jnp.dot(modes_p, coeffs, precision=HIGH)
        load = jnp.concatenate(
            [(-mul_t(mortar_p, direction_p)).astype(bf16), (weights * direction).astype(bf16)],
            axis=0,
        )
        curved = jnp.dot(kff, load, preferred_element_type=f32)
        sums = jnp.stack(
            [jnp.sum(direction * direction, axis=0), jnp.sum(load.astype(f32) * curved, axis=0)]
        )
        totals = jnp.sum(gathered(sums), axis=0)
        step = (totals[0] / totals[1])[None, :]
        moved = field - step * direction
        field = jnp.where(clipped, jnp.maximum(moved, 0.0), moved)
        moved_p = field_p - step * direction_p
        field_p = jnp.where(clipped_p, jnp.maximum(moved_p, 0.0), moved_p)
        traces = solve(mul_t(mortar_p, field_p).astype(bf16), field)
    from_n = shifted(traces[:ms], -1)
    gradient = weights * traces[ms:].astype(f32) - mul(mortar, from_n)
    return (field[None], gradient[None])


def solution(mesh):
    placed = (
        P(AXES, None, None),
        P(AXES, None, None),
        P(AXES, None, None),
        P(AXES, None),
        P(AXES, None),
        P(AXES, None, None),
        P(AXES, None),
        P(AXES, None),
        P(AXES, None, None),
    )
    return jax.shard_map(
        on_device,
        mesh=mesh,
        in_specs=placed,
        out_specs=(P(AXES, None, None), P(AXES, None, None)),
        check_vma=False,
    )
```

```python
import jax
import jax.numpy as jnp
import numpy as np
from jax import lax
from jax.experimental import pallas as pl
from jax.experimental.pallas import tpu as pltpu
from jax.sharding import PartitionSpec as P

STEPS = 3
AXES = ("sub", "grp")
F32, BF16 = jnp.float32, jnp.bfloat16
TILE = 128
TILE_ROWS = 192
HALO = 32
MIB = 1 << 20


def shifted(block, distance):
    size = lax.axis_size("sub")
    return lax.ppermute(block, "sub", [((i - distance) % size, i) for i in range(size)])


def swapped(block):
    size = lax.axis_size("sub")
    return lax.ppermute(block, "sub", [(i ^ 1, i) for i in range(size)])


def dot(left, right):
    return jnp.dot(left, right, preferred_element_type=F32)


def halves(value):
    high = value.astype(BF16).astype(F32)
    return high, (value - high).astype(BF16).astype(F32)


def column(row):
    return jnp.broadcast_to(row, (TILE, row.shape[1])).T


def mortar_times(tiles, values):
    count = values.shape[0] // TILE
    rows = TILE + 2 * HALO
    parts = [
        dot(tiles[rows * t : rows * (t + 1), :], values[TILE * t : TILE * (t + 1)])
        for t in range(count)
    ]
    out = []
    none = jnp.zeros((HALO, values.shape[1]), F32)
    for t in range(count):
        before = parts[t - 1][TILE + HALO :] if t else none
        after = parts[t + 1][TILE : TILE + HALO] if t + 1 < count else none
        gap = jnp.zeros((TILE - 2 * HALO, values.shape[1]), F32)
        out.append(parts[t][:TILE] + jnp.concatenate([before, gap, after], axis=0))
    return jnp.concatenate(out, axis=0)


def mortar_t_times(tiles_t, values):
    count = values.shape[0] // TILE
    none = jnp.zeros((HALO, values.shape[1]), BF16)
    fill = jnp.zeros((TILE - 2 * HALO, values.shape[1]), BF16)
    out = []
    for t in range(count):
        low, high = TILE * t, TILE * (t + 1)
        before = values[low - HALO : low] if t else none
        after = values[high : high + HALO] if t + 1 < count else none
        window = jnp.concatenate([values[low:high], before, after, fill], axis=0)
        out.append(dot(tiles_t[TILE * t : TILE * (t + 1), :], window))
    return jnp.concatenate(out, axis=0)


def unpacked(pack, t):
    edge = pack[160 * t : 160 * t + HALO, :].astype(F32)
    lane = lax.broadcasted_iota(jnp.int32, edge.shape, 1)
    above = jnp.where(lane < TILE // 2, edge, 0.0)
    below = jnp.where(lane < TILE // 2, 0.0, edge)
    middle = pack[160 * t + HALO : 160 * (t + 1), :].astype(F32)
    return jnp.concatenate([middle, above, below], axis=0)


def with_fill(tile):
    return jnp.concatenate([tile, jnp.zeros((TILE - 2 * HALO, TILE), F32)], axis=0)


class Moves:
    def __init__(self, sems):
        self.sems, self.used = sems, 0

    def start(self, source, target):
        copy = pltpu.make_async_copy(source, target, self.sems.at[self.used])
        self.used += 1
        copy.start()
        return copy


CHUNK = 256
SIDE = 32


def start_faces(moves, kinv, held, ms):
    copies = []
    for r in range(2 * ms // CHUNK):
        row = r * CHUNK + (ms if r * CHUNK >= ms else 0)
        pair = []
        for to, at in ((0, 0), (ms, 2 * ms)):
            pair.append(
                moves.start(
                    kinv.at[pl.ds(row, CHUNK), pl.ds(at, ms)],
                    held.at[pl.ds(r * CHUNK, CHUNK), pl.ds(to, ms)],
                )
            )
        copies.append(pair)
    return copies


def solved(copies, held, load, fixed, um, us, ms):
    for r, pair in enumerate(copies):
        for copy in pair:
            copy.wait()
        row = r * CHUNK
        u = (dot(held[row : row + CHUNK, :], load) + fixed[row : row + CHUNK, :]).astype(BF16)
        if row < ms:
            um[row : row + CHUNK, :] = u
        else:
            us[row - ms : row - ms + CHUNK, :] = u


def residual(zt, um, us, ms):
    both = dot(zt[:, :ms], um[...]) + dot(zt[:, ms:], us[...])
    return both[:24] + both[24:]


def loads_of(push, scaled, loads_m, loads_s):
    master = (-push.astype(F32) - loads_m.astype(F32)).astype(BF16)
    slave = (scaled - loads_s.astype(F32)).astype(BF16)
    return jnp.concatenate([master, slave], axis=0)


def pack_kernel(mortar, seg, field, rigid, coarse, weights, cand, out, behind):
    ms = mortar.shape[0]
    nr = rigid.shape[0]
    count = ms // TILE
    ids = seg[...].astype(F32)
    ids_col = column(ids)
    none = jnp.zeros((HALO, TILE), F32)

    def masked(low, high, t):
        own = slice(TILE * t, TILE * (t + 1))
        same = ids_col[low:high] == ids[:, own]
        return jnp.where(same, mortar[low:high, own].astype(F32), 0.0)

    tiles = []
    for t in range(count):
        low, high = TILE * t, TILE * (t + 1)
        middle = masked(low, high, t)
        above = masked(low - HALO, low, t) if t else none
        below = masked(high, high + HALO, t) if t + 1 < count else none
        out[160 * t : 160 * t + HALO, :] = (above + below).astype(BF16)
        out[160 * t + HALO : 160 * (t + 1), :] = middle.astype(BF16)
        tile = jnp.concatenate([middle, above, below], axis=0)
        tiles.append(with_fill(tile).T.astype(BF16))
    push = mortar_t_times(jnp.concatenate(tiles, axis=0), field[...].astype(BF16))
    out[160 * count : 160 * count + ms, :] = push.astype(BF16)

    behind[...] = jnp.zeros_like(behind)
    behind[0:nr, :] = rigid[:, :ms]
    behind[8 : 8 + nr, :] = coarse[...]
    for t in range(count):
        own = slice(TILE * t, TILE * (t + 1))
        chosen = jnp.zeros((1, TILE), F32)
        if TILE * (t + 1) <= cand.shape[1]:
            chosen = cand[:, own].astype(F32)
        lanes = slice(ms + TILE * t, ms + TILE * (t + 1))
        pad = jnp.zeros((8 - nr, TILE), F32)
        rows = [rigid[:, lanes], pad, coarse[:, own], pad, weights[:, own], chosen]
        value = jnp.concatenate(rows + [jnp.zeros((SIDE - 18, TILE), F32)], axis=0)
        high, low = halves(value)
        base = 160 * count + ms + 2 * SIDE * t
        out[base : base + SIDE, :] = high.astype(BF16)
        out[base + SIDE : base + 2 * SIDE, :] = low.astype(BF16)


def side_rows(pack_p, ms):
    count = ms // TILE
    out = []
    for t in range(count):
        base = 160 * count + ms + 2 * SIDE * t
        high = pack_p[base : base + SIDE, :].astype(F32)
        out.append(high + pack_p[base + SIDE : base + 2 * SIDE, :].astype(F32))
    return jnp.concatenate(out, axis=1)


def fixed_kernel(loads, kinv, out, held, sems):
    ms = loads.shape[0] // 3
    moves = Moves(sems)
    copies = []
    for r in range(2 * ms // CHUNK):
        row = r * CHUNK + (ms if r * CHUNK >= ms else 0)
        copies.append(
            moves.start(
                kinv.at[pl.ds(row, CHUNK), pl.ds(ms, ms)], held.at[pl.ds(r * CHUNK, CHUNK), :]
            )
        )
    for r, copy in enumerate(copies):
        copy.wait()
        out[r * CHUNK : (r + 1) * CHUNK, :] = -dot(
            held[r * CHUNK : (r + 1) * CHUNK, :], loads[ms : 2 * ms, :]
        )


def setup_kernel(
    pack, pack_p, side_n, weights, rigid, loads, field, fixed, parity, kinv,
    tiles_s, tiles_p, tiles_pt, side_p, zt, md, md_p, um, us, resid,
    held, rows, modes, modes_p, sems,
):
    ms = weights.shape[1]
    nr = rigid.shape[0]
    count = ms // TILE
    span = TILE + 2 * HALO
    copies = start_faces(Moves(sems), kinv, held, ms)
    for t in range(count):
        tiles_s[span * t : span * (t + 1), :] = unpacked(pack, t).astype(BF16)
        tile = unpacked(pack_p, t)
        tiles_p[span * t : span * (t + 1), :] = tile.astype(BF16)
        tiles_pt[TILE * t : TILE * (t + 1), :] = with_fill(tile).T.astype(BF16)
    side_p[...] = side_rows(pack_p, ms)

    push = pack_p[160 * count : 160 * count + ms, :]
    scaled = column(weights[...]) * field[...]
    load = loads_of(push, scaled, loads[:ms, :], loads[2 * ms :, :])
    solved(copies, held, load, fixed, um, us, ms)

    def through(tiles, values):
        rows[...] = jnp.zeros_like(rows)
        high, low = halves(values)
        rows[0:nr, :] = high
        rows[8 : 8 + nr, :] = low
        moved = mortar_times(tiles, rows[...].T.astype(BF16)).T
        return moved[0:nr] + moved[8 : 8 + nr]

    modes[...] = jnp.zeros_like(modes)
    modes_p[...] = jnp.zeros_like(modes_p)
    modes[nr : 2 * nr, :] = rigid[:, ms:] * weights[...]
    modes[2 * nr : 3 * nr, :] = -through(tiles_s, side_n[0:nr, :])
    modes_p[0:nr, :] = side_p[0:nr, :] * side_p[16:17, :]
    modes_p[nr : 2 * nr, :] = -through(tiles_p, rigid[:, :ms])

    def stacked(values):
        high, low = halves(values)
        rows[...] = jnp.zeros_like(rows)
        rows[0:24, :] = high
        rows[32:56, :] = low
        rows[64:88, :] = high
        return rows[...].T.astype(BF16)

    md[...] = stacked(modes[...])
    columns = stacked(modes_p[...])
    md_p[...] = columns
    pushed = mortar_t_times(tiles_pt, columns).T
    odd = jnp.concatenate([parity[...]] * (ms // TILE), axis=1) > 0.0

    def placed(values):
        later = jnp.concatenate([values[18:24], values[0:18]], axis=0)
        return halves(jnp.where(odd, later, values))

    high, low = placed(-(pushed[0:24] + pushed[32:56]))
    zt[0:24, :ms] = high.astype(BF16)
    zt[24:48, :ms] = low.astype(BF16)
    high, low = placed(modes[...] * weights[...])
    zt[0:24, ms:] = high.astype(BF16)
    zt[24:48, ms:] = low.astype(BF16)
    resid[...] = residual(zt, um, us, ms)


def coarse_kernel(coarse, side_p, side_n, source, cand, out, floors, rows):
    nr, width = coarse.shape
    rows[...] = jnp.zeros_like(rows)
    rows[0:nr, :] = side_p[8 : 8 + nr, :]
    rows[nr : 2 * nr, :] = coarse[...]
    rows[2 * nr : 3 * nr, :] = side_n[8 : 8 + nr, :]
    high, low = halves(rows[...])
    both = jnp.concatenate([high, low], axis=0).astype(BF16)
    for n in range(0, out.shape[1], CHUNK):
        index = lax.broadcasted_iota(jnp.int32, (width, CHUNK), 0)
        pick = jnp.where(index == source[:, n : n + CHUNK], 1.0, 0.0).astype(BF16)
        out[:, n : n + CHUNK] = dot(both, pick).astype(BF16)

    floors[...] = jnp.zeros_like(floors)
    chosen = (cand[...].astype(F32), side_p[17:18, : cand.shape[1]])
    for t in range(floors.shape[1] // TILE):
        place = lax.broadcasted_iota(jnp.int32, (TILE, cand.shape[1]), 0) + TILE * t
        for n, which in enumerate(chosen):
            hit = jnp.where(place.astype(F32) == which, 1.0, 0.0)
            found = jnp.broadcast_to(jnp.max(hit, axis=1, keepdims=True), (TILE, TILE)).T
            floors[n : n + 1, TILE * t : TILE * (t + 1)] = jnp.where(
                found[0:1] > 0.0, 0.0, -jnp.inf
            )


def pair_kernel(resid, other, out):
    pair = (resid[...] + other[...]).astype(BF16)
    out[...] = jnp.broadcast_to(pair[None], out.shape)


def last_kernel(us, um_n, weights, tiles_s, grad):
    grad[...] = column(weights[...]) * us[...].astype(F32) - mortar_times(tiles_s, um_n[...])


def project_kernel(*refs):
    names = 12
    kinv, d_out, dp_out, sums = refs[names : names + 4]
    held = refs[names + 4]
    local = refs[names + 5 : 2 * names + 5]
    d, dp, sems = refs[2 * names + 5 :]
    ms = d.shape[0]
    moves = Moves(sems)
    arrive = [moves.start(a, b) for a, b in zip(refs[:names], local)]
    copies = start_faces(moves, kinv, held, ms)
    weights, side_p, um, us_p, tiles_p, every, coarse, md_p, us, um_n, tiles_s, md = local[:12]

    def wait(*which):
        for n in which:
            arrive[n].wait()

    wait(0, 1)
    wcol = column(weights[...])
    wcol_p = column(side_p[16:17, :])
    wait(2, 3, 4)
    grad_p = wcol_p * us_p[...].astype(F32) - mortar_times(tiles_p, um[...])
    wait(5, 6)
    both = dot(coarse[...], every[...].reshape(coarse.shape[1], TILE))
    high, low = halves(both[:24] + both[24:])
    gap = jnp.zeros((8, TILE), F32)
    rest = jnp.zeros((TILE - 88, TILE), F32)
    stack = jnp.concatenate([high, gap, high, gap, low, rest], axis=0).astype(BF16)
    wait(7)
    dp[...] = grad_p - dot(md_p[...], stack)
    out_p = moves.start(dp, dp_out)
    tiles_pt = []
    for t in range(ms // TILE):
        tile = tiles_p[TILE_ROWS * t : TILE_ROWS * (t + 1), :].astype(F32)
        tiles_pt.append(with_fill(tile).T.astype(BF16))
    tiles_pt = jnp.concatenate(tiles_pt, axis=0)
    master = (-mortar_t_times(tiles_pt, dp[...].astype(BF16))).astype(BF16)
    wait(8, 9, 10, 11)
    grad = wcol * us[...].astype(F32) - mortar_times(tiles_s, um_n[...])
    d[...] = grad - dot(md[...], stack)
    out_s = moves.start(d, d_out)
    slave = (wcol * d[...]).astype(BF16)
    load = jnp.concatenate([master, slave], axis=0)
    norm = jnp.sum(d[...] * d[...], axis=0, keepdims=True)
    curve = jnp.zeros((CHUNK, TILE), F32)
    for r, pair in enumerate(copies):
        for copy in pair:
            copy.wait()
        row = r * CHUNK
        curve += load[row : row + CHUNK].astype(F32) * dot(held[row : row + CHUNK, :], load)
    total = jnp.concatenate([norm, jnp.sum(curve, axis=0, keepdims=True)], axis=0)
    sums[...] = jnp.broadcast_to(total[None], sums.shape)
    out_p.wait()
    out_s.wait()


def step_kernel(*refs):
    names = 10
    loads, kinv = refs[names : names + 2]
    y_out, yp_out, um_out, us_out, resid = refs[names + 2 : names + 7]
    held = refs[names + 7]
    local = refs[names + 8 : 2 * names + 8]
    loads_m, loads_s, um, us, sems = refs[2 * names + 8 :]
    weights, floors, sums, field_p, dp, tiles_pt, field, d, fixed, zt = local[:10]
    ms = d.shape[0]
    moves = Moves(sems)
    arrive = [moves.start(refs[n], local[n]) for n in range(8)]
    arrive_m = moves.start(loads.at[pl.ds(0, ms), :], loads_m)
    arrive_s = moves.start(loads.at[pl.ds(2 * ms, ms), :], loads_s)
    copies = start_faces(moves, kinv, held, ms)
    arrive += [moves.start(refs[n], local[n]) for n in range(8, 10)]

    def wait(*which):
        for n in which:
            arrive[n].wait()

    wait(0, 1)
    wcol = column(weights[...])
    floor, floor_p = column(floors[0:1, :]), column(floors[1:2, :])
    wait(2)
    total = jnp.sum(sums[...], axis=0)
    step = total[0:1] / total[1:2]
    wait(3, 4)
    field_p[...] = jnp.maximum(field_p[...] - step * dp[...], floor_p)
    out_p = moves.start(field_p, yp_out)
    wait(5)
    push = mortar_t_times(tiles_pt, field_p[...].astype(BF16)).astype(BF16)
    wait(6, 7)
    field[...] = jnp.maximum(field[...] - step * d[...], floor)
    out_s = moves.start(field, y_out)
    arrive_m.wait()
    arrive_s.wait()
    load = loads_of(push, wcol * field[...], loads_m[...], loads_s[...])
    wait(8)
    solved(copies, held, load, fixed, um, us, ms)
    out_um = moves.start(um, um_out)
    out_us = moves.start(us, us_out)
    wait(9)
    resid[...] = residual(zt, um, us, ms)
    out_p.wait()
    out_s.wait()
    out_um.wait()
    out_us.wait()


def shape(dims, dtype):
    return jax.ShapeDtypeStruct(dims, dtype)


def kernel_call(body, outs, *operands, anywhere=(), anywhere_out=(), scratch=(), flops=0):
    here = pl.BlockSpec(memory_space=pltpu.VMEM)
    far = pl.BlockSpec(memory_space=pl.ANY)
    moved = sum(int(np.prod(o.shape)) * o.dtype.itemsize for o in list(operands) + list(outs))
    return pl.pallas_call(
        body,
        out_shape=tuple(outs),
        in_specs=[far if n in anywhere else here for n in range(len(operands))],
        out_specs=tuple(far if n in anywhere_out else here for n in range(len(outs))),
        scratch_shapes=list(scratch),
        compiler_params=pltpu.CompilerParams(vmem_limit_bytes=67_000_000),
        cost_estimate=pl.CostEstimate(flops=flops, bytes_accessed=moved, transcendentals=0),
    )(*operands)


def on_device(
    inverse_blocks,
    primal_loads,
    mortar_values,
    segment_ids,
    slave_weights,
    rigid_modes,
    coarse_inverse,
    candidates,
    start_multipliers,
):
    ms = mortar_values.shape[1]
    nr = rigid_modes.shape[1]
    nc = coarse_inverse.shape[1]
    lc = start_multipliers.shape[2]
    sub, grp = lax.axis_size("sub"), lax.axis_size("grp")
    chips = sub * grp // 2
    kinv = inverse_blocks[0]
    loads = primal_loads[0]
    rigid = rigid_modes[0]
    field = start_multipliers[0]
    count = ms // TILE
    face = lambda dtype: shape((ms, lc), dtype)
    kff = pltpu.VMEM((2 * ms, 2 * ms), BF16)
    chunks = 2 * ms // CHUNK

    pack, behind = kernel_call(
        pack_kernel,
        [shape(((160 + 2 * SIDE) * count + ms, lc), BF16), shape((16, ms), F32)],
        mortar_values[0],
        segment_ids,
        field,
        rigid,
        coarse_inverse,
        slave_weights,
        candidates,
    )
    pack_p = shifted(pack, 1)
    side_n = shifted(behind, -1)
    field_p = shifted(field, 1)
    (fixed,) = kernel_call(
        fixed_kernel,
        [shape((2 * ms, lc), F32)],
        loads,
        kinv,
        anywhere=(1,),
        scratch=[pltpu.VMEM((2 * ms, ms), BF16), pltpu.SemaphoreType.DMA((chunks,))],
        flops=4 * ms * ms * lc,
    )
    second = lax.axis_index("sub") % 2 == 1
    parity = jnp.broadcast_to(jnp.where(second, 1.0, 0.0).astype(F32), (1, TILE))
    (tiles_s, tiles_p, tiles_pt, side_p, zt, md, md_p, um, us, resid) = kernel_call(
        setup_kernel,
        [
            shape((TILE_ROWS * count, TILE), BF16),
            shape((TILE_ROWS * count, TILE), BF16),
            shape((ms, 2 * TILE), BF16),
            shape((SIDE, ms), F32),
            shape((48, 2 * ms), BF16),
            face(BF16),
            face(BF16),
            face(BF16),
            face(BF16),
            shape((24, lc), F32),
        ],
        pack,
        pack_p,
        side_n,
        slave_weights,
        rigid,
        loads,
        field,
        fixed,
        parity,
        kinv,
        anywhere=(9,),
        scratch=[
            kff,
            pltpu.VMEM((TILE, ms), F32),
            pltpu.VMEM((24, ms), F32),
            pltpu.VMEM((24, ms), F32),
            pltpu.SemaphoreType.DMA((2 * chunks,)),
        ],
        flops=8 * ms * ms * lc,
    )

    chip, group, near, mode = np.meshgrid(
        np.arange(sub // 2), np.arange(grp), np.arange(4), np.arange(nr), indexing="ij"
    )
    source = (((2 * chip + near - 1) % sub) * grp + group) * nr + mode
    source = jnp.asarray(source.reshape(1, -1), jnp.int32)
    coarse, floors = kernel_call(
        coarse_kernel,
        [shape((48, source.shape[1]), BF16), shape((8, ms), F32)],
        coarse_inverse,
        side_p,
        side_n,
        source,
        candidates,
        scratch=[pltpu.VMEM((24, nc), F32)],
        flops=2 * 48 * nc * source.shape[1],
    )

    same_core = [
        [(2 * m + core) * grp + z for m in range(sub // 2) for z in range(grp)]
        for core in range(2)
    ]
    for _ in range(STEPS):
        (pieces,) = kernel_call(
            pair_kernel, [shape((chips, 24, lc), BF16)], resid, swapped(resid)
        )
        every = lax.all_to_all(
            pieces, AXES, 0, 0, tiled=True, axis_index_groups=same_core
        )
        um_n = shifted(um, -1)
        us_p = shifted(us, 1)
        operands = (
            slave_weights, side_p, um, us_p, tiles_p, every, coarse, md_p, us, um_n, tiles_s, md,
        )
        d, d_p, sums = kernel_call(
            project_kernel,
            [face(F32), face(F32), shape((2 * chips, 2, lc), F32)],
            *operands,
            kinv,
            anywhere=range(len(operands) + 1),
            anywhere_out=(0, 1),
            scratch=[kff]
            + [pltpu.VMEM(o.shape, o.dtype) for o in operands]
            + [
                pltpu.VMEM((ms, lc), F32),
                pltpu.VMEM((ms, lc), F32),
                pltpu.SemaphoreType.DMA((len(operands) + 2 * chunks + 2,)),
            ],
            flops=8 * ms * ms * lc,
        )
        totals = lax.all_to_all(sums, AXES, 0, 0, tiled=True)
        operands = (
            slave_weights, floors, totals, field_p, d_p, tiles_pt, field, d, fixed, zt,
        )
        field, field_p, um, us, resid = kernel_call(
            step_kernel,
            [face(F32), face(F32), face(BF16), face(BF16), shape((24, lc), F32)],
            *operands,
            loads,
            kinv,
            anywhere=range(len(operands) + 2),
            anywhere_out=(0, 1, 2, 3),
            scratch=[kff]
            + [pltpu.VMEM(o.shape, o.dtype) for o in operands]
            + [pltpu.VMEM((ms, lc), BF16)] * 4
            + [pltpu.SemaphoreType.DMA((len(operands) + 2 * chunks + 6,))],
            flops=8 * ms * ms * lc,
        )
    um_n = shifted(um, -1)
    (gradient,) = kernel_call(
        last_kernel, [face(F32)], us, um_n, slave_weights, tiles_s, flops=2 * 192 * ms * lc
    )
    return (field[None], gradient[None])


def solution(mesh):
    placed = (
        P(AXES, None, None),
        P(AXES, None, None),
        P(AXES, None, None),
        P(AXES, None),
        P(AXES, None),
        P(AXES, None, None),
        P(AXES, None),
        P(AXES, None),
        P(AXES, None, None),
    )
    return jax.shard_map(
        on_device,
        mesh=mesh,
        in_specs=placed,
        out_specs=(P(AXES, None, None), P(AXES, None, None)),
        check_vma=False,
    )
```

```python
import functools

import jax
import jax.numpy as jnp
import numpy as np
from jax import lax
from jax.experimental import pallas as pl
from jax.experimental.pallas import tpu as pltpu
from jax.sharding import PartitionSpec as P

STEPS = 3
AXES = ("sub", "grp")
F32, BF16 = jnp.float32, jnp.bfloat16
TILE = 128
TILE_ROWS = 192
HALO = 32
MIB = 1 << 20


def shifted(block, distance):
    size = lax.axis_size("sub")
    return lax.ppermute(block, "sub", [((i - distance) % size, i) for i in range(size)])


def swapped(block):
    size = lax.axis_size("sub")
    return lax.ppermute(block, "sub", [(i ^ 1, i) for i in range(size)])


def swapped_out(block):
    size = lax.axis_size("sub")
    other = [(i + 1 if i % 2 else i - 1) % size for i in range(size)]
    return lax.ppermute(block, "sub", [(other[i], i) for i in range(size)])


def is_odd():
    return lax.rem(lax.axis_index("sub"), 2) == 1


def rows_of(flat, count):
    width = flat.shape[1] // count
    return jnp.concatenate([flat[:, width * k : width * (k + 1)] for k in range(count)], axis=0)


def dot(left, right):
    return jnp.dot(left, right, preferred_element_type=F32)


def halves(value):
    high = value.astype(BF16).astype(F32)
    return high, (value - high).astype(BF16).astype(F32)


def column(row):
    return jnp.broadcast_to(row, (TILE, row.shape[1])).T


def mortar_times(tiles, values):
    count = values.shape[0] // TILE
    rows = TILE + 2 * HALO
    parts = [
        dot(tiles[rows * t : rows * (t + 1), :], values[TILE * t : TILE * (t + 1)])
        for t in range(count)
    ]
    out = []
    none = jnp.zeros((HALO, values.shape[1]), F32)
    for t in range(count):
        before = parts[t - 1][TILE + HALO :] if t else none
        after = parts[t + 1][TILE : TILE + HALO] if t + 1 < count else none
        gap = jnp.zeros((TILE - 2 * HALO, values.shape[1]), F32)
        out.append(parts[t][:TILE] + jnp.concatenate([before, gap, after], axis=0))
    return jnp.concatenate(out, axis=0)


def mortar_t_times(tiles_t, values):
    count = values.shape[0] // TILE
    none = jnp.zeros((HALO, values.shape[1]), BF16)
    fill = jnp.zeros((TILE - 2 * HALO, values.shape[1]), BF16)
    out = []
    for t in range(count):
        low, high = TILE * t, TILE * (t + 1)
        before = values[low - HALO : low] if t else none
        after = values[high : high + HALO] if t + 1 < count else none
        window = jnp.concatenate([values[low:high], before, after, fill], axis=0)
        out.append(dot(tiles_t[TILE * t : TILE * (t + 1), :], window))
    return jnp.concatenate(out, axis=0)


def unpacked(pack, t):
    edge = pack[160 * t : 160 * t + HALO, :].astype(F32)
    lane = lax.broadcasted_iota(jnp.int32, edge.shape, 1)
    above = jnp.where(lane < TILE // 2, edge, 0.0)
    below = jnp.where(lane < TILE // 2, 0.0, edge)
    middle = pack[160 * t + HALO : 160 * (t + 1), :].astype(F32)
    return jnp.concatenate([middle, above, below], axis=0)


def with_fill(tile):
    return jnp.concatenate([tile, jnp.zeros((TILE - 2 * HALO, TILE), F32)], axis=0)


class Moves:
    def __init__(self, sems):
        self.sems, self.used = sems, 0

    def start(self, source, target):
        copy = pltpu.make_async_copy(source, target, self.sems.at[self.used])
        self.used += 1
        copy.start()
        return copy


CHUNK = 256
SIDE = 32


def start_faces(moves, kinv, held, ms):
    copies = []
    for r in range(2 * ms // CHUNK):
        row = r * CHUNK + (ms if r * CHUNK >= ms else 0)
        pair = []
        for to, at in ((0, 0), (ms, 2 * ms)):
            pair.append(
                moves.start(
                    kinv.at[pl.ds(row, CHUNK), pl.ds(at, ms)],
                    held.at[pl.ds(r * CHUNK, CHUNK), pl.ds(to, ms)],
                )
            )
        copies.append(pair)
    return copies


def solved(copies, held, load, fixed, zt, um, us, ms):
    both = 0.0
    for r, pair in enumerate(copies):
        for copy in pair:
            copy.wait()
        row = r * CHUNK
        u = (dot(held[row : row + CHUNK, :], load) + fixed[row : row + CHUNK, :]).astype(BF16)
        if row < ms:
            um[row : row + CHUNK, :] = u
        else:
            us[row - ms : row - ms + CHUNK, :] = u
        if zt is not None:
            both += dot(zt[:, row : row + CHUNK], u)
    return None if zt is None else both[:24] + both[24:]


def loads_of(push, scaled, loads_m, loads_s):
    master = (-push.astype(F32) - loads_m.astype(F32)).astype(BF16)
    slave = (scaled - loads_s.astype(F32)).astype(BF16)
    return jnp.concatenate([master, slave], axis=0)


def pack_kernel(mortar, seg, field, modes, coarse, weights, cand, out, behind):
    ms = mortar.shape[0]
    nr = coarse.shape[0]
    rigid = rows_of(modes, nr)
    count = ms // TILE
    ids = seg[...].astype(F32)
    ids_col = column(ids)
    none = jnp.zeros((HALO, TILE), F32)

    def masked(low, high, t):
        own = slice(TILE * t, TILE * (t + 1))
        same = ids_col[low:high] == ids[:, own]
        return jnp.where(same, mortar[low:high, own].astype(F32), 0.0)

    tiles = []
    for t in range(count):
        low, high = TILE * t, TILE * (t + 1)
        middle = masked(low, high, t)
        above = masked(low - HALO, low, t) if t else none
        below = masked(high, high + HALO, t) if t + 1 < count else none
        out[160 * t : 160 * t + HALO, :] = (above + below).astype(BF16)
        out[160 * t + HALO : 160 * (t + 1), :] = middle.astype(BF16)
        tile = jnp.concatenate([middle, above, below], axis=0)
        tiles.append(with_fill(tile).T.astype(BF16))
    push = mortar_t_times(jnp.concatenate(tiles, axis=0), field[...].astype(BF16))
    out[160 * count : 160 * count + ms, :] = push.astype(BF16)

    behind[...] = jnp.zeros_like(behind)
    behind[0:nr, :] = rigid[:, :ms]
    behind[8 : 8 + nr, :] = coarse[...]
    for t in range(count):
        own = slice(TILE * t, TILE * (t + 1))
        chosen = jnp.zeros((1, TILE), F32)
        if TILE * (t + 1) <= cand.shape[1]:
            chosen = cand[:, own].astype(F32)
        lanes = slice(ms + TILE * t, ms + TILE * (t + 1))
        pad = jnp.zeros((8 - nr, TILE), F32)
        rows = [rigid[:, lanes], pad, coarse[:, own], pad, weights[:, own], chosen]
        value = jnp.concatenate(rows + [jnp.zeros((SIDE - 18, TILE), F32)], axis=0)
        high, low = halves(value)
        base = 160 * count + ms + 2 * SIDE * t
        out[base : base + SIDE, :] = high.astype(BF16)
        out[base + SIDE : base + 2 * SIDE, :] = low.astype(BF16)


def side_rows(pack_p, ms):
    count = ms // TILE
    out = []
    for t in range(count):
        base = 160 * count + ms + 2 * SIDE * t
        high = pack_p[base : base + SIDE, :].astype(F32)
        out.append(high + pack_p[base + SIDE : base + 2 * SIDE, :].astype(F32))
    return jnp.concatenate(out, axis=1)


def fixed_kernel(loads, kinv, out, held, sems):
    ms = loads.shape[0] // 3
    moves = Moves(sems)
    copies = []
    for r in range(2 * ms // CHUNK):
        row = r * CHUNK + (ms if r * CHUNK >= ms else 0)
        copies.append(
            moves.start(
                kinv.at[pl.ds(row, CHUNK), pl.ds(ms, ms)], held.at[pl.ds(r * CHUNK, CHUNK), :]
            )
        )
    for r, copy in enumerate(copies):
        copy.wait()
        out[r * CHUNK : (r + 1) * CHUNK, :] = -dot(
            held[r * CHUNK : (r + 1) * CHUNK, :], loads[ms : 2 * ms, :]
        )


def setup_kernel(
    pack, pack_p, side_n, weights, rigid_row, loads, field, fixed, kinv,
    tiles_s, tiles_p, tiles_pt, side_p, zt, md, md_p, near, far, resid,
    held, rows, modes, modes_p, um, us, sems,
):
    ms = weights.shape[1]
    nr = rigid_row.shape[1] // (2 * ms)
    rigid = rows_of(rigid_row, nr)
    odd = is_odd()
    count = ms // TILE
    span = TILE + 2 * HALO
    copies = start_faces(Moves(sems), kinv, held, ms)
    for t in range(count):
        tiles_s[span * t : span * (t + 1), :] = unpacked(pack, t).astype(BF16)
        tile = unpacked(pack_p, t)
        tiles_p[span * t : span * (t + 1), :] = tile.astype(BF16)
        tiles_pt[TILE * t : TILE * (t + 1), :] = with_fill(tile).T.astype(BF16)
    side_p[...] = side_rows(pack_p, ms)

    push = pack_p[160 * count : 160 * count + ms, :]
    scaled = column(weights[...]) * field[...]
    load = loads_of(push, scaled, loads[:ms, :], loads[2 * ms :, :])
    solved(copies, held, load, fixed, None, um, us, ms)
    near[...] = jnp.where(odd, um[...], us[...])
    far[...] = jnp.where(odd, us[...], um[...])

    def through(tiles, values):
        rows[...] = jnp.zeros_like(rows)
        high, low = halves(values)
        rows[0:nr, :] = high
        rows[8 : 8 + nr, :] = low
        moved = mortar_times(tiles, rows[...].T.astype(BF16)).T
        return moved[0:nr] + moved[8 : 8 + nr]

    modes[...] = jnp.zeros_like(modes)
    modes_p[...] = jnp.zeros_like(modes_p)
    modes[nr : 2 * nr, :] = rigid[:, ms:] * weights[...]
    modes[2 * nr : 3 * nr, :] = -through(tiles_s, side_n[0:nr, :])
    modes_p[0:nr, :] = side_p[0:nr, :] * side_p[16:17, :]
    modes_p[nr : 2 * nr, :] = -through(tiles_p, rigid[:, :ms])

    def placed(values):
        later = jnp.concatenate([values[18:24], values[0:18]], axis=0)
        return jnp.where(odd, later, values)

    def stacked(values):
        high, low = halves(values)
        rows[...] = jnp.zeros_like(rows)
        rows[0:24, :] = high
        rows[32:56, :] = low
        rows[64:88, :] = high
        return rows[...].T.astype(BF16)

    own = placed(modes[...])
    md[...] = stacked(own)
    columns = stacked(placed(modes_p[...]))
    md_p[...] = columns
    pushed = mortar_t_times(tiles_pt, columns).T
    high, low = halves(-(pushed[0:24] + pushed[32:56]))
    zt[0:24, :ms] = high.astype(BF16)
    zt[24:48, :ms] = low.astype(BF16)
    high, low = halves(own * weights[...])
    zt[0:24, ms:] = high.astype(BF16)
    zt[24:48, ms:] = low.astype(BF16)
    both = dot(zt[:, :ms], um[...]) + dot(zt[:, ms:], us[...])
    resid[...] = both[:24] + both[24:]


def coarse_kernel(coarse, side_p, side_n, source, cand, out, floors, rows):
    nr, width = coarse.shape
    rows[...] = jnp.zeros_like(rows)
    rows[0:nr, :] = side_p[8 : 8 + nr, :]
    rows[nr : 2 * nr, :] = coarse[...]
    rows[2 * nr : 3 * nr, :] = side_n[8 : 8 + nr, :]
    later = jnp.concatenate([rows[18:24, :], rows[0:18, :]], axis=0)
    high, low = halves(jnp.where(is_odd(), later, rows[...]))
    both = jnp.concatenate([high, low], axis=0).astype(BF16)
    for n in range(0, out.shape[1], CHUNK):
        index = lax.broadcasted_iota(jnp.int32, (width, CHUNK), 0)
        pick = jnp.where(index == source[:, n : n + CHUNK], 1.0, 0.0).astype(BF16)
        out[:, n : n + CHUNK] = dot(both, pick).astype(BF16)

    floors[...] = jnp.zeros_like(floors)
    chosen = (cand[...].astype(F32), side_p[17:18, : cand.shape[1]])
    for t in range(floors.shape[1] // TILE):
        place = lax.broadcasted_iota(jnp.int32, (TILE, cand.shape[1]), 0) + TILE * t
        for n, which in enumerate(chosen):
            hit = jnp.where(place.astype(F32) == which, 1.0, 0.0)
            found = jnp.broadcast_to(jnp.max(hit, axis=1, keepdims=True), (TILE, TILE)).T
            floors[n : n + 1, TILE * t : TILE * (t + 1)] = jnp.where(
                found[0:1] > 0.0, 0.0, -jnp.inf
            )


def pair_kernel(resid, other, out):
    pair = (resid[...] + other[...]).astype(BF16)
    out[...] = jnp.broadcast_to(pair[None], out.shape)


def last_kernel(us, um_n, weights, tiles_s, grad):
    grad[...] = column(weights[...]) * us[...].astype(F32) - mortar_times(tiles_s, um_n[...])


def dot_rows(left, right):
    return lax.dot_general(left, right, (((1,), (1,)), ((), ())), preferred_element_type=F32)


def forms_kernel(zt, md, near, kinv, klt, mrows, forms, held, long, square, sems):
    del near
    ms = md.shape[0]
    copies = start_faces(Moves(sems), kinv, held, ms)
    mrows[...] = md[...].astype(F32).T[0:64].astype(BF16)
    long[...] = jnp.zeros_like(long)
    long[0:24, :] = zt[0:24, :].astype(F32)
    long[32:56, :] = zt[24:48, :].astype(F32)
    columns = long[...].T.astype(BF16)
    for r, pair in enumerate(copies):
        for copy in pair:
            copy.wait()
        row = r * CHUNK
        long[:, row : row + CHUNK] = dot(held[row : row + CHUNK, :], columns).T
    high, low = halves(long[0:24, :] + long[32:56, :])
    klt[0:24, :] = high.astype(BF16)
    klt[24:48, :] = low.astype(BF16)

    def form(at, product):
        square[...] = jnp.zeros_like(square)
        square[0:24, 0:64] = product[0:24] + product[32:56]
        turned = square[...].T
        high, low = halves(turned[0:24] + turned[32:56])
        square[...] = jnp.zeros_like(square)
        square[0:24, :] = high
        square[32:56, :] = low
        square[64:88, :] = high
        forms[at : at + 24, :] = square[...].T[0:24].astype(BF16)

    gap = jnp.zeros((8, 2 * ms), BF16)
    left = jnp.concatenate([zt[0:24, :], gap, zt[24:48, :], gap], axis=0)
    right = jnp.concatenate([klt[0:24, :], gap, klt[24:48, :], gap], axis=0)
    form(0, dot_rows(mrows[...], mrows[...]))
    form(24, dot_rows(left, right))


def gradient_kernel(*refs):
    names = 12
    kinv, _, g_out, gp_out, stats = refs[names : names + 5]
    held = refs[names + 5]
    local = refs[names + 6 : 2 * names + 6]
    g, gp, solution, sems = refs[2 * names + 6 :]
    ms = g.shape[0]
    moves = Moves(sems)
    arrive = [moves.start(a, b) for a, b in zip(refs[:names], local)]
    copies = start_faces(moves, kinv, held, ms)
    weights, side_p, near, far, near_r, far_r, tiles_p, tiles_pt, tiles_s, mrows, zt, klt = local

    def wait(*which):
        for n in which:
            arrive[n].wait()

    wait(0, 1, 2, 3, 4, 5, 6)
    odd = is_odd()
    um, us = jnp.where(odd, near[...], far[...]), jnp.where(odd, far[...], near[...])
    um_n = jnp.where(odd, far_r[...], near_r[...])
    us_p = jnp.where(odd, near_r[...], far_r[...])
    wcol = column(weights[...])
    gp[...] = column(side_p[16:17, :]) * us_p.astype(F32) - mortar_times(tiles_p, um)
    out_p = moves.start(gp, gp_out)
    wait(7)
    master = (-mortar_t_times(tiles_pt, gp[...].astype(BF16))).astype(BF16)
    wait(8)
    g[...] = wcol * us.astype(F32) - mortar_times(tiles_s, um_n)
    out_s = moves.start(g, g_out)
    load = jnp.concatenate([master, (wcol * g[...]).astype(BF16)], axis=0)
    curve = jnp.zeros((CHUNK, TILE), F32)
    for r, pair in enumerate(copies):
        for copy in pair:
            copy.wait()
        row = r * CHUNK
        part = dot(held[row : row + CHUNK, :], load)
        solution[row : row + CHUNK, :] = part
        curve += load[row : row + CHUNK].astype(F32) * part
    wait(9, 10, 11)
    stats[...] = jnp.zeros_like(stats)
    stats[0:1, :] = jnp.sum(g[...] * g[...], axis=0, keepdims=True)
    stats[1:2, :] = jnp.sum(curve, axis=0, keepdims=True)
    high, low = halves(g[...])
    first = dot(mrows[...], high.astype(BF16))
    second = dot(mrows[0:32, :], low.astype(BF16))
    stats[8:32, :] = first[0:24] + first[32:56] + second[0:24]
    high, low = halves(solution[...])
    first = dot(zt[...], high.astype(BF16)) + dot(klt[...], load)
    second = dot(zt[0:32, :], low.astype(BF16))
    stats[32:56, :] = first[0:24] + first[24:48] + second[0:24]
    out_p.wait()
    out_s.wait()


def project_kernel(every, coarse, forms, stats, stack, sums):
    both = dot(coarse[...], every[...].reshape(coarse.shape[1], TILE))
    c = both[:24] + both[24:]
    high, low = halves(c)
    gap = jnp.zeros((8, TILE), F32)
    rest = jnp.zeros((TILE - 88, TILE), F32)
    operand = jnp.concatenate([high, gap, high, gap, low, rest], axis=0).astype(BF16)
    stack[...] = operand
    moved = dot(forms[...], operand)
    norm = stats[0:1, :] + jnp.sum(
        c * (moved[0:24] - 2.0 * stats[8:32, :]), axis=0, keepdims=True
    )
    curve = stats[1:2, :] + jnp.sum(c * (moved[24:48] - stats[32:56, :]), axis=0, keepdims=True)
    total = jnp.concatenate([norm, curve], axis=0)
    sums[...] = jnp.broadcast_to(total[None], sums.shape)


def direction_kernel(stack, g, gp, md, md_p, d, dp):
    d[...] = g[...] - dot(md[...], stack[...])
    dp[...] = gp[...] - dot(md_p[...], stack[...])


def marker_kernel(near, out):
    del near
    out[...] = jnp.zeros_like(out)


def last_kernel(us, um_n, weights, tiles_s, grad):
    grad[...] = column(weights[...]) * us[...].astype(F32) - mortar_times(tiles_s, um_n[...])


def dot_rows(left, right):
    return lax.dot_general(left, right, (((1,), (1,)), ((), ())), preferred_element_type=F32)


def forms_kernel(zt, md, um, kinv, klt, mrows, forms, held, long, square, sems):
    del um
    ms = md.shape[0]
    copies = start_faces(Moves(sems), kinv, held, ms)
    mrows[...] = md[...].astype(F32).T[0:64].astype(BF16)
    long[...] = jnp.zeros_like(long)
    long[0:24, :] = zt[0:24, :].astype(F32)
    long[32:56, :] = zt[24:48, :].astype(F32)
    columns = long[...].T.astype(BF16)
    for r, pair in enumerate(copies):
        for copy in pair:
            copy.wait()
        row = r * CHUNK
        long[:, row : row + CHUNK] = dot(held[row : row + CHUNK, :], columns).T
    high, low = halves(long[0:24, :] + long[32:56, :])
    klt[0:24, :] = high.astype(BF16)
    klt[24:48, :] = low.astype(BF16)

    def form(at, product):
        square[...] = jnp.zeros_like(square)
        square[0:24, 0:64] = product[0:24] + product[32:56]
        turned = square[...].T
        high, low = halves(turned[0:24] + turned[32:56])
        square[...] = jnp.zeros_like(square)
        square[0:24, :] = high
        square[32:56, :] = low
        square[64:88, :] = high
        forms[at : at + 24, :] = square[...].T[0:24].astype(BF16)

    gap = jnp.zeros((8, 2 * ms), BF16)
    left = jnp.concatenate([zt[0:24, :], gap, zt[24:48, :], gap], axis=0)
    right = jnp.concatenate([klt[0:24, :], gap, klt[24:48, :], gap], axis=0)
    form(0, dot_rows(mrows[...], mrows[...]))
    form(24, dot_rows(left, right))


def gradient_kernel(*refs):
    names = 12
    kinv, _, g_out, gp_out, stats = refs[names : names + 5]
    held = refs[names + 5]
    local = refs[names + 6 : 2 * names + 6]
    g, gp, solution, sems = refs[2 * names + 6 :]
    ms = g.shape[0]
    moves = Moves(sems)
    arrive = [moves.start(a, b) for a, b in zip(refs[:names], local)]
    copies = start_faces(moves, kinv, held, ms)
    weights, side_p, near, far, near_r, far_r, tiles_p, tiles_pt, tiles_s, mrows, zt, klt = local

    def wait(*which):
        for n in which:
            arrive[n].wait()

    wait(0, 1, 2, 3, 4, 5, 6)
    odd = is_odd()
    um, us = jnp.where(odd, near[...], far[...]), jnp.where(odd, far[...], near[...])
    um_n = jnp.where(odd, far_r[...], near_r[...])
    us_p = jnp.where(odd, near_r[...], far_r[...])
    wcol = column(weights[...])
    gp[...] = column(side_p[16:17, :]) * us_p.astype(F32) - mortar_times(tiles_p, um)
    out_p = moves.start(gp, gp_out)
    wait(7)
    master = (-mortar_t_times(tiles_pt, gp[...].astype(BF16))).astype(BF16)
    wait(8)
    g[...] = wcol * us.astype(F32) - mortar_times(tiles_s, um_n)
    out_s = moves.start(g, g_out)
    load = jnp.concatenate([master, (wcol * g[...]).astype(BF16)], axis=0)
    curve = jnp.zeros((CHUNK, TILE), F32)
    for r, pair in enumerate(copies):
        for copy in pair:
            copy.wait()
        row = r * CHUNK
        part = dot(held[row : row + CHUNK, :], load)
        solution[row : row + CHUNK, :] = part
        curve += load[row : row + CHUNK].astype(F32) * part
    wait(9, 10, 11)
    stats[...] = jnp.zeros_like(stats)
    stats[0:1, :] = jnp.sum(g[...] * g[...], axis=0, keepdims=True)
    stats[1:2, :] = jnp.sum(curve, axis=0, keepdims=True)
    high, low = halves(g[...])
    first = dot(mrows[...], high.astype(BF16))
    second = dot(mrows[0:32, :], low.astype(BF16))
    stats[8:32, :] = first[0:24] + first[32:56] + second[0:24]
    high, low = halves(solution[...])
    first = dot(zt[...], high.astype(BF16)) + dot(klt[...], load)
    second = dot(zt[0:32, :], low.astype(BF16))
    stats[32:56, :] = first[0:24] + first[24:48] + second[0:24]
    out_p.wait()
    out_s.wait()


def project_kernel(every, coarse, forms, stats, stack, sums):
    both = dot(coarse[...], every[...].reshape(coarse.shape[1], TILE))
    c = both[:24] + both[24:]
    high, low = halves(c)
    gap = jnp.zeros((8, TILE), F32)
    rest = jnp.zeros((TILE - 88, TILE), F32)
    operand = jnp.concatenate([high, gap, high, gap, low, rest], axis=0).astype(BF16)
    stack[...] = operand
    moved = dot(forms[...], operand)
    norm = stats[0:1, :] + jnp.sum(
        c * (moved[0:24] - 2.0 * stats[8:32, :]), axis=0, keepdims=True
    )
    curve = stats[1:2, :] + jnp.sum(c * (moved[24:48] - stats[32:56, :]), axis=0, keepdims=True)
    total = jnp.concatenate([norm, curve], axis=0)
    sums[...] = jnp.broadcast_to(total[None], sums.shape)


def direction_kernel(stack, g, gp, md, md_p, d, dp):
    d[...] = g[...] - dot(md[...], stack[...])
    dp[...] = gp[...] - dot(md_p[...], stack[...])


def weights_kernel(um, weights, out):
    del um
    out[...] = weights[...]


def step_kernel(final, *refs):
    names = 10
    loads, kinv = refs[names : names + 2]
    y_out, yp_out, near_out, far_out, resid_out = refs[names + 2 : names + 7]
    held = refs[names + 7]
    local = refs[names + 8 : 2 * names + 8]
    loads_m, loads_s, um, us, near, far, resid, sems = refs[2 * names + 8 :]
    weights, floors, sums, field_p, dp, tiles_pt, field, d, zt, fixed = local[:10]
    ms = d.shape[0]
    moves = Moves(sems)
    arrive = [moves.start(refs[n], local[n]) for n in range(8)]
    arrive_m = moves.start(loads.at[pl.ds(0, ms), :], loads_m)
    arrive_s = moves.start(loads.at[pl.ds(2 * ms, ms), :], loads_s)
    arrive += [moves.start(refs[n], local[n]) for n in range(8, 10)]
    copies = start_faces(moves, kinv, held, ms)

    def wait(*which):
        for n in which:
            arrive[n].wait()

    wait(0, 1)
    wcol = column(weights[...])
    floor, floor_p = column(floors[0:1, :]), column(floors[1:2, :])
    wait(2)
    total = jnp.sum(sums[...], axis=0)
    step = total[0:1] / total[1:2]
    wait(3, 4)
    field_p[...] = jnp.maximum(field_p[...] - step * dp[...], floor_p)
    out_p = moves.start(field_p, yp_out)
    wait(5)
    push = mortar_t_times(tiles_pt, field_p[...].astype(BF16)).astype(BF16)
    wait(6, 7)
    field[...] = jnp.maximum(field[...] - step * d[...], floor)
    out_s = moves.start(field, y_out)
    arrive_m.wait()
    arrive_s.wait()
    load = loads_of(push, wcol * field[...], loads_m[...], loads_s[...])
    wait(8, 9)
    pieces = solved(copies, held, load, fixed, zt, um, us, ms)
    if final:
        outs = [moves.start(um, near_out), moves.start(us, far_out)]
    else:
        odd = is_odd()
        near[...] = jnp.where(odd, um[...], us[...])
        far[...] = jnp.where(odd, us[...], um[...])
        outs = [moves.start(far, far_out), moves.start(near, near_out)]
    resid[...] = pieces
    outs.append(moves.start(resid, resid_out))
    for copy in [out_p, out_s] + outs:
        copy.wait()


def shape(dims, dtype):
    return jax.ShapeDtypeStruct(dims, dtype)


def kernel_call(body, outs, *operands, anywhere=(), anywhere_out=(), scratch=(), flops=0):
    here = pl.BlockSpec(memory_space=pltpu.VMEM)
    far = pl.BlockSpec(memory_space=pl.ANY)
    moved = sum(int(np.prod(o.shape)) * o.dtype.itemsize for o in list(operands) + list(outs))
    return pl.pallas_call(
        body,
        out_shape=tuple(outs),
        in_specs=[far if n in anywhere else here for n in range(len(operands))],
        out_specs=tuple(far if n in anywhere_out else here for n in range(len(outs))),
        scratch_shapes=list(scratch),
        compiler_params=pltpu.CompilerParams(vmem_limit_bytes=64 * MIB),
        cost_estimate=pl.CostEstimate(flops=flops, bytes_accessed=moved, transcendentals=0),
    )(*operands)


def on_device(
    inverse_blocks,
    primal_loads,
    mortar_values,
    segment_ids,
    slave_weights,
    rigid_modes,
    coarse_inverse,
    candidates,
    start_multipliers,
):
    ms = mortar_values.shape[1]
    nr = rigid_modes.shape[1]
    nc = coarse_inverse.shape[1]
    lc = start_multipliers.shape[2]
    sub, grp = lax.axis_size("sub"), lax.axis_size("grp")
    chips = sub * grp // 2
    kinv = inverse_blocks[0]
    loads = primal_loads[0]
    rigid = rigid_modes.reshape(1, -1)
    field = start_multipliers[0]
    count = ms // TILE
    face = lambda dtype: shape((ms, lc), dtype)
    kff = pltpu.VMEM((2 * ms, 2 * ms), BF16)
    chunks = 2 * ms // CHUNK

    pack, behind = kernel_call(
        pack_kernel,
        [shape(((160 + 2 * SIDE) * count + ms, lc), BF16), shape((16, ms), F32)],
        mortar_values[0],
        segment_ids,
        field,
        rigid,
        coarse_inverse,
        slave_weights,
        candidates,
    )
    pack_p = shifted(pack, 1)
    side_n = shifted(behind, -1)
    field_p = shifted(field, 1)
    (fixed,) = kernel_call(
        fixed_kernel,
        [shape((2 * ms, lc), F32)],
        loads,
        kinv,
        anywhere=(1,),
        scratch=[pltpu.VMEM((2 * ms, ms), BF16), pltpu.SemaphoreType.DMA((chunks,))],
        flops=4 * ms * ms * lc,
    )
    (tiles_s, tiles_p, tiles_pt, side_p, zt, md, md_p, near, far, resid) = kernel_call(
        setup_kernel,
        [
            shape((TILE_ROWS * count, TILE), BF16),
            shape((TILE_ROWS * count, TILE), BF16),
            shape((ms, 2 * TILE), BF16),
            shape((SIDE, ms), F32),
            shape((48, 2 * ms), BF16),
            face(BF16),
            face(BF16),
            face(BF16),
            face(BF16),
            shape((24, lc), F32),
        ],
        pack,
        pack_p,
        side_n,
        slave_weights,
        rigid,
        loads,
        field,
        fixed,
        kinv,
        anywhere=(8,),
        scratch=[
            kff,
            pltpu.VMEM((TILE, ms), F32),
            pltpu.VMEM((24, ms), F32),
            pltpu.VMEM((24, ms), F32),
            pltpu.VMEM((ms, lc), BF16),
            pltpu.VMEM((ms, lc), BF16),
            pltpu.SemaphoreType.DMA((2 * chunks,)),
        ],
        flops=8 * ms * ms * lc,
    )

    chip, group, spot, mode = np.meshgrid(
        np.arange(sub // 2), np.arange(grp), np.arange(4), np.arange(nr), indexing="ij"
    )
    source = (((2 * chip + spot - 1) % sub) * grp + group) * nr + mode
    source = jnp.asarray(source.reshape(1, -1), jnp.int32)
    coarse, floors = kernel_call(
        coarse_kernel,
        [shape((48, source.shape[1]), BF16), shape((8, ms), F32)],
        coarse_inverse,
        side_p,
        side_n,
        source,
        candidates,
        scratch=[pltpu.VMEM((24, nc), F32)],
        flops=2 * 48 * nc * source.shape[1],
    )

    klt, mrows, forms = kernel_call(
        forms_kernel,
        [shape((48, 2 * ms), BF16), shape((64, ms), BF16), shape((48, TILE), BF16)],
        zt,
        md,
        near,
        kinv,
        anywhere=(2, 3),
        scratch=[
            kff,
            pltpu.VMEM((TILE, 2 * ms), F32),
            pltpu.VMEM((TILE, TILE), F32),
            pltpu.SemaphoreType.DMA((2 * chunks,)),
        ],
        flops=10**11,
    )

    same_core = [
        [(2 * m + core) * grp + z for m in range(sub // 2) for z in range(grp)]
        for core in range(2)
    ]
    for turn in range(STEPS):
        (pieces,) = kernel_call(
            pair_kernel, [shape((chips, 24, lc), BF16)], resid, swapped(resid)
        )
        every = lax.all_to_all(
            pieces, AXES, 0, 0, tiled=True, axis_index_groups=same_core
        )
        far_r = swapped_out(far)
        near_r = swapped(near)
        (marker,) = kernel_call(
            marker_kernel, [shape((8, TILE), F32)], near, anywhere=(0,), flops=10**12
        )
        operands = (
            slave_weights, side_p, near, far, near_r, far_r, tiles_p, tiles_pt, tiles_s,
            mrows, zt, klt,
        )
        g, g_p, stats = kernel_call(
            gradient_kernel,
            [face(F32), face(F32), shape((64, lc), F32)],
            *operands,
            kinv,
            marker,
            anywhere=range(len(operands) + 2),
            anywhere_out=(0, 1),
            scratch=[kff]
            + [pltpu.VMEM(o.shape, o.dtype) for o in operands]
            + [
                pltpu.VMEM((ms, lc), F32),
                pltpu.VMEM((ms, lc), F32),
                pltpu.VMEM((2 * ms, lc), F32),
                pltpu.SemaphoreType.DMA((len(operands) + 2 * chunks + 2,)),
            ],
            flops=8 * ms * ms * lc,
        )
        stack, sums = kernel_call(
            project_kernel,
            [shape((TILE, lc), BF16), shape((2 * chips, 2, lc), F32)],
            every, coarse, forms, stats,
            flops=2 * 48 * every.shape[0] * every.shape[1] * lc,
        )
        d, d_p = kernel_call(
            direction_kernel,
            [face(F32), face(F32)],
            stack, g, g_p, md, md_p,
            flops=4 * ms * TILE * lc,
        )
        totals = lax.all_to_all(sums, AXES, 0, 0, tiled=True)
        operands = (
            slave_weights, floors, totals, field_p, d_p, tiles_pt, field, d, zt, fixed,
        )
        field, field_p, near, far, resid = kernel_call(
            functools.partial(step_kernel, turn == STEPS - 1),
            [face(F32), face(F32), face(BF16), face(BF16), shape((24, lc), F32)],
            *operands,
            loads,
            kinv,
            anywhere=range(len(operands) + 2),
            anywhere_out=(0, 1, 2, 3, 4),
            scratch=[kff]
            + [pltpu.VMEM(o.shape, o.dtype) for o in operands]
            + [pltpu.VMEM((ms, lc), BF16)] * 6
            + [
                pltpu.VMEM((24, lc), F32),
                pltpu.SemaphoreType.DMA((len(operands) + 2 * chunks + 7,)),
            ],
            flops=8 * ms * ms * lc,
        )
    um, us = near, far
    um_n = shifted(um, -1)
    (gradient,) = kernel_call(
        last_kernel, [face(F32)], us, um_n, slave_weights, tiles_s, flops=2 * 192 * ms * lc
    )
    return (field[None], gradient[None])


def solution(mesh):
    placed = (
        P(AXES, None, None),
        P(AXES, None, None),
        P(AXES, None, None),
        P(AXES, None),
        P(AXES, None),
        P(AXES, None, None),
        P(AXES, None),
        P(AXES, None),
        P(AXES, None, None),
    )
    return jax.shard_map(
        on_device,
        mesh=mesh,
        in_specs=placed,
        out_specs=(P(AXES, None, None), P(AXES, None, None)),
        check_vma=False,
    )
```

```python
import functools

import jax
import jax.numpy as jnp
import numpy as np
from jax import lax
from jax.experimental import pallas as pl
from jax.experimental.pallas import tpu as pltpu
from jax.sharding import PartitionSpec as P

STEPS = 3
AXES = ("sub", "grp")
F32, BF16 = jnp.float32, jnp.bfloat16
TILE = 128
TILE_ROWS = 192
HALO = 32
MIB = 1 << 20


def shifted(block, distance):
    size = lax.axis_size("sub")
    return lax.ppermute(block, "sub", [((i - distance) % size, i) for i in range(size)])


def swapped(block):
    size = lax.axis_size("sub")
    return lax.ppermute(block, "sub", [(i ^ 1, i) for i in range(size)])


def swapped_out(block):
    size = lax.axis_size("sub")
    other = [(i + 1 if i % 2 else i - 1) % size for i in range(size)]
    return lax.ppermute(block, "sub", [(other[i], i) for i in range(size)])


def is_odd():
    return lax.rem(lax.axis_index("sub"), 2) == 1


def rows_of(flat, count):
    width = flat.shape[1] // count
    return jnp.concatenate([flat[:, width * k : width * (k + 1)] for k in range(count)], axis=0)


def dot(left, right):
    return jnp.dot(left, right, preferred_element_type=F32)


def halves(value):
    high = value.astype(BF16).astype(F32)
    return high, (value - high).astype(BF16).astype(F32)


def column(row):
    return jnp.broadcast_to(row, (TILE, row.shape[1])).T


def mortar_times(tiles, values):
    count = values.shape[0] // TILE
    rows = TILE + 2 * HALO
    parts = [
        dot(tiles[rows * t : rows * (t + 1), :], values[TILE * t : TILE * (t + 1)])
        for t in range(count)
    ]
    out = []
    none = jnp.zeros((HALO, values.shape[1]), F32)
    for t in range(count):
        before = parts[t - 1][TILE + HALO :] if t else none
        after = parts[t + 1][TILE : TILE + HALO] if t + 1 < count else none
        gap = jnp.zeros((TILE - 2 * HALO, values.shape[1]), F32)
        out.append(parts[t][:TILE] + jnp.concatenate([before, gap, after], axis=0))
    return jnp.concatenate(out, axis=0)


def mortar_t_times(tiles_t, values):
    count = values.shape[0] // TILE
    none = jnp.zeros((HALO, values.shape[1]), BF16)
    fill = jnp.zeros((TILE - 2 * HALO, values.shape[1]), BF16)
    out = []
    for t in range(count):
        low, high = TILE * t, TILE * (t + 1)
        before = values[low - HALO : low] if t else none
        after = values[high : high + HALO] if t + 1 < count else none
        window = jnp.concatenate([values[low:high], before, after, fill], axis=0)
        out.append(dot(tiles_t[TILE * t : TILE * (t + 1), :], window))
    return jnp.concatenate(out, axis=0)


def unpacked(pack, t):
    edge = pack[160 * t : 160 * t + HALO, :].astype(F32)
    lane = lax.broadcasted_iota(jnp.int32, edge.shape, 1)
    above = jnp.where(lane < TILE // 2, edge, 0.0)
    below = jnp.where(lane < TILE // 2, 0.0, edge)
    middle = pack[160 * t + HALO : 160 * (t + 1), :].astype(F32)
    return jnp.concatenate([middle, above, below], axis=0)


def with_fill(tile):
    return jnp.concatenate([tile, jnp.zeros((TILE - 2 * HALO, TILE), F32)], axis=0)


class Moves:
    def __init__(self, sems):
        self.sems, self.used = sems, 0

    def start(self, source, target):
        copy = pltpu.make_async_copy(source, target, self.sems.at[self.used])
        self.used += 1
        copy.start()
        return copy


CHUNK = 256
SIDE = 32


def start_faces(moves, kinv, held, ms, first=0, end=None):
    copies = []
    for r in range(first, 2 * ms // CHUNK if end is None else end):
        row = r * CHUNK + (ms if r * CHUNK >= ms else 0)
        pair = []
        for to, at in ((0, 0), (ms, 2 * ms)):
            pair.append(
                moves.start(
                    kinv.at[pl.ds(row, CHUNK), pl.ds(at, ms)],
                    held.at[pl.ds(r * CHUNK, CHUNK), pl.ds(to, ms)],
                )
            )
        copies.append(pair)
    return copies


def solved(copies, held, load, fixed, zt, um, us, ms, start=0):
    both = 0.0
    for r, pair in enumerate(copies, start):
        for copy in pair:
            copy.wait()
        row = r * CHUNK
        u = (dot(held[row : row + CHUNK, :], load) + fixed[row : row + CHUNK, :]).astype(BF16)
        if row < ms:
            um[row : row + CHUNK, :] = u
        else:
            us[row - ms : row - ms + CHUNK, :] = u
        if zt is not None:
            both += dot(zt[:, row : row + CHUNK], u)
    return None if zt is None else both[:24] + both[24:]


def loads_of(push, scaled, loads_m, loads_s):
    master = (-push.astype(F32) - loads_m.astype(F32)).astype(BF16)
    slave = (scaled - loads_s.astype(F32)).astype(BF16)
    return jnp.concatenate([master, slave], axis=0)


def pack_kernel(mortar, seg, field, modes, coarse, weights, cand, out, behind):
    ms = mortar.shape[0]
    nr = coarse.shape[0]
    rigid = rows_of(modes, nr)
    count = ms // TILE
    ids = seg[...].astype(F32)
    ids_col = column(ids)
    none = jnp.zeros((HALO, TILE), F32)

    def masked(low, high, t):
        own = slice(TILE * t, TILE * (t + 1))
        same = ids_col[low:high] == ids[:, own]
        return jnp.where(same, mortar[low:high, own].astype(F32), 0.0)

    tiles = []
    for t in range(count):
        low, high = TILE * t, TILE * (t + 1)
        middle = masked(low, high, t)
        above = masked(low - HALO, low, t) if t else none
        below = masked(high, high + HALO, t) if t + 1 < count else none
        out[160 * t : 160 * t + HALO, :] = (above + below).astype(BF16)
        out[160 * t + HALO : 160 * (t + 1), :] = middle.astype(BF16)
        tile = jnp.concatenate([middle, above, below], axis=0)
        tiles.append(with_fill(tile).T.astype(BF16))
    push = mortar_t_times(jnp.concatenate(tiles, axis=0), field[...].astype(BF16))
    out[160 * count : 160 * count + ms, :] = push.astype(BF16)

    behind[...] = jnp.zeros_like(behind)
    behind[0:nr, :] = rigid[:, :ms]
    behind[8 : 8 + nr, :] = coarse[...]
    for t in range(count):
        own = slice(TILE * t, TILE * (t + 1))
        chosen = jnp.zeros((1, TILE), F32)
        if TILE * (t + 1) <= cand.shape[1]:
            chosen = cand[:, own].astype(F32)
        lanes = slice(ms + TILE * t, ms + TILE * (t + 1))
        pad = jnp.zeros((8 - nr, TILE), F32)
        rows = [rigid[:, lanes], pad, coarse[:, own], pad, weights[:, own], chosen]
        value = jnp.concatenate(rows + [jnp.zeros((SIDE - 18, TILE), F32)], axis=0)
        high, low = halves(value)
        base = 160 * count + ms + 2 * SIDE * t
        out[base : base + SIDE, :] = high.astype(BF16)
        out[base + SIDE : base + 2 * SIDE, :] = low.astype(BF16)


def side_rows(pack_p, ms):
    count = ms // TILE
    out = []
    for t in range(count):
        base = 160 * count + ms + 2 * SIDE * t
        high = pack_p[base : base + SIDE, :].astype(F32)
        out.append(high + pack_p[base + SIDE : base + 2 * SIDE, :].astype(F32))
    return jnp.concatenate(out, axis=1)


def fixed_kernel(loads, kinv, out, held, sems):
    ms = loads.shape[0] // 3
    moves = Moves(sems)
    copies = []
    for r in range(2 * ms // CHUNK):
        row = r * CHUNK + (ms if r * CHUNK >= ms else 0)
        copies.append(
            moves.start(
                kinv.at[pl.ds(row, CHUNK), pl.ds(ms, ms)], held.at[pl.ds(r * CHUNK, CHUNK), :]
            )
        )
    for r, copy in enumerate(copies):
        copy.wait()
        out[r * CHUNK : (r + 1) * CHUNK, :] = -dot(
            held[r * CHUNK : (r + 1) * CHUNK, :], loads[ms : 2 * ms, :]
        )


def setup_kernel(*refs):
    names, results = 8, 10
    kinv = refs[names]
    far_outs = refs[names + 1 : names + 1 + results]
    rest = refs[names + 1 + results :]
    local, rest = rest[:names], rest[names:]
    outs, rest = rest[:results], rest[results:]
    held, rows, modes, modes_p, um, us, sems = rest
    pack_p, field, weights, loads, rigid_row, pack, side_n, fixed = local
    tiles_s, tiles_p, tiles_pt, side_p, zt, md, md_p, near, far, resid = outs
    ms = weights.shape[1]
    nr = rigid_row.shape[1] // (2 * ms)
    odd = is_odd()
    count = ms // TILE
    span = TILE + 2 * HALO
    moves = Moves(sems)
    arrive = [moves.start(a, b) for a, b in zip(refs[:names], local)]
    copies = start_faces(moves, kinv, held, ms)
    leaving = []

    def wait(*which):
        for n in which:
            arrive[n].wait()

    def leave(*which):
        for n in which:
            leaving.append(moves.start(outs[n], far_outs[n]))

    wait(0)
    for t in range(count):
        tile = unpacked(pack_p, t)
        tiles_p[span * t : span * (t + 1), :] = tile.astype(BF16)
        tiles_pt[TILE * t : TILE * (t + 1), :] = with_fill(tile).T.astype(BF16)
    side_p[...] = side_rows(pack_p, ms)
    leave(1, 2, 3)

    push = pack_p[160 * count : 160 * count + ms, :]
    wait(1, 2, 3, 4)
    rigid = rows_of(rigid_row, nr)
    scaled = column(weights[...]) * field[...]
    load = loads_of(push, scaled, loads[:ms, :], loads[2 * ms :, :])
    wait(5, 6, 7)
    solved(copies, held, load, fixed, None, um, us, ms)
    near[...] = jnp.where(odd, um[...], us[...])
    far[...] = jnp.where(odd, us[...], um[...])
    leave(8, 7)
    for t in range(count):
        tiles_s[span * t : span * (t + 1), :] = unpacked(pack, t).astype(BF16)
    leave(0)

    def through(tiles, values):
        rows[...] = jnp.zeros_like(rows)
        high, low = halves(values)
        rows[0:nr, :] = high
        rows[8 : 8 + nr, :] = low
        moved = mortar_times(tiles, rows[...].T.astype(BF16)).T
        return moved[0:nr] + moved[8 : 8 + nr]

    modes[...] = jnp.zeros_like(modes)
    modes_p[...] = jnp.zeros_like(modes_p)
    modes[nr : 2 * nr, :] = rigid[:, ms:] * weights[...]
    modes[2 * nr : 3 * nr, :] = -through(tiles_s, side_n[0:nr, :])
    modes_p[0:nr, :] = side_p[0:nr, :] * side_p[16:17, :]
    modes_p[nr : 2 * nr, :] = -through(tiles_p, rigid[:, :ms])

    def placed(values):
        later = jnp.concatenate([values[18:24], values[0:18]], axis=0)
        return jnp.where(odd, later, values)

    def stacked(values):
        high, low = halves(values)
        rows[...] = jnp.zeros_like(rows)
        rows[0:24, :] = high
        rows[32:56, :] = low
        rows[64:88, :] = high
        return rows[...].T.astype(BF16)

    own = placed(modes[...])
    md[...] = stacked(own)
    columns = stacked(placed(modes_p[...]))
    md_p[...] = columns
    leave(5, 6)
    pushed = mortar_t_times(tiles_pt, columns).T
    high, low = halves(-(pushed[0:24] + pushed[32:56]))
    zt[0:24, :ms] = high.astype(BF16)
    zt[24:48, :ms] = low.astype(BF16)
    high, low = halves(own * weights[...])
    zt[0:24, ms:] = high.astype(BF16)
    zt[24:48, ms:] = low.astype(BF16)
    leave(4)
    both = dot(zt[:, :ms], um[...]) + dot(zt[:, ms:], us[...])
    resid[...] = both[:24] + both[24:]
    leave(9)
    for copy in leaving:
        copy.wait()


def coarse_rows(coarse, side_p, side_n, source, cand, out, floors, rows):
    nr, width = coarse.shape
    rows[...] = jnp.zeros_like(rows)
    rows[0:nr, :] = side_p[8 : 8 + nr, :]
    rows[nr : 2 * nr, :] = coarse[...]
    rows[2 * nr : 3 * nr, :] = side_n[8 : 8 + nr, :]
    later = jnp.concatenate([rows[18:24, :], rows[0:18, :]], axis=0)
    high, low = halves(jnp.where(is_odd(), later, rows[...]))
    both = jnp.concatenate([high, low], axis=0).astype(BF16)
    for n in range(0, out.shape[1], CHUNK):
        index = lax.broadcasted_iota(jnp.int32, (width, CHUNK), 0)
        pick = jnp.where(index == source[:, n : n + CHUNK], 1.0, 0.0).astype(BF16)
        out[:, n : n + CHUNK] = dot(both, pick).astype(BF16)

    floors[...] = jnp.zeros_like(floors)
    chosen = (cand[...].astype(F32), side_p[17:18, : cand.shape[1]])
    for t in range(floors.shape[1] // TILE):
        place = lax.broadcasted_iota(jnp.int32, (TILE, cand.shape[1]), 0) + TILE * t
        for n, which in enumerate(chosen):
            hit = jnp.where(place.astype(F32) == which, 1.0, 0.0)
            found = jnp.broadcast_to(jnp.max(hit, axis=1, keepdims=True), (TILE, TILE)).T
            floors[n : n + 1, TILE * t : TILE * (t + 1)] = jnp.where(
                found[0:1] > 0.0, 0.0, -jnp.inf
            )


def pair_kernel(resid, other, out):
    pair = (resid[...] + other[...]).astype(BF16)
    out[...] = jnp.broadcast_to(pair[None], out.shape)


def last_kernel(slave, um_n, tiles_s, grad):
    grad[...] = slave[...] - mortar_times(tiles_s, um_n[...])


def dot_rows(left, right):
    return lax.dot_general(left, right, (((1,), (1,)), ((), ())), preferred_element_type=F32)


def forms_kernel(
    zt, md, coarse, side_p, side_n, source, cand, near, kinv,
    klt, mrows, forms, coarse_of, floors,
    held, long, square, rows, sems,
):
    del near
    ms = md.shape[0]
    copies = start_faces(Moves(sems), kinv, held, ms)
    coarse_rows(coarse, side_p, side_n, source, cand, coarse_of, floors, rows)
    mrows[...] = md[...].astype(F32).T[0:64].astype(BF16)
    long[...] = jnp.zeros_like(long)
    long[0:24, :] = zt[0:24, :].astype(F32)
    long[32:56, :] = zt[24:48, :].astype(F32)
    columns = long[...].T.astype(BF16)
    for r, pair in enumerate(copies):
        for copy in pair:
            copy.wait()
        row = r * CHUNK
        long[:, row : row + CHUNK] = dot(held[row : row + CHUNK, :], columns).T
    high, low = halves(long[0:24, :] + long[32:56, :])
    klt[0:24, :] = high.astype(BF16)
    klt[24:48, :] = low.astype(BF16)

    def form(at, product):
        square[...] = jnp.zeros_like(square)
        square[0:24, 0:64] = product[0:24] + product[32:56]
        turned = square[...].T
        high, low = halves(turned[0:24] + turned[32:56])
        square[...] = jnp.zeros_like(square)
        square[0:24, :] = high
        square[32:56, :] = low
        square[64:88, :] = high
        forms[at : at + 24, :] = square[...].T[0:24].astype(BF16)

    gap = jnp.zeros((8, 2 * ms), BF16)
    left = jnp.concatenate([zt[0:24, :], gap, zt[24:48, :], gap], axis=0)
    right = jnp.concatenate([klt[0:24, :], gap, klt[24:48, :], gap], axis=0)
    form(0, dot_rows(mrows[...], mrows[...]))
    form(24, dot_rows(left, right))


def gradient_kernel(*refs):
    names = 12
    kinv, _, g_out, gp_out, stats = refs[names : names + 5]
    held = refs[names + 5]
    local = refs[names + 6 : 2 * names + 6]
    g, gp, solution, sems = refs[2 * names + 6 :]
    ms = g.shape[0]
    moves = Moves(sems)
    arrive = [moves.start(a, b) for a, b in zip(refs[:names], local)]
    copies = start_faces(moves, kinv, held, ms)
    weights, side_p, near, far, near_r, far_r, tiles_p, tiles_pt, tiles_s, mrows, zt, klt = local

    def wait(*which):
        for n in which:
            arrive[n].wait()

    wait(0, 1, 2, 3, 4, 5, 6)
    odd = is_odd()
    um, us = jnp.where(odd, near[...], far[...]), jnp.where(odd, far[...], near[...])
    um_n = jnp.where(odd, far_r[...], near_r[...])
    us_p = jnp.where(odd, near_r[...], far_r[...])
    wcol = column(weights[...])
    gp[...] = column(side_p[16:17, :]) * us_p.astype(F32) - mortar_times(tiles_p, um)
    out_p = moves.start(gp, gp_out)
    wait(7)
    master = (-mortar_t_times(tiles_pt, gp[...].astype(BF16))).astype(BF16)
    wait(8)
    g[...] = wcol * us.astype(F32) - mortar_times(tiles_s, um_n)
    out_s = moves.start(g, g_out)
    load = jnp.concatenate([master, (wcol * g[...]).astype(BF16)], axis=0)
    curve = jnp.zeros((CHUNK, TILE), F32)
    for r, pair in enumerate(copies):
        for copy in pair:
            copy.wait()
        row = r * CHUNK
        part = dot(held[row : row + CHUNK, :], load)
        solution[row : row + CHUNK, :] = part
        curve += load[row : row + CHUNK].astype(F32) * part
    wait(9, 10, 11)
    stats[...] = jnp.zeros_like(stats)
    stats[0:1, :] = jnp.sum(g[...] * g[...], axis=0, keepdims=True)
    stats[1:2, :] = jnp.sum(curve, axis=0, keepdims=True)
    high, low = halves(g[...])
    first = dot(mrows[...], high.astype(BF16))
    second = dot(mrows[0:32, :], low.astype(BF16))
    stats[8:32, :] = first[0:24] + first[32:56] + second[0:24]
    high, low = halves(solution[...])
    first = dot(zt[...], high.astype(BF16)) + dot(klt[...], load)
    second = dot(zt[0:32, :], low.astype(BF16))
    stats[32:56, :] = first[0:24] + first[24:48] + second[0:24]
    out_p.wait()
    out_s.wait()


def project_kernel(every, coarse, forms, stats, stack, sums):
    both = dot(coarse[...], every[...].reshape(coarse.shape[1], TILE))
    c = both[:24] + both[24:]
    high, low = halves(c)
    gap = jnp.zeros((8, TILE), F32)
    rest = jnp.zeros((TILE - 88, TILE), F32)
    operand = jnp.concatenate([high, gap, high, gap, low, rest], axis=0).astype(BF16)
    stack[...] = operand
    moved = dot(forms[...], operand)
    norm = stats[0:1, :] + jnp.sum(
        c * (moved[0:24] - 2.0 * stats[8:32, :]), axis=0, keepdims=True
    )
    curve = stats[1:2, :] + jnp.sum(c * (moved[24:48] - stats[32:56, :]), axis=0, keepdims=True)
    total = jnp.concatenate([norm, curve], axis=0)
    sums[...] = jnp.broadcast_to(total[None], sums.shape)


def direction_kernel(stack, g, gp, md, md_p, d, dp):
    d[...] = g[...] - dot(md[...], stack[...])
    dp[...] = gp[...] - dot(md_p[...], stack[...])


def marker_kernel(near, out):
    del near
    out[...] = jnp.zeros_like(out)


def step_kernel(final, *refs):
    names = 10
    loads, kinv = refs[names : names + 2]
    y_out, yp_out, near_out, far_out, resid_out = refs[names + 2 : names + 7]
    held = refs[names + 7]
    local = refs[names + 8 : 2 * names + 8]
    loads_m, loads_s, um, us, near, far, resid, sems = refs[2 * names + 8 :]
    weights, floors, sums, field_p, dp, tiles_pt, field, d, zt, fixed = local[:10]
    ms = d.shape[0]
    moves = Moves(sems)
    arrive = [moves.start(refs[n], local[n]) for n in range(8)]
    arrive_m = moves.start(loads.at[pl.ds(0, ms), :], loads_m)
    arrive_s = moves.start(loads.at[pl.ds(2 * ms, ms), :], loads_s)
    arrive += [moves.start(refs[n], local[n]) for n in range(8, 10)]
    copies = start_faces(moves, kinv, held, ms, 0, ms // CHUNK if final else None)

    def wait(*which):
        for n in which:
            arrive[n].wait()

    wait(0, 1)
    wcol = column(weights[...])
    floor, floor_p = column(floors[0:1, :]), column(floors[1:2, :])
    wait(2)
    total = jnp.sum(sums[...], axis=0)
    step = total[0:1] / total[1:2]
    wait(3, 4)
    field_p[...] = jnp.maximum(field_p[...] - step * dp[...], floor_p)
    out_p = None if final else moves.start(field_p, yp_out)
    wait(5)
    push = mortar_t_times(tiles_pt, field_p[...].astype(BF16)).astype(BF16)
    wait(6, 7)
    field[...] = jnp.maximum(field[...] - step * d[...], floor)
    out_s = moves.start(field, y_out)
    arrive_m.wait()
    arrive_s.wait()
    load = loads_of(push, wcol * field[...], loads_m[...], loads_s[...])
    wait(8, 9)
    if final:
        near[...] = load[:ms]
        far[...] = load[ms:]
        outs = [moves.start(near, near_out), moves.start(far, far_out)]
        solved(copies, held, load, fixed, None, um, us, ms)
        outs += [out_s, moves.start(um, yp_out)]
    else:
        resid[...] = solved(copies, held, load, fixed, zt, um, us, ms)
        odd = is_odd()
        near[...] = jnp.where(odd, um[...], us[...])
        far[...] = jnp.where(odd, us[...], um[...])
        outs = [moves.start(far, far_out), moves.start(near, near_out)]
        outs += [out_p, out_s, moves.start(resid, resid_out)]
    for copy in outs:
        copy.wait()


def slave_kernel(load_m, load_s, weights, fixed, kinv, out, held, us, sems):
    ms = weights.shape[1]
    copies = start_faces(Moves(sems), kinv, held, ms, ms // CHUNK)
    load = jnp.concatenate([load_m[...], load_s[...]], axis=0)
    solved(copies, held, load, fixed, None, None, us, ms, ms // CHUNK)
    out[...] = column(weights[...]) * us[...].astype(F32)


def shape(dims, dtype):
    return jax.ShapeDtypeStruct(dims, dtype)


def kernel_call(body, outs, *operands, anywhere=(), anywhere_out=(), scratch=(), flops=0):
    here = pl.BlockSpec(memory_space=pltpu.VMEM)
    far = pl.BlockSpec(memory_space=pl.ANY)
    moved = sum(int(np.prod(o.shape)) * o.dtype.itemsize for o in list(operands) + list(outs))
    return pl.pallas_call(
        body,
        out_shape=tuple(outs),
        in_specs=[far if n in anywhere else here for n in range(len(operands))],
        out_specs=tuple(far if n in anywhere_out else here for n in range(len(outs))),
        scratch_shapes=list(scratch),
        compiler_params=pltpu.CompilerParams(vmem_limit_bytes=64 * MIB),
        cost_estimate=pl.CostEstimate(flops=flops, bytes_accessed=moved, transcendentals=0),
    )(*operands)


def on_device(
    inverse_blocks,
    primal_loads,
    mortar_values,
    segment_ids,
    slave_weights,
    rigid_modes,
    coarse_inverse,
    candidates,
    start_multipliers,
):
    ms = mortar_values.shape[1]
    nr = rigid_modes.shape[1]
    nc = coarse_inverse.shape[1]
    lc = start_multipliers.shape[2]
    sub, grp = lax.axis_size("sub"), lax.axis_size("grp")
    chips = sub * grp // 2
    kinv = inverse_blocks[0]
    loads = primal_loads[0]
    rigid = rigid_modes.reshape(1, -1)
    field = start_multipliers[0]
    count = ms // TILE
    face = lambda dtype: shape((ms, lc), dtype)
    kff = pltpu.VMEM((2 * ms, 2 * ms), BF16)
    chunks = 2 * ms // CHUNK

    pack, behind = kernel_call(
        pack_kernel,
        [shape(((160 + 2 * SIDE) * count + ms, lc), BF16), shape((16, ms), F32)],
        mortar_values[0],
        segment_ids,
        field,
        rigid,
        coarse_inverse,
        slave_weights,
        candidates,
    )
    pack_p = shifted(pack, 1)
    side_n = shifted(behind, -1)
    field_p = shifted(field, 1)
    (fixed,) = kernel_call(
        fixed_kernel,
        [shape((2 * ms, lc), F32)],
        loads,
        kinv,
        anywhere=(1,),
        scratch=[pltpu.VMEM((2 * ms, ms), BF16), pltpu.SemaphoreType.DMA((chunks,))],
        flops=4 * ms * ms * lc,
    )
    outs = [
        shape((TILE_ROWS * count, TILE), BF16),
        shape((TILE_ROWS * count, TILE), BF16),
        shape((ms, 2 * TILE), BF16),
        shape((SIDE, ms), F32),
        shape((48, 2 * ms), BF16),
        face(BF16),
        face(BF16),
        face(BF16),
        face(BF16),
        shape((24, lc), F32),
    ]
    operands = (pack_p, field, slave_weights, loads, rigid, pack, side_n, fixed)
    (tiles_s, tiles_p, tiles_pt, side_p, zt, md, md_p, near, far, resid) = kernel_call(
        setup_kernel,
        outs,
        *operands,
        kinv,
        anywhere=range(len(operands) + 1),
        anywhere_out=range(len(outs)),
        scratch=[pltpu.VMEM(o.shape, o.dtype) for o in operands]
        + [pltpu.VMEM(o.shape, o.dtype) for o in outs]
        + [
            kff,
            pltpu.VMEM((TILE, ms), F32),
            pltpu.VMEM((24, ms), F32),
            pltpu.VMEM((24, ms), F32),
            pltpu.VMEM((ms, lc), BF16),
            pltpu.VMEM((ms, lc), BF16),
            pltpu.SemaphoreType.DMA((len(operands) + len(outs) + 2 * chunks,)),
        ],
        flops=8 * ms * ms * lc,
    )

    chip, group, spot, mode = np.meshgrid(
        np.arange(sub // 2), np.arange(grp), np.arange(4), np.arange(nr), indexing="ij"
    )
    source = (((2 * chip + spot - 1) % sub) * grp + group) * nr + mode
    source = jnp.asarray(source.reshape(1, -1), jnp.int32)
    klt, mrows, forms, coarse, floors = kernel_call(
        forms_kernel,
        [
            shape((48, 2 * ms), BF16),
            shape((64, ms), BF16),
            shape((48, TILE), BF16),
            shape((48, source.shape[1]), BF16),
            shape((8, ms), F32),
        ],
        zt,
        md,
        coarse_inverse,
        side_p,
        side_n,
        source,
        candidates,
        near,
        kinv,
        anywhere=(7, 8),
        scratch=[
            kff,
            pltpu.VMEM((TILE, 2 * ms), F32),
            pltpu.VMEM((TILE, TILE), F32),
            pltpu.VMEM((24, nc), F32),
            pltpu.SemaphoreType.DMA((2 * chunks,)),
        ],
        flops=10**11,
    )

    same_core = [
        [(2 * m + core) * grp + z for m in range(sub // 2) for z in range(grp)]
        for core in range(2)
    ]
    for turn in range(STEPS):
        (pieces,) = kernel_call(
            pair_kernel, [shape((chips, 24, lc), BF16)], resid, swapped(resid)
        )
        every = lax.all_to_all(
            pieces, AXES, 0, 0, tiled=True, axis_index_groups=same_core
        )
        far_r = swapped_out(far)
        near_r = swapped(near)
        (marker,) = kernel_call(
            marker_kernel, [shape((8, TILE), F32)], near, anywhere=(0,), flops=10**12
        )
        operands = (
            slave_weights, side_p, near, far, near_r, far_r, tiles_p, tiles_pt, tiles_s,
            mrows, zt, klt,
        )
        g, g_p, stats = kernel_call(
            gradient_kernel,
            [face(F32), face(F32), shape((64, lc), F32)],
            *operands,
            kinv,
            marker,
            anywhere=range(len(operands) + 2),
            anywhere_out=(0, 1),
            scratch=[kff]
            + [pltpu.VMEM(o.shape, o.dtype) for o in operands]
            + [
                pltpu.VMEM((ms, lc), F32),
                pltpu.VMEM((ms, lc), F32),
                pltpu.VMEM((2 * ms, lc), F32),
                pltpu.SemaphoreType.DMA((len(operands) + 2 * chunks + 2,)),
            ],
            flops=8 * ms * ms * lc,
        )
        stack, sums = kernel_call(
            project_kernel,
            [shape((TILE, lc), BF16), shape((2 * chips, 2, lc), F32)],
            every, coarse, forms, stats,
            flops=2 * 48 * every.shape[0] * every.shape[1] * lc,
        )
        d, d_p = kernel_call(
            direction_kernel,
            [face(F32), face(F32)],
            stack, g, g_p, md, md_p,
            flops=4 * ms * TILE * lc,
        )
        totals = lax.all_to_all(sums, AXES, 0, 0, tiled=True)
        operands = (
            slave_weights, floors, totals, field_p, d_p, tiles_pt, field, d, zt, fixed,
        )
        final = turn == STEPS - 1
        field, field_p, near, far, resid = kernel_call(
            functools.partial(step_kernel, final),
            [
                face(F32),
                face(BF16 if final else F32),
                face(BF16),
                face(BF16),
                shape((24, lc), F32),
            ],
            *operands,
            loads,
            kinv,
            anywhere=range(len(operands) + 2),
            anywhere_out=(0, 1, 2, 3, 4),
            scratch=[kff]
            + [pltpu.VMEM(o.shape, o.dtype) for o in operands]
            + [pltpu.VMEM((ms, lc), BF16)] * 6
            + [
                pltpu.VMEM((24, lc), F32),
                pltpu.SemaphoreType.DMA((len(operands) + 2 * chunks + 7,)),
            ],
            flops=8 * ms * ms * lc,
        )
    um_n = shifted(field_p, -1)
    (slave,) = kernel_call(
        slave_kernel,
        [face(F32)],
        near, far, slave_weights, fixed, kinv,
        anywhere=(4,),
        scratch=[kff, pltpu.VMEM((ms, lc), BF16), pltpu.SemaphoreType.DMA((chunks,))],
        flops=10**11,
    )
    (gradient,) = kernel_call(
        last_kernel, [face(F32)], slave, um_n, tiles_s, flops=2 * 192 * ms * lc
    )
    return (field[None], gradient[None])


def solution(mesh):
    placed = (
        P(AXES, None, None),
        P(AXES, None, None),
        P(AXES, None, None),
        P(AXES, None),
        P(AXES, None),
        P(AXES, None, None),
        P(AXES, None),
        P(AXES, None),
        P(AXES, None, None),
    )
    return jax.shard_map(
        on_device,
        mesh=mesh,
        in_specs=placed,
        out_specs=(P(AXES, None, None), P(AXES, None, None)),
        check_vma=False,
    )
```

```python
import functools

import jax
import jax.numpy as jnp
import numpy as np
from jax import lax
from jax.experimental import pallas as pl
from jax.experimental.pallas import tpu as pltpu
from jax.sharding import PartitionSpec as P

STEPS = 3
AXES = ("sub", "grp")
F32, BF16 = jnp.float32, jnp.bfloat16
TILE = 128
TILE_ROWS = 192
HALO = 32
MIB = 1 << 20


def shifted(block, distance):
    size = lax.axis_size("sub")
    return lax.ppermute(block, "sub", [((i - distance) % size, i) for i in range(size)])


def swapped(block):
    size = lax.axis_size("sub")
    return lax.ppermute(block, "sub", [(i ^ 1, i) for i in range(size)])


def swapped_out(block):
    size = lax.axis_size("sub")
    other = [(i + 1 if i % 2 else i - 1) % size for i in range(size)]
    return lax.ppermute(block, "sub", [(other[i], i) for i in range(size)])


def is_odd():
    return lax.rem(lax.axis_index("sub"), 2) == 1


def rows_of(flat, count):
    width = flat.shape[1] // count
    return jnp.concatenate([flat[:, width * k : width * (k + 1)] for k in range(count)], axis=0)


def dot(left, right):
    return jnp.dot(left, right, preferred_element_type=F32)


def halves(value):
    high = value.astype(BF16).astype(F32)
    return high, (value - high).astype(BF16).astype(F32)


def column(row):
    return jnp.broadcast_to(row, (TILE, row.shape[1])).T


def mortar_times(tiles, values):
    count = values.shape[0] // TILE
    rows = TILE + 2 * HALO
    parts = [
        dot(tiles[rows * t : rows * (t + 1), :], values[TILE * t : TILE * (t + 1)])
        for t in range(count)
    ]
    out = []
    none = jnp.zeros((HALO, values.shape[1]), F32)
    for t in range(count):
        before = parts[t - 1][TILE + HALO :] if t else none
        after = parts[t + 1][TILE : TILE + HALO] if t + 1 < count else none
        gap = jnp.zeros((TILE - 2 * HALO, values.shape[1]), F32)
        out.append(parts[t][:TILE] + jnp.concatenate([before, gap, after], axis=0))
    return jnp.concatenate(out, axis=0)


def mortar_t_times(tiles_t, values):
    count = values.shape[0] // TILE
    none = jnp.zeros((HALO, values.shape[1]), BF16)
    fill = jnp.zeros((TILE - 2 * HALO, values.shape[1]), BF16)
    out = []
    for t in range(count):
        low, high = TILE * t, TILE * (t + 1)
        before = values[low - HALO : low] if t else none
        after = values[high : high + HALO] if t + 1 < count else none
        window = jnp.concatenate([values[low:high], before, after, fill], axis=0)
        out.append(dot(tiles_t[TILE * t : TILE * (t + 1), :], window))
    return jnp.concatenate(out, axis=0)


def unpacked(pack, t):
    edge = pack[160 * t : 160 * t + HALO, :].astype(F32)
    lane = lax.broadcasted_iota(jnp.int32, edge.shape, 1)
    above = jnp.where(lane < TILE // 2, edge, 0.0)
    below = jnp.where(lane < TILE // 2, 0.0, edge)
    middle = pack[160 * t + HALO : 160 * (t + 1), :].astype(F32)
    return jnp.concatenate([middle, above, below], axis=0)


def with_fill(tile):
    return jnp.concatenate([tile, jnp.zeros((TILE - 2 * HALO, TILE), F32)], axis=0)


class Moves:
    def __init__(self, sems):
        self.sems, self.used = sems, 0

    def start(self, source, target):
        copy = pltpu.make_async_copy(source, target, self.sems.at[self.used])
        self.used += 1
        copy.start()
        return copy


CHUNK = 256
SIDE = 32


def start_faces(moves, kinv, held, ms, first=0, end=None):
    copies = []
    for r in range(first, 2 * ms // CHUNK if end is None else end):
        row = r * CHUNK + (ms if r * CHUNK >= ms else 0)
        pair = []
        for to, at in ((0, 0), (ms, 2 * ms)):
            pair.append(
                moves.start(
                    kinv.at[pl.ds(row, CHUNK), pl.ds(at, ms)],
                    held.at[pl.ds(r * CHUNK, CHUNK), pl.ds(to, ms)],
                )
            )
        copies.append(pair)
    return copies


def solved(copies, held, load, fixed, zt, um, us, ms, start=0):
    for r, pair in enumerate(copies, start):
        for copy in pair:
            copy.wait()
        row = r * CHUNK
        u = (dot(held[row : row + CHUNK, :], load) + fixed[row : row + CHUNK, :]).astype(BF16)
        if row < ms:
            um[row : row + CHUNK, :] = u
        else:
            us[row - ms : row - ms + CHUNK, :] = u
    if zt is None:
        return None
    both = dot(zt[:, :ms], um[...]) + dot(zt[:, ms:], us[...])
    return both[:24] + both[24:]


def loads_of(push, scaled, loads_m, loads_s):
    master = (-push.astype(F32) - loads_m.astype(F32)).astype(BF16)
    slave = (scaled - loads_s.astype(F32)).astype(BF16)
    return jnp.concatenate([master, slave], axis=0)


def pack_kernel(mortar, seg, field, modes, coarse, weights, cand, out, behind):
    ms = mortar.shape[0]
    nr = coarse.shape[0]
    rigid = rows_of(modes, nr)
    count = ms // TILE
    ids = seg[...].astype(F32)
    ids_col = column(ids)
    none = jnp.zeros((HALO, TILE), F32)

    def masked(low, high, t):
        own = slice(TILE * t, TILE * (t + 1))
        same = ids_col[low:high] == ids[:, own]
        return jnp.where(same, mortar[low:high, own].astype(F32), 0.0)

    tiles = []
    for t in range(count):
        low, high = TILE * t, TILE * (t + 1)
        middle = masked(low, high, t)
        above = masked(low - HALO, low, t) if t else none
        below = masked(high, high + HALO, t) if t + 1 < count else none
        out[160 * t : 160 * t + HALO, :] = (above + below).astype(BF16)
        out[160 * t + HALO : 160 * (t + 1), :] = middle.astype(BF16)
        tile = jnp.concatenate([middle, above, below], axis=0)
        tiles.append(with_fill(tile).T.astype(BF16))
    push = mortar_t_times(jnp.concatenate(tiles, axis=0), field[...].astype(BF16))
    out[160 * count : 160 * count + ms, :] = push.astype(BF16)

    behind[...] = jnp.zeros_like(behind)
    behind[0:nr, :] = rigid[:, :ms]
    behind[8 : 8 + nr, :] = coarse[...]
    for t in range(count):
        own = slice(TILE * t, TILE * (t + 1))
        chosen = jnp.zeros((1, TILE), F32)
        if TILE * (t + 1) <= cand.shape[1]:
            chosen = cand[:, own].astype(F32)
        lanes = slice(ms + TILE * t, ms + TILE * (t + 1))
        pad = jnp.zeros((8 - nr, TILE), F32)
        rows = [rigid[:, lanes], pad, coarse[:, own], pad, weights[:, own], chosen]
        value = jnp.concatenate(rows + [jnp.zeros((SIDE - 18, TILE), F32)], axis=0)
        high, low = halves(value)
        base = 160 * count + ms + 2 * SIDE * t
        out[base : base + SIDE, :] = high.astype(BF16)
        out[base + SIDE : base + 2 * SIDE, :] = low.astype(BF16)


def side_rows(pack_p, ms):
    count = ms // TILE
    out = []
    for t in range(count):
        base = 160 * count + ms + 2 * SIDE * t
        high = pack_p[base : base + SIDE, :].astype(F32)
        out.append(high + pack_p[base + SIDE : base + 2 * SIDE, :].astype(F32))
    return jnp.concatenate(out, axis=1)


def fixed_kernel(loads, kinv, out, held, sems):
    ms = loads.shape[0] // 3
    moves = Moves(sems)
    copies = []
    for r in range(2 * ms // CHUNK):
        row = r * CHUNK + (ms if r * CHUNK >= ms else 0)
        copies.append(
            moves.start(
                kinv.at[pl.ds(row, CHUNK), pl.ds(ms, ms)], held.at[pl.ds(r * CHUNK, CHUNK), :]
            )
        )
    for r, copy in enumerate(copies):
        copy.wait()
        out[r * CHUNK : (r + 1) * CHUNK, :] = -dot(
            held[r * CHUNK : (r + 1) * CHUNK, :], loads[ms : 2 * ms, :]
        )


def setup_kernel(*refs):
    names, results = 8, 10
    kinv = refs[names]
    far_outs = refs[names + 1 : names + 1 + results]
    rest = refs[names + 1 + results :]
    local, rest = rest[:names], rest[names:]
    outs, rest = rest[:results], rest[results:]
    held, rows, modes, modes_p, um, us, sems = rest
    pack_p, weights, rigid_row, side_n, pack, field, loads, fixed = local
    tiles_s, tiles_p, tiles_pt, side_p, zt, md, md_p, near, far, resid = outs
    ms = weights.shape[1]
    nr = rigid_row.shape[1] // (2 * ms)
    odd = is_odd()
    count = ms // TILE
    span = TILE + 2 * HALO
    moves = Moves(sems)
    arrive = [moves.start(a, b) for a, b in zip(refs[:names], local)]
    copies = start_faces(moves, kinv, held, ms)
    leaving = []

    def wait(*which):
        for n in which:
            arrive[n].wait()

    def leave(*which):
        for n in which:
            leaving.append(moves.start(outs[n], far_outs[n]))

    wait(0)
    for t in range(count):
        tile = unpacked(pack_p, t)
        tiles_p[span * t : span * (t + 1), :] = tile.astype(BF16)
        tiles_pt[TILE * t : TILE * (t + 1), :] = with_fill(tile).T.astype(BF16)
    side_p[...] = side_rows(pack_p, ms)
    leave(1, 2, 3)

    wait(1, 2, 3, 4)
    rigid = rows_of(rigid_row, nr)
    for t in range(count):
        tiles_s[span * t : span * (t + 1), :] = unpacked(pack, t).astype(BF16)
    leave(0)

    def through(tiles, values):
        rows[...] = jnp.zeros_like(rows)
        high, low = halves(values)
        rows[0:nr, :] = high
        rows[8 : 8 + nr, :] = low
        moved = mortar_times(tiles, rows[...].T.astype(BF16)).T
        return moved[0:nr] + moved[8 : 8 + nr]

    modes[...] = jnp.zeros_like(modes)
    modes_p[...] = jnp.zeros_like(modes_p)
    modes[nr : 2 * nr, :] = rigid[:, ms:] * weights[...]
    modes[2 * nr : 3 * nr, :] = -through(tiles_s, side_n[0:nr, :])
    modes_p[0:nr, :] = side_p[0:nr, :] * side_p[16:17, :]
    modes_p[nr : 2 * nr, :] = -through(tiles_p, rigid[:, :ms])

    def placed(values):
        later = jnp.concatenate([values[18:24], values[0:18]], axis=0)
        return jnp.where(odd, later, values)

    def stacked(values):
        high, low = halves(values)
        rows[...] = jnp.zeros_like(rows)
        rows[0:24, :] = high
        rows[32:56, :] = low
        rows[64:88, :] = high
        return rows[...].T.astype(BF16)

    own = placed(modes[...])
    md[...] = stacked(own)
    columns = stacked(placed(modes_p[...]))
    md_p[...] = columns
    leave(5, 6)
    pushed = mortar_t_times(tiles_pt, columns).T
    high, low = halves(-(pushed[0:24] + pushed[32:56]))
    zt[0:24, :ms] = high.astype(BF16)
    zt[24:48, :ms] = low.astype(BF16)
    high, low = halves(own * weights[...])
    zt[0:24, ms:] = high.astype(BF16)
    zt[24:48, ms:] = low.astype(BF16)
    leave(4)
    push = pack_p[160 * count : 160 * count + ms, :]
    wait(5, 6, 7)
    scaled = column(weights[...]) * field[...]
    load = loads_of(push, scaled, loads[:ms, :], loads[2 * ms :, :])
    resid[...] = solved(copies, held, load, fixed, zt, um, us, ms)
    near[...] = jnp.where(odd, um[...], us[...])
    far[...] = jnp.where(odd, us[...], um[...])
    leave(9, 8, 7)
    for copy in leaving:
        copy.wait()


def coarse_rows(coarse, side_p, side_n, source, cand, out, floors, rows):
    nr, width = coarse.shape
    rows[...] = jnp.zeros_like(rows)
    rows[0:nr, :] = side_p[8 : 8 + nr, :]
    rows[nr : 2 * nr, :] = coarse[...]
    rows[2 * nr : 3 * nr, :] = side_n[8 : 8 + nr, :]
    later = jnp.concatenate([rows[18:24, :], rows[0:18, :]], axis=0)
    high, low = halves(jnp.where(is_odd(), later, rows[...]))
    both = jnp.concatenate([high, low], axis=0).astype(BF16)
    count = width // TILE
    for n in range(out.shape[1] // CHUNK):
        near_by = [(n + k) % count for k in (-1, 0, 1)]
        left = jnp.concatenate([both[:, TILE * t : TILE * (t + 1)] for t in near_by], axis=1)
        wanted = source[:, n * CHUNK : (n + 1) * CHUNK]
        picks = []
        for t in near_by:
            index = lax.broadcasted_iota(jnp.int32, (TILE, CHUNK), 0) + TILE * t
            picks.append(jnp.where(index == wanted, 1.0, 0.0).astype(BF16))
        out[:, n * CHUNK : (n + 1) * CHUNK] = dot(left, jnp.concatenate(picks, axis=0)).astype(
            BF16
        )

    floors[...] = jnp.zeros_like(floors)
    chosen = (cand[...].astype(F32), side_p[17:18, : cand.shape[1]])
    for t in range(floors.shape[1] // TILE):
        place = lax.broadcasted_iota(jnp.int32, (TILE, cand.shape[1]), 0) + TILE * t
        for n, which in enumerate(chosen):
            hit = jnp.where(place.astype(F32) == which, 1.0, 0.0)
            found = jnp.broadcast_to(jnp.max(hit, axis=1, keepdims=True), (TILE, TILE)).T
            floors[n : n + 1, TILE * t : TILE * (t + 1)] = jnp.where(
                found[0:1] > 0.0, 0.0, -jnp.inf
            )


def pair_kernel(resid, other, out):
    pair = (resid[...] + other[...]).astype(BF16)
    out[...] = jnp.broadcast_to(pair[None], out.shape)


def last_kernel(slave, um_n, tiles_s, grad):
    grad[...] = slave[...] - mortar_times(tiles_s, um_n[...])


def dot_rows(left, right):
    return lax.dot_general(left, right, (((1,), (1,)), ((), ())), preferred_element_type=F32)


def forms_kernel(
    zt, md, coarse, side_p, side_n, source, cand, near, kinv,
    klt, mrows, forms, coarse_of, floors,
    held, long, square, rows, sems,
):
    del near
    ms = md.shape[0]
    copies = start_faces(Moves(sems), kinv, held, ms)
    coarse_rows(coarse, side_p, side_n, source, cand, coarse_of, floors, rows)
    mrows[...] = md[...].astype(F32).T[0:64].astype(BF16)
    long[...] = jnp.zeros_like(long)
    long[0:24, :] = zt[0:24, :].astype(F32)
    long[32:56, :] = zt[24:48, :].astype(F32)
    columns = long[...].T.astype(BF16)
    last = None
    for r, pair in enumerate(copies):
        for copy in pair:
            copy.wait()
        row = r * CHUNK
        part = dot(held[row : row + CHUNK, :], columns)
        if last is not None:
            long[:, row - CHUNK : row] = last.T
        last = part
    long[:, 2 * ms - CHUNK :] = last.T
    high, low = halves(long[0:24, :] + long[32:56, :])
    klt[0:24, :] = high.astype(BF16)
    klt[24:48, :] = low.astype(BF16)

    def form(at, product):
        square[...] = jnp.zeros_like(square)
        square[0:24, 0:64] = product[0:24] + product[32:56]
        turned = square[...].T
        high, low = halves(turned[0:24] + turned[32:56])
        square[...] = jnp.zeros_like(square)
        square[0:24, :] = high
        square[32:56, :] = low
        square[64:88, :] = high
        forms[at : at + 24, :] = square[...].T[0:24].astype(BF16)

    gap = jnp.zeros((8, 2 * ms), BF16)
    left = jnp.concatenate([zt[0:24, :], gap, zt[24:48, :], gap], axis=0)
    right = jnp.concatenate([klt[0:24, :], gap, klt[24:48, :], gap], axis=0)
    form(0, dot_rows(mrows[...], mrows[...]))
    form(24, dot_rows(left, right))


def gradient_kernel(*refs):
    names = 12
    kinv, _, g_out, gp_out, stats = refs[names : names + 5]
    held = refs[names + 5]
    local = refs[names + 6 : 2 * names + 6]
    g, gp, solution, sems = refs[2 * names + 6 :]
    ms = g.shape[0]
    moves = Moves(sems)
    arrive = [moves.start(a, b) for a, b in zip(refs[:9], local[:9])]
    copies = start_faces(moves, kinv, held, ms)
    arrive += [moves.start(a, b) for a, b in zip(refs[9:names], local[9:])]
    weights, side_p, near, far, near_r, far_r, tiles_p, tiles_pt, tiles_s, mrows, zt, klt = local

    def wait(*which):
        for n in which:
            arrive[n].wait()

    wait(0, 1, 2, 3, 4, 5, 6)
    odd = is_odd()
    um, us = jnp.where(odd, near[...], far[...]), jnp.where(odd, far[...], near[...])
    um_n = jnp.where(odd, far_r[...], near_r[...])
    us_p = jnp.where(odd, near_r[...], far_r[...])
    wcol = column(weights[...])
    gp[...] = column(side_p[16:17, :]) * us_p.astype(F32) - mortar_times(tiles_p, um)
    out_p = moves.start(gp, gp_out)
    wait(7)
    master = (-mortar_t_times(tiles_pt, gp[...].astype(BF16))).astype(BF16)
    wait(8)
    g[...] = wcol * us.astype(F32) - mortar_times(tiles_s, um_n)
    out_s = moves.start(g, g_out)
    load = jnp.concatenate([master, (wcol * g[...]).astype(BF16)], axis=0)
    curve = jnp.zeros((CHUNK, TILE), F32)
    for r, pair in enumerate(copies):
        for copy in pair:
            copy.wait()
        row = r * CHUNK
        part = dot(held[row : row + CHUNK, :], load)
        solution[row : row + CHUNK, :] = part
        curve += load[row : row + CHUNK].astype(F32) * part
    wait(9, 10, 11)
    stats[...] = jnp.zeros_like(stats)
    stats[0:1, :] = jnp.sum(g[...] * g[...], axis=0, keepdims=True)
    stats[1:2, :] = jnp.sum(curve, axis=0, keepdims=True)
    high, low = halves(g[...])
    first = dot(mrows[...], high.astype(BF16))
    second = dot(mrows[0:32, :], low.astype(BF16))
    stats[8:32, :] = first[0:24] + first[32:56] + second[0:24]
    high, low = halves(solution[...])
    first = dot(zt[...], high.astype(BF16)) + dot(klt[...], load)
    second = dot(zt[0:32, :], low.astype(BF16))
    stats[32:56, :] = first[0:24] + first[24:48] + second[0:24]
    out_p.wait()
    out_s.wait()


def project_kernel(every, coarse, forms, stats, stack, sums):
    both = dot(coarse[...], every[...].reshape(coarse.shape[1], TILE))
    c = both[:24] + both[24:]
    high, low = halves(c)
    gap = jnp.zeros((8, TILE), F32)
    rest = jnp.zeros((TILE - 88, TILE), F32)
    operand = jnp.concatenate([high, gap, high, gap, low, rest], axis=0).astype(BF16)
    stack[...] = operand
    moved = dot(forms[...], operand)
    norm = stats[0:1, :] + jnp.sum(
        c * (moved[0:24] - 2.0 * stats[8:32, :]), axis=0, keepdims=True
    )
    curve = stats[1:2, :] + jnp.sum(c * (moved[24:48] - stats[32:56, :]), axis=0, keepdims=True)
    total = jnp.concatenate([norm, curve], axis=0)
    sums[...] = jnp.broadcast_to(total[None], sums.shape)


def direction_kernel(stack, g, gp, md, md_p, d, dp):
    d[...] = g[...] - dot(md[...], stack[...])
    dp[...] = gp[...] - dot(md_p[...], stack[...])


def marker_kernel(near, out):
    del near
    out[...] = jnp.zeros_like(out)


def step_kernel(final, *refs):
    names = 10
    loads, kinv = refs[names : names + 2]
    y_out, yp_out, near_out, far_out, resid_out = refs[names + 2 : names + 7]
    held = refs[names + 7]
    local = refs[names + 8 : 2 * names + 8]
    loads_m, loads_s, um, us, near, far, resid, sems = refs[2 * names + 8 :]
    weights, floors, sums, field_p, dp, tiles_pt, field, d, zt, fixed = local[:10]
    ms = d.shape[0]
    moves = Moves(sems)
    arrive = [moves.start(refs[n], local[n]) for n in range(8)]
    arrive_m = moves.start(loads.at[pl.ds(0, ms), :], loads_m)
    arrive_s = moves.start(loads.at[pl.ds(2 * ms, ms), :], loads_s)
    arrive += [moves.start(refs[n], local[n]) for n in range(8, 10)]
    copies = start_faces(moves, kinv, held, ms, 0, ms // CHUNK if final else None)

    def wait(*which):
        for n in which:
            arrive[n].wait()

    wait(0, 1)
    wcol = column(weights[...])
    floor, floor_p = column(floors[0:1, :]), column(floors[1:2, :])
    wait(2)
    total = jnp.sum(sums[...], axis=0)
    step = total[0:1] / total[1:2]
    wait(3, 4)
    field_p[...] = jnp.maximum(field_p[...] - step * dp[...], floor_p)
    out_p = None if final else moves.start(field_p, yp_out)
    wait(5)
    push = mortar_t_times(tiles_pt, field_p[...].astype(BF16)).astype(BF16)
    wait(6, 7)
    field[...] = jnp.maximum(field[...] - step * d[...], floor)
    out_s = moves.start(field, y_out)
    arrive_m.wait()
    arrive_s.wait()
    load = loads_of(push, wcol * field[...], loads_m[...], loads_s[...])
    wait(8, 9)
    if final:
        near[...] = load[:ms]
        far[...] = load[ms:]
        outs = [moves.start(near, near_out), moves.start(far, far_out)]
        solved(copies, held, load, fixed, None, um, us, ms)
        outs += [out_s, moves.start(um, yp_out)]
    else:
        resid[...] = solved(copies, held, load, fixed, zt, um, us, ms)
        odd = is_odd()
        near[...] = jnp.where(odd, um[...], us[...])
        far[...] = jnp.where(odd, us[...], um[...])
        outs = [moves.start(far, far_out), moves.start(near, near_out)]
        outs += [out_p, out_s, moves.start(resid, resid_out)]
    for copy in outs:
        copy.wait()


def slave_kernel(load_m, load_s, weights, fixed, kinv, out, held, us, sems):
    ms = weights.shape[1]
    copies = start_faces(Moves(sems), kinv, held, ms, ms // CHUNK)
    load = jnp.concatenate([load_m[...], load_s[...]], axis=0)
    solved(copies, held, load, fixed, None, None, us, ms, ms // CHUNK)
    out[...] = column(weights[...]) * us[...].astype(F32)


def shape(dims, dtype):
    return jax.ShapeDtypeStruct(dims, dtype)


def kernel_call(body, outs, *operands, anywhere=(), anywhere_out=(), scratch=(), flops=0):
    here = pl.BlockSpec(memory_space=pltpu.VMEM)
    far = pl.BlockSpec(memory_space=pl.ANY)
    moved = sum(int(np.prod(o.shape)) * o.dtype.itemsize for o in list(operands) + list(outs))
    return pl.pallas_call(
        body,
        out_shape=tuple(outs),
        in_specs=[far if n in anywhere else here for n in range(len(operands))],
        out_specs=tuple(far if n in anywhere_out else here for n in range(len(outs))),
        scratch_shapes=list(scratch),
        compiler_params=pltpu.CompilerParams(vmem_limit_bytes=64 * MIB),
        cost_estimate=pl.CostEstimate(flops=flops, bytes_accessed=moved, transcendentals=0),
    )(*operands)


def on_device(
    inverse_blocks,
    primal_loads,
    mortar_values,
    segment_ids,
    slave_weights,
    rigid_modes,
    coarse_inverse,
    candidates,
    start_multipliers,
):
    ms = mortar_values.shape[1]
    nr = rigid_modes.shape[1]
    nc = coarse_inverse.shape[1]
    lc = start_multipliers.shape[2]
    sub, grp = lax.axis_size("sub"), lax.axis_size("grp")
    chips = sub * grp // 2
    kinv = inverse_blocks[0]
    loads = primal_loads[0]
    rigid = rigid_modes.reshape(1, -1)
    field = start_multipliers[0]
    count = ms // TILE
    face = lambda dtype: shape((ms, lc), dtype)
    kff = pltpu.VMEM((2 * ms, 2 * ms), BF16)
    chunks = 2 * ms // CHUNK

    pack, behind = kernel_call(
        pack_kernel,
        [shape(((160 + 2 * SIDE) * count + ms, lc), BF16), shape((16, ms), F32)],
        mortar_values[0],
        segment_ids,
        field,
        rigid,
        coarse_inverse,
        slave_weights,
        candidates,
    )
    pack_p = shifted(pack, 1)
    side_n = shifted(behind, -1)
    field_p = shifted(field, 1)
    (fixed,) = kernel_call(
        fixed_kernel,
        [shape((2 * ms, lc), F32)],
        loads,
        kinv,
        anywhere=(1,),
        scratch=[pltpu.VMEM((2 * ms, ms), BF16), pltpu.SemaphoreType.DMA((chunks,))],
        flops=4 * ms * ms * lc,
    )
    outs = [
        shape((TILE_ROWS * count, TILE), BF16),
        shape((TILE_ROWS * count, TILE), BF16),
        shape((ms, 2 * TILE), BF16),
        shape((SIDE, ms), F32),
        shape((48, 2 * ms), BF16),
        face(BF16),
        face(BF16),
        face(BF16),
        face(BF16),
        shape((24, lc), F32),
    ]
    operands = (pack_p, slave_weights, rigid, side_n, pack, field, loads, fixed)
    (tiles_s, tiles_p, tiles_pt, side_p, zt, md, md_p, near, far, resid) = kernel_call(
        setup_kernel,
        outs,
        *operands,
        kinv,
        anywhere=range(len(operands) + 1),
        anywhere_out=range(len(outs)),
        scratch=[pltpu.VMEM(o.shape, o.dtype) for o in operands]
        + [pltpu.VMEM(o.shape, o.dtype) for o in outs]
        + [
            kff,
            pltpu.VMEM((TILE, ms), F32),
            pltpu.VMEM((24, ms), F32),
            pltpu.VMEM((24, ms), F32),
            pltpu.VMEM((ms, lc), BF16),
            pltpu.VMEM((ms, lc), BF16),
            pltpu.SemaphoreType.DMA((len(operands) + len(outs) + 2 * chunks,)),
        ],
        flops=8 * ms * ms * lc,
    )

    chip, group, spot, mode = np.meshgrid(
        np.arange(sub // 2), np.arange(grp), np.arange(4), np.arange(nr), indexing="ij"
    )
    source = (((2 * chip + spot - 1) % sub) * grp + group) * nr + mode
    source = jnp.asarray(source.reshape(1, -1), jnp.int32)
    klt, mrows, forms, coarse, floors = kernel_call(
        forms_kernel,
        [
            shape((48, 2 * ms), BF16),
            shape((64, ms), BF16),
            shape((48, TILE), BF16),
            shape((48, source.shape[1]), BF16),
            shape((8, ms), F32),
        ],
        zt,
        md,
        coarse_inverse,
        side_p,
        side_n,
        source,
        candidates,
        near,
        kinv,
        anywhere=(7, 8),
        scratch=[
            kff,
            pltpu.VMEM((TILE, 2 * ms), F32),
            pltpu.VMEM((TILE, TILE), F32),
            pltpu.VMEM((24, nc), F32),
            pltpu.SemaphoreType.DMA((2 * chunks,)),
        ],
        flops=10**11,
    )

    same_core = [
        [(2 * m + core) * grp + z for m in range(sub // 2) for z in range(grp)]
        for core in range(2)
    ]
    for turn in range(STEPS):
        (pieces,) = kernel_call(
            pair_kernel, [shape((chips, 24, lc), BF16)], resid, swapped(resid)
        )
        every = lax.all_to_all(
            pieces, AXES, 0, 0, tiled=True, axis_index_groups=same_core
        )
        far_r = swapped_out(far)
        near_r = swapped(near)
        (marker,) = kernel_call(
            marker_kernel, [shape((8, TILE), F32)], near, anywhere=(0,), flops=10**12
        )
        operands = (
            slave_weights, side_p, near, far, near_r, far_r, tiles_p, tiles_pt, tiles_s,
            mrows, zt, klt,
        )
        g, g_p, stats = kernel_call(
            gradient_kernel,
            [face(F32), face(F32), shape((64, lc), F32)],
            *operands,
            kinv,
            marker,
            anywhere=range(len(operands) + 2),
            anywhere_out=(0, 1),
            scratch=[kff]
            + [pltpu.VMEM(o.shape, o.dtype) for o in operands]
            + [
                pltpu.VMEM((ms, lc), F32),
                pltpu.VMEM((ms, lc), F32),
                pltpu.VMEM((2 * ms, lc), F32),
                pltpu.SemaphoreType.DMA((len(operands) + 2 * chunks + 2,)),
            ],
            flops=8 * ms * ms * lc,
        )
        stack, sums = kernel_call(
            project_kernel,
            [shape((TILE, lc), BF16), shape((2 * chips, 2, lc), F32)],
            every, coarse, forms, stats,
            flops=2 * 48 * every.shape[0] * every.shape[1] * lc,
        )
        d, d_p = kernel_call(
            direction_kernel,
            [face(F32), face(F32)],
            stack, g, g_p, md, md_p,
            flops=4 * ms * TILE * lc,
        )
        totals = lax.all_to_all(sums, AXES, 0, 0, tiled=True)
        operands = (
            slave_weights, floors, totals, field_p, d_p, tiles_pt, field, d, zt, fixed,
        )
        final = turn == STEPS - 1
        field, field_p, near, far, resid = kernel_call(
            functools.partial(step_kernel, final),
            [
                face(F32),
                face(BF16 if final else F32),
                face(BF16),
                face(BF16),
                shape((24, lc), F32),
            ],
            *operands,
            loads,
            kinv,
            anywhere=range(len(operands) + 2),
            anywhere_out=(0, 1, 2, 3, 4),
            scratch=[kff]
            + [pltpu.VMEM(o.shape, o.dtype) for o in operands]
            + [pltpu.VMEM((ms, lc), BF16)] * 6
            + [
                pltpu.VMEM((24, lc), F32),
                pltpu.SemaphoreType.DMA((len(operands) + 2 * chunks + 7,)),
            ],
            flops=8 * ms * ms * lc,
        )
    um_n = shifted(field_p, -1)
    (slave,) = kernel_call(
        slave_kernel,
        [face(F32)],
        near, far, slave_weights, fixed, kinv,
        anywhere=(4,),
        scratch=[kff, pltpu.VMEM((ms, lc), BF16), pltpu.SemaphoreType.DMA((chunks,))],
        flops=10**11,
    )
    (gradient,) = kernel_call(
        last_kernel, [face(F32)], slave, um_n, tiles_s, flops=2 * 192 * ms * lc
    )
    return (field[None], gradient[None])


def solution(mesh):
    placed = (
        P(AXES, None, None),
        P(AXES, None, None),
        P(AXES, None, None),
        P(AXES, None),
        P(AXES, None),
        P(AXES, None, None),
        P(AXES, None),
        P(AXES, None),
        P(AXES, None, None),
    )
    return jax.shard_map(
        on_device,
        mesh=mesh,
        in_specs=placed,
        out_specs=(P(AXES, None, None), P(AXES, None, None)),
        check_vma=False,
    )
```

```python
import functools

import jax
import jax.numpy as jnp
import numpy as np
from jax import lax
from jax.experimental import pallas as pl
from jax.experimental.pallas import tpu as pltpu
from jax.sharding import PartitionSpec as P

STEPS = 3
AXES = ("sub", "grp")
F32, BF16 = jnp.float32, jnp.bfloat16
TILE = 128
TILE_ROWS = 192
HALO = 32
MIB = 1 << 20


def shifted(block, distance):
    size = lax.axis_size("sub")
    return lax.ppermute(block, "sub", [((i - distance) % size, i) for i in range(size)])


def swapped(block):
    size = lax.axis_size("sub")
    return lax.ppermute(block, "sub", [(i ^ 1, i) for i in range(size)])


def swapped_out(block):
    size = lax.axis_size("sub")
    other = [(i + 1 if i % 2 else i - 1) % size for i in range(size)]
    return lax.ppermute(block, "sub", [(other[i], i) for i in range(size)])


def is_odd():
    return lax.rem(lax.axis_index("sub"), 2) == 1


def rows_of(flat, count):
    width = flat.shape[1] // count
    return jnp.concatenate([flat[:, width * k : width * (k + 1)] for k in range(count)], axis=0)


def dot(left, right):
    return jnp.dot(left, right, preferred_element_type=F32)


def halves(value):
    high = value.astype(BF16).astype(F32)
    return high, (value - high).astype(BF16).astype(F32)


def column(row):
    return jnp.broadcast_to(row, (TILE, row.shape[1])).T


def mortar_times(tiles, values):
    count = values.shape[0] // TILE
    rows = TILE + 2 * HALO
    parts = [
        dot(tiles[rows * t : rows * (t + 1), :], values[TILE * t : TILE * (t + 1)])
        for t in range(count)
    ]
    out = []
    none = jnp.zeros((HALO, values.shape[1]), F32)
    for t in range(count):
        before = parts[t - 1][TILE + HALO :] if t else none
        after = parts[t + 1][TILE : TILE + HALO] if t + 1 < count else none
        gap = jnp.zeros((TILE - 2 * HALO, values.shape[1]), F32)
        out.append(parts[t][:TILE] + jnp.concatenate([before, gap, after], axis=0))
    return jnp.concatenate(out, axis=0)


def mortar_t_times(tiles_t, values):
    count = values.shape[0] // TILE
    none = jnp.zeros((HALO, values.shape[1]), BF16)
    fill = jnp.zeros((TILE - 2 * HALO, values.shape[1]), BF16)
    out = []
    for t in range(count):
        low, high = TILE * t, TILE * (t + 1)
        before = values[low - HALO : low] if t else none
        after = values[high : high + HALO] if t + 1 < count else none
        window = jnp.concatenate([values[low:high], before, after, fill], axis=0)
        out.append(dot(tiles_t[TILE * t : TILE * (t + 1), :], window))
    return jnp.concatenate(out, axis=0)


def unpacked(pack, t):
    edge = pack[160 * t : 160 * t + HALO, :].astype(F32)
    lane = lax.broadcasted_iota(jnp.int32, edge.shape, 1)
    above = jnp.where(lane < TILE // 2, edge, 0.0)
    below = jnp.where(lane < TILE // 2, 0.0, edge)
    middle = pack[160 * t + HALO : 160 * (t + 1), :].astype(F32)
    return jnp.concatenate([middle, above, below], axis=0)


def with_fill(tile):
    return jnp.concatenate([tile, jnp.zeros((TILE - 2 * HALO, TILE), F32)], axis=0)


class Moves:
    def __init__(self, sems):
        self.sems, self.used = sems, 0

    def start(self, source, target):
        copy = pltpu.make_async_copy(source, target, self.sems.at[self.used])
        self.used += 1
        copy.start()
        return copy


CHUNK = 256
SIDE = 32


def start_faces(moves, kinv, held, ms, first=0, end=None):
    copies = []
    for r in range(first, 2 * ms // CHUNK if end is None else end):
        row = r * CHUNK + (ms if r * CHUNK >= ms else 0)
        pair = []
        for to, at in ((0, 0), (ms, 2 * ms)):
            pair.append(
                moves.start(
                    kinv.at[pl.ds(row, CHUNK), pl.ds(at, ms)],
                    held.at[pl.ds(r * CHUNK, CHUNK), pl.ds(to, ms)],
                )
            )
        copies.append(pair)
    return copies


def solved(copies, held, load, fixed, zt, um, us, ms, start=0):
    for r, pair in enumerate(copies, start):
        for copy in pair:
            copy.wait()
        row = r * CHUNK
        u = (dot(held[row : row + CHUNK, :], load) + fixed[row : row + CHUNK, :]).astype(BF16)
        if row < ms:
            um[row : row + CHUNK, :] = u
        else:
            us[row - ms : row - ms + CHUNK, :] = u
    if zt is None:
        return None
    both = dot(zt[:, :ms], um[...]) + dot(zt[:, ms:], us[...])
    return both[:24] + both[24:]


def loads_of(push, scaled, loads_m, loads_s):
    master = (-push.astype(F32) - loads_m.astype(F32)).astype(BF16)
    slave = (scaled - loads_s.astype(F32)).astype(BF16)
    return jnp.concatenate([master, slave], axis=0)


def pack_kernel(mortar, seg, field, modes, coarse, weights, cand, out, behind):
    ms = mortar.shape[0]
    nr = coarse.shape[0]
    rigid = rows_of(modes, nr)
    count = ms // TILE
    ids = seg[...].astype(F32)
    ids_col = column(ids)
    none = jnp.zeros((HALO, TILE), F32)

    def masked(low, high, t):
        own = slice(TILE * t, TILE * (t + 1))
        same = ids_col[low:high] == ids[:, own]
        return jnp.where(same, mortar[low:high, own].astype(F32), 0.0)

    tiles = []
    for t in range(count):
        low, high = TILE * t, TILE * (t + 1)
        middle = masked(low, high, t)
        above = masked(low - HALO, low, t) if t else none
        below = masked(high, high + HALO, t) if t + 1 < count else none
        out[160 * t : 160 * t + HALO, :] = (above + below).astype(BF16)
        out[160 * t + HALO : 160 * (t + 1), :] = middle.astype(BF16)
        tile = jnp.concatenate([middle, above, below], axis=0)
        tiles.append(with_fill(tile).T.astype(BF16))
    push = mortar_t_times(jnp.concatenate(tiles, axis=0), field[...].astype(BF16))
    out[160 * count : 160 * count + ms, :] = push.astype(BF16)

    behind[...] = jnp.zeros_like(behind)
    behind[0:nr, :] = rigid[:, :ms]
    behind[8 : 8 + nr, :] = coarse[...]
    for t in range(count):
        own = slice(TILE * t, TILE * (t + 1))
        chosen = jnp.zeros((1, TILE), F32)
        if TILE * (t + 1) <= cand.shape[1]:
            chosen = cand[:, own].astype(F32)
        lanes = slice(ms + TILE * t, ms + TILE * (t + 1))
        pad = jnp.zeros((8 - nr, TILE), F32)
        rows = [rigid[:, lanes], pad, coarse[:, own], pad, weights[:, own], chosen]
        value = jnp.concatenate(rows + [jnp.zeros((SIDE - 18, TILE), F32)], axis=0)
        high, low = halves(value)
        base = 160 * count + ms + 2 * SIDE * t
        out[base : base + SIDE, :] = high.astype(BF16)
        out[base + SIDE : base + 2 * SIDE, :] = low.astype(BF16)


def side_rows(pack_p, ms):
    count = ms // TILE
    out = []
    for t in range(count):
        base = 160 * count + ms + 2 * SIDE * t
        high = pack_p[base : base + SIDE, :].astype(F32)
        out.append(high + pack_p[base + SIDE : base + 2 * SIDE, :].astype(F32))
    return jnp.concatenate(out, axis=1)


def fixed_kernel(loads, kinv, out, held, sems):
    ms = loads.shape[0] // 3
    moves = Moves(sems)
    copies = []
    for r in range(2 * ms // CHUNK):
        row = r * CHUNK + (ms if r * CHUNK >= ms else 0)
        copies.append(
            moves.start(
                kinv.at[pl.ds(row, CHUNK), pl.ds(ms, ms)], held.at[pl.ds(r * CHUNK, CHUNK), :]
            )
        )
    for r, copy in enumerate(copies):
        copy.wait()
        out[r * CHUNK : (r + 1) * CHUNK, :] = -dot(
            held[r * CHUNK : (r + 1) * CHUNK, :], loads[ms : 2 * ms, :]
        )


def setup_kernel(*refs):
    names, results = 8, 11
    kinv = refs[names]
    far_outs = refs[names + 1 : names + 1 + results]
    rest = refs[names + 1 + results :]
    local, rest = rest[:names], rest[names:]
    outs, rest = rest[:results], rest[results:]
    held, rows, modes, modes_p, um, us, long, sems = rest
    pack_p, weights, rigid_row, side_n, pack, field, loads, fixed = local
    tiles_s, tiles_p, tiles_pt, side_p, zt, md, md_p, near, far, resid, klt = outs
    ms = weights.shape[1]
    nr = rigid_row.shape[1] // (2 * ms)
    odd = is_odd()
    count = ms // TILE
    span = TILE + 2 * HALO
    moves = Moves(sems)
    arrive = [moves.start(a, b) for a, b in zip(refs[:names], local)]
    copies = start_faces(moves, kinv, held, ms)
    leaving = []

    def wait(*which):
        for n in which:
            arrive[n].wait()

    def leave(*which):
        for n in which:
            leaving.append(moves.start(outs[n], far_outs[n]))

    wait(0)
    for t in range(count):
        tile = unpacked(pack_p, t)
        tiles_p[span * t : span * (t + 1), :] = tile.astype(BF16)
        tiles_pt[TILE * t : TILE * (t + 1), :] = with_fill(tile).T.astype(BF16)
    side_p[...] = side_rows(pack_p, ms)
    leave(1, 2, 3)

    wait(1, 2, 3, 4)
    rigid = rows_of(rigid_row, nr)
    for t in range(count):
        tiles_s[span * t : span * (t + 1), :] = unpacked(pack, t).astype(BF16)
    leave(0)

    def through(tiles, values):
        rows[...] = jnp.zeros_like(rows)
        high, low = halves(values)
        rows[0:nr, :] = high
        rows[8 : 8 + nr, :] = low
        moved = mortar_times(tiles, rows[...].T.astype(BF16)).T
        return moved[0:nr] + moved[8 : 8 + nr]

    modes[...] = jnp.zeros_like(modes)
    modes_p[...] = jnp.zeros_like(modes_p)
    modes[nr : 2 * nr, :] = rigid[:, ms:] * weights[...]
    modes[2 * nr : 3 * nr, :] = -through(tiles_s, side_n[0:nr, :])
    modes_p[0:nr, :] = side_p[0:nr, :] * side_p[16:17, :]
    modes_p[nr : 2 * nr, :] = -through(tiles_p, rigid[:, :ms])

    def placed(values):
        later = jnp.concatenate([values[18:24], values[0:18]], axis=0)
        return jnp.where(odd, later, values)

    def stacked(values):
        high, low = halves(values)
        rows[...] = jnp.zeros_like(rows)
        rows[0:24, :] = high
        rows[32:56, :] = low
        rows[64:88, :] = high
        return rows[...].T.astype(BF16)

    own = placed(modes[...])
    md[...] = stacked(own)
    columns = stacked(placed(modes_p[...]))
    md_p[...] = columns
    leave(5, 6)
    pushed = mortar_t_times(tiles_pt, columns).T
    high, low = halves(-(pushed[0:24] + pushed[32:56]))
    zt[0:24, :ms] = high.astype(BF16)
    zt[24:48, :ms] = low.astype(BF16)
    high, low = halves(own * weights[...])
    zt[0:24, ms:] = high.astype(BF16)
    zt[24:48, ms:] = low.astype(BF16)
    leave(4)
    push = pack_p[160 * count : 160 * count + ms, :]
    wait(5, 6, 7)
    scaled = column(weights[...]) * field[...]
    load = loads_of(push, scaled, loads[:ms, :], loads[2 * ms :, :])
    long[...] = jnp.zeros_like(long)
    long[0:24, :] = zt[0:24, :].astype(F32)
    long[32:56, :] = zt[24:48, :].astype(F32)
    values = jnp.concatenate([load, long[...].T.astype(BF16)], axis=1)
    for r, pair in enumerate(copies):
        for copy in pair:
            copy.wait()
        row = r * CHUNK
        part = dot(held[row : row + CHUNK, :], values)
        u = (part[:, :TILE] + fixed[row : row + CHUNK, :]).astype(BF16)
        if row < ms:
            um[row : row + CHUNK, :] = u
        else:
            us[row - ms : row - ms + CHUNK, :] = u
        long[:, row : row + CHUNK] = part[:, TILE:].T
    both = dot(zt[:, :ms], um[...]) + dot(zt[:, ms:], us[...])
    resid[...] = both[:24] + both[24:]
    near[...] = jnp.where(odd, um[...], us[...])
    far[...] = jnp.where(odd, us[...], um[...])
    leave(9, 8, 7)
    high, low = halves(long[0:24, :] + long[32:56, :])
    klt[0:24, :] = high.astype(BF16)
    klt[24:48, :] = low.astype(BF16)
    leave(10)
    for copy in leaving:
        copy.wait()


def coarse_rows(coarse, side_p, side_n, source, cand, out, floors, rows):
    nr, width = coarse.shape
    rows[...] = jnp.zeros_like(rows)
    rows[0:nr, :] = side_p[8 : 8 + nr, :]
    rows[nr : 2 * nr, :] = coarse[...]
    rows[2 * nr : 3 * nr, :] = side_n[8 : 8 + nr, :]
    later = jnp.concatenate([rows[18:24, :], rows[0:18, :]], axis=0)
    high, low = halves(jnp.where(is_odd(), later, rows[...]))
    both = jnp.concatenate([high, low], axis=0).astype(BF16)
    count = width // TILE
    for n in range(out.shape[1] // CHUNK):
        near_by = [(n + k) % count for k in (-1, 0, 1)]
        left = jnp.concatenate([both[:, TILE * t : TILE * (t + 1)] for t in near_by], axis=1)
        wanted = source[:, n * CHUNK : (n + 1) * CHUNK]
        picks = []
        for t in near_by:
            index = lax.broadcasted_iota(jnp.int32, (TILE, CHUNK), 0) + TILE * t
            picks.append(jnp.where(index == wanted, 1.0, 0.0).astype(BF16))
        out[:, n * CHUNK : (n + 1) * CHUNK] = dot(left, jnp.concatenate(picks, axis=0)).astype(
            BF16
        )

    floors[...] = jnp.zeros_like(floors)
    chosen = (cand[...].astype(F32), side_p[17:18, : cand.shape[1]])
    for t in range(floors.shape[1] // TILE):
        place = lax.broadcasted_iota(jnp.int32, (TILE, cand.shape[1]), 0) + TILE * t
        for n, which in enumerate(chosen):
            hit = jnp.where(place.astype(F32) == which, 1.0, 0.0)
            found = jnp.broadcast_to(jnp.max(hit, axis=1, keepdims=True), (TILE, TILE)).T
            floors[n : n + 1, TILE * t : TILE * (t + 1)] = jnp.where(
                found[0:1] > 0.0, 0.0, -jnp.inf
            )


def pair_kernel(resid, other, out):
    pair = (resid[...] + other[...]).astype(BF16)
    out[...] = jnp.broadcast_to(pair[None], out.shape)


def last_kernel(slave, um_n, tiles_s, grad):
    grad[...] = slave[...] - mortar_times(tiles_s, um_n[...])


def dot_rows(left, right):
    return lax.dot_general(left, right, (((1,), (1,)), ((), ())), preferred_element_type=F32)


def forms_kernel(
    zt, md, klt, coarse, side_p, side_n, source, cand, near,
    mrows, forms, coarse_of, floors,
    square, rows,
):
    del near
    ms = md.shape[0]
    coarse_rows(coarse, side_p, side_n, source, cand, coarse_of, floors, rows)
    mrows[...] = md[...].astype(F32).T[0:64].astype(BF16)

    def form(at, product):
        square[...] = jnp.zeros_like(square)
        square[0:24, 0:64] = product[0:24] + product[32:56]
        turned = square[...].T
        high, low = halves(turned[0:24] + turned[32:56])
        square[...] = jnp.zeros_like(square)
        square[0:24, :] = high
        square[32:56, :] = low
        square[64:88, :] = high
        forms[at : at + 24, :] = square[...].T[0:24].astype(BF16)

    gap = jnp.zeros((8, 2 * ms), BF16)
    left = jnp.concatenate([zt[0:24, :], gap, zt[24:48, :], gap], axis=0)
    right = jnp.concatenate([klt[0:24, :], gap, klt[24:48, :], gap], axis=0)
    form(0, dot_rows(mrows[...], mrows[...]))
    form(24, dot_rows(left, right))


def gradient_kernel(*refs):
    names = 12
    kinv, _, g_out, gp_out, stats = refs[names : names + 5]
    held = refs[names + 5]
    local = refs[names + 6 : 2 * names + 6]
    g, gp, solution, sems = refs[2 * names + 6 :]
    ms = g.shape[0]
    moves = Moves(sems)
    arrive = [moves.start(a, b) for a, b in zip(refs[:9], local[:9])]
    copies = start_faces(moves, kinv, held, ms)
    arrive += [moves.start(a, b) for a, b in zip(refs[9:names], local[9:])]
    weights, side_p, near, far, near_r, far_r, tiles_p, tiles_pt, tiles_s, mrows, zt, klt = local

    def wait(*which):
        for n in which:
            arrive[n].wait()

    wait(0, 1, 2, 3, 4, 5, 6)
    odd = is_odd()
    um, us = jnp.where(odd, near[...], far[...]), jnp.where(odd, far[...], near[...])
    um_n = jnp.where(odd, far_r[...], near_r[...])
    us_p = jnp.where(odd, near_r[...], far_r[...])
    wcol = column(weights[...])
    gp[...] = column(side_p[16:17, :]) * us_p.astype(F32) - mortar_times(tiles_p, um)
    out_p = moves.start(gp, gp_out)
    wait(7)
    master = (-mortar_t_times(tiles_pt, gp[...].astype(BF16))).astype(BF16)
    wait(8)
    g[...] = wcol * us.astype(F32) - mortar_times(tiles_s, um_n)
    out_s = moves.start(g, g_out)
    load = jnp.concatenate([master, (wcol * g[...]).astype(BF16)], axis=0)
    curve = jnp.zeros((CHUNK, TILE), F32)
    for r, pair in enumerate(copies):
        for copy in pair:
            copy.wait()
        row = r * CHUNK
        part = dot(held[row : row + CHUNK, :], load)
        solution[row : row + CHUNK, :] = part
        curve += load[row : row + CHUNK].astype(F32) * part
    wait(9, 10, 11)
    stats[...] = jnp.zeros_like(stats)
    stats[0:1, :] = jnp.sum(g[...] * g[...], axis=0, keepdims=True)
    stats[1:2, :] = jnp.sum(curve, axis=0, keepdims=True)
    high, low = halves(g[...])
    first = dot(mrows[...], high.astype(BF16))
    second = dot(mrows[0:32, :], low.astype(BF16))
    stats[8:32, :] = first[0:24] + first[32:56] + second[0:24]
    high, low = halves(solution[...])
    first = dot(zt[...], high.astype(BF16)) + dot(klt[...], load)
    second = dot(zt[0:32, :], low.astype(BF16))
    stats[32:56, :] = first[0:24] + first[24:48] + second[0:24]
    out_p.wait()
    out_s.wait()


def project_kernel(every, coarse, forms, stats, stack, sums):
    both = dot(coarse[...], every[...].reshape(coarse.shape[1], TILE))
    c = both[:24] + both[24:]
    high, low = halves(c)
    gap = jnp.zeros((8, TILE), F32)
    rest = jnp.zeros((TILE - 88, TILE), F32)
    operand = jnp.concatenate([high, gap, high, gap, low, rest], axis=0).astype(BF16)
    stack[...] = operand
    moved = dot(forms[...], operand)
    norm = stats[0:1, :] + jnp.sum(
        c * (moved[0:24] - 2.0 * stats[8:32, :]), axis=0, keepdims=True
    )
    curve = stats[1:2, :] + jnp.sum(c * (moved[24:48] - stats[32:56, :]), axis=0, keepdims=True)
    total = jnp.concatenate([norm, curve], axis=0)
    sums[...] = jnp.broadcast_to(total[None], sums.shape)


def direction_kernel(stack, g, gp, md, md_p, d, dp):
    d[...] = g[...] - dot(md[...], stack[...])
    dp[...] = gp[...] - dot(md_p[...], stack[...])


def marker_kernel(near, out):
    del near
    out[...] = jnp.zeros_like(out)


def step_kernel(final, *refs):
    names = 10
    loads, kinv = refs[names : names + 2]
    y_out, yp_out, near_out, far_out, resid_out = refs[names + 2 : names + 7]
    held = refs[names + 7]
    local = refs[names + 8 : 2 * names + 8]
    loads_m, loads_s, um, us, near, far, resid, sems = refs[2 * names + 8 :]
    weights, floors, sums, field_p, dp, tiles_pt, field, d, zt, fixed = local[:10]
    ms = d.shape[0]
    moves = Moves(sems)
    arrive = [moves.start(refs[n], local[n]) for n in range(8)]
    arrive_m = moves.start(loads.at[pl.ds(0, ms), :], loads_m)
    arrive_s = moves.start(loads.at[pl.ds(2 * ms, ms), :], loads_s)
    arrive += [moves.start(refs[n], local[n]) for n in range(8, 10)]
    copies = start_faces(moves, kinv, held, ms, 0, ms // CHUNK if final else None)

    def wait(*which):
        for n in which:
            arrive[n].wait()

    wait(0, 1)
    wcol = column(weights[...])
    floor, floor_p = column(floors[0:1, :]), column(floors[1:2, :])
    wait(2)
    total = jnp.sum(sums[...], axis=0)
    step = total[0:1] / total[1:2]
    wait(3, 4)
    field_p[...] = jnp.maximum(field_p[...] - step * dp[...], floor_p)
    out_p = None if final else moves.start(field_p, yp_out)
    wait(5)
    push = mortar_t_times(tiles_pt, field_p[...].astype(BF16)).astype(BF16)
    wait(6, 7)
    field[...] = jnp.maximum(field[...] - step * d[...], floor)
    out_s = moves.start(field, y_out)
    arrive_m.wait()
    arrive_s.wait()
    load = loads_of(push, wcol * field[...], loads_m[...], loads_s[...])
    wait(8, 9)
    if final:
        near[...] = load[:ms]
        far[...] = load[ms:]
        outs = [moves.start(near, near_out), moves.start(far, far_out)]
        solved(copies, held, load, fixed, None, um, us, ms)
        outs += [out_s, moves.start(um, yp_out)]
    else:
        resid[...] = solved(copies, held, load, fixed, zt, um, us, ms)
        odd = is_odd()
        near[...] = jnp.where(odd, um[...], us[...])
        far[...] = jnp.where(odd, us[...], um[...])
        outs = [moves.start(far, far_out), moves.start(near, near_out)]
        outs += [out_p, out_s, moves.start(resid, resid_out)]
    for copy in outs:
        copy.wait()


def slave_kernel(load_m, load_s, weights, fixed, kinv, out, held, us, sems):
    ms = weights.shape[1]
    copies = start_faces(Moves(sems), kinv, held, ms, ms // CHUNK)
    load = jnp.concatenate([load_m[...], load_s[...]], axis=0)
    solved(copies, held, load, fixed, None, None, us, ms, ms // CHUNK)
    out[...] = column(weights[...]) * us[...].astype(F32)


def shape(dims, dtype):
    return jax.ShapeDtypeStruct(dims, dtype)


def kernel_call(body, outs, *operands, anywhere=(), anywhere_out=(), scratch=(), flops=0):
    here = pl.BlockSpec(memory_space=pltpu.VMEM)
    far = pl.BlockSpec(memory_space=pl.ANY)
    moved = sum(int(np.prod(o.shape)) * o.dtype.itemsize for o in list(operands) + list(outs))
    return pl.pallas_call(
        body,
        out_shape=tuple(outs),
        in_specs=[far if n in anywhere else here for n in range(len(operands))],
        out_specs=tuple(far if n in anywhere_out else here for n in range(len(outs))),
        scratch_shapes=list(scratch),
        compiler_params=pltpu.CompilerParams(vmem_limit_bytes=64 * MIB),
        cost_estimate=pl.CostEstimate(flops=flops, bytes_accessed=moved, transcendentals=0),
    )(*operands)


def on_device(
    inverse_blocks,
    primal_loads,
    mortar_values,
    segment_ids,
    slave_weights,
    rigid_modes,
    coarse_inverse,
    candidates,
    start_multipliers,
):
    ms = mortar_values.shape[1]
    nr = rigid_modes.shape[1]
    nc = coarse_inverse.shape[1]
    lc = start_multipliers.shape[2]
    sub, grp = lax.axis_size("sub"), lax.axis_size("grp")
    chips = sub * grp // 2
    kinv = inverse_blocks[0]
    loads = primal_loads[0]
    rigid = rigid_modes.reshape(1, -1)
    field = start_multipliers[0]
    count = ms // TILE
    face = lambda dtype: shape((ms, lc), dtype)
    kff = pltpu.VMEM((2 * ms, 2 * ms), BF16)
    chunks = 2 * ms // CHUNK

    pack, behind = kernel_call(
        pack_kernel,
        [shape(((160 + 2 * SIDE) * count + ms, lc), BF16), shape((16, ms), F32)],
        mortar_values[0],
        segment_ids,
        field,
        rigid,
        coarse_inverse,
        slave_weights,
        candidates,
    )
    pack_p = shifted(pack, 1)
    side_n = shifted(behind, -1)
    field_p = shifted(field, 1)
    (fixed,) = kernel_call(
        fixed_kernel,
        [shape((2 * ms, lc), F32)],
        loads,
        kinv,
        anywhere=(1,),
        scratch=[pltpu.VMEM((2 * ms, ms), BF16), pltpu.SemaphoreType.DMA((chunks,))],
        flops=4 * ms * ms * lc,
    )
    outs = [
        shape((TILE_ROWS * count, TILE), BF16),
        shape((TILE_ROWS * count, TILE), BF16),
        shape((ms, 2 * TILE), BF16),
        shape((SIDE, ms), F32),
        shape((48, 2 * ms), BF16),
        face(BF16),
        face(BF16),
        face(BF16),
        face(BF16),
        shape((24, lc), F32),
        shape((48, 2 * ms), BF16),
    ]
    operands = (pack_p, slave_weights, rigid, side_n, pack, field, loads, fixed)
    (tiles_s, tiles_p, tiles_pt, side_p, zt, md, md_p, near, far, resid, klt) = kernel_call(
        setup_kernel,
        outs,
        *operands,
        kinv,
        anywhere=range(len(operands) + 1),
        anywhere_out=range(len(outs)),
        scratch=[pltpu.VMEM(o.shape, o.dtype) for o in operands]
        + [pltpu.VMEM(o.shape, o.dtype) for o in outs]
        + [
            kff,
            pltpu.VMEM((TILE, ms), F32),
            pltpu.VMEM((24, ms), F32),
            pltpu.VMEM((24, ms), F32),
            pltpu.VMEM((ms, lc), BF16),
            pltpu.VMEM((ms, lc), BF16),
            pltpu.VMEM((TILE, 2 * ms), F32),
            pltpu.SemaphoreType.DMA((len(operands) + len(outs) + 2 * chunks,)),
        ],
        flops=8 * ms * ms * lc,
    )

    chip, group, spot, mode = np.meshgrid(
        np.arange(sub // 2), np.arange(grp), np.arange(4), np.arange(nr), indexing="ij"
    )
    source = (((2 * chip + spot - 1) % sub) * grp + group) * nr + mode
    source = jnp.asarray(source.reshape(1, -1), jnp.int32)
    mrows, forms, coarse, floors = kernel_call(
        forms_kernel,
        [
            shape((64, ms), BF16),
            shape((48, TILE), BF16),
            shape((48, source.shape[1]), BF16),
            shape((8, ms), F32),
        ],
        zt,
        md,
        klt,
        coarse_inverse,
        side_p,
        side_n,
        source,
        candidates,
        near,
        anywhere=(8,),
        scratch=[pltpu.VMEM((TILE, TILE), F32), pltpu.VMEM((24, nc), F32)],
        flops=10**11,
    )

    same_core = [
        [(2 * m + core) * grp + z for m in range(sub // 2) for z in range(grp)]
        for core in range(2)
    ]
    for turn in range(STEPS):
        (pieces,) = kernel_call(
            pair_kernel, [shape((chips, 24, lc), BF16)], resid, swapped(resid)
        )
        every = lax.all_to_all(
            pieces, AXES, 0, 0, tiled=True, axis_index_groups=same_core
        )
        far_r = swapped_out(far)
        near_r = swapped(near)
        (marker,) = kernel_call(
            marker_kernel, [shape((8, TILE), F32)], near, anywhere=(0,), flops=10**12
        )
        operands = (
            slave_weights, side_p, near, far, near_r, far_r, tiles_p, tiles_pt, tiles_s,
            mrows, zt, klt,
        )
        g, g_p, stats = kernel_call(
            gradient_kernel,
            [face(F32), face(F32), shape((64, lc), F32)],
            *operands,
            kinv,
            marker,
            anywhere=range(len(operands) + 2),
            anywhere_out=(0, 1),
            scratch=[kff]
            + [pltpu.VMEM(o.shape, o.dtype) for o in operands]
            + [
                pltpu.VMEM((ms, lc), F32),
                pltpu.VMEM((ms, lc), F32),
                pltpu.VMEM((2 * ms, lc), F32),
                pltpu.SemaphoreType.DMA((len(operands) + 2 * chunks + 2,)),
            ],
            flops=8 * ms * ms * lc,
        )
        stack, sums = kernel_call(
            project_kernel,
            [shape((TILE, lc), BF16), shape((2 * chips, 2, lc), F32)],
            every, coarse, forms, stats,
            flops=2 * 48 * every.shape[0] * every.shape[1] * lc,
        )
        d, d_p = kernel_call(
            direction_kernel,
            [face(F32), face(F32)],
            stack, g, g_p, md, md_p,
            flops=4 * ms * TILE * lc,
        )
        totals = lax.all_to_all(sums, AXES, 0, 0, tiled=True)
        operands = (
            slave_weights, floors, totals, field_p, d_p, tiles_pt, field, d, zt, fixed,
        )
        final = turn == STEPS - 1
        field, field_p, near, far, resid = kernel_call(
            functools.partial(step_kernel, final),
            [
                face(F32),
                face(BF16 if final else F32),
                face(BF16),
                face(BF16),
                shape((24, lc), F32),
            ],
            *operands,
            loads,
            kinv,
            anywhere=range(len(operands) + 2),
            anywhere_out=(0, 1, 2, 3, 4),
            scratch=[kff]
            + [pltpu.VMEM(o.shape, o.dtype) for o in operands]
            + [pltpu.VMEM((ms, lc), BF16)] * 6
            + [
                pltpu.VMEM((24, lc), F32),
                pltpu.SemaphoreType.DMA((len(operands) + 2 * chunks + 7,)),
            ],
            flops=8 * ms * ms * lc,
        )
    um_n = shifted(field_p, -1)
    (slave,) = kernel_call(
        slave_kernel,
        [face(F32)],
        near, far, slave_weights, fixed, kinv,
        anywhere=(4,),
        scratch=[kff, pltpu.VMEM((ms, lc), BF16), pltpu.SemaphoreType.DMA((chunks,))],
        flops=10**11,
    )
    (gradient,) = kernel_call(
        last_kernel, [face(F32)], slave, um_n, tiles_s, flops=2 * 192 * ms * lc
    )
    return (field[None], gradient[None])


def solution(mesh):
    placed = (
        P(AXES, None, None),
        P(AXES, None, None),
        P(AXES, None, None),
        P(AXES, None),
        P(AXES, None),
        P(AXES, None, None),
        P(AXES, None),
        P(AXES, None),
        P(AXES, None, None),
    )
    return jax.shard_map(
        on_device,
        mesh=mesh,
        in_specs=placed,
        out_specs=(P(AXES, None, None), P(AXES, None, None)),
        check_vma=False,
    )
```

```python
import functools

import jax
import jax.numpy as jnp
import numpy as np
from jax import lax
from jax.experimental import pallas as pl
from jax.experimental.pallas import tpu as pltpu
from jax.sharding import PartitionSpec as P

STEPS = 3
AXES = ("sub", "grp")
F32, BF16 = jnp.float32, jnp.bfloat16
TILE = 128
TILE_ROWS = 192
HALO = 32
MIB = 1 << 20


def shifted(block, distance):
    size = lax.axis_size("sub")
    return lax.ppermute(block, "sub", [((i - distance) % size, i) for i in range(size)])


def swapped(block):
    size = lax.axis_size("sub")
    return lax.ppermute(block, "sub", [(i ^ 1, i) for i in range(size)])


def swapped_out(block):
    size = lax.axis_size("sub")
    other = [(i + 1 if i % 2 else i - 1) % size for i in range(size)]
    return lax.ppermute(block, "sub", [(other[i], i) for i in range(size)])


def is_odd():
    return lax.rem(lax.axis_index("sub"), 2) == 1


def rows_of(flat, count):
    width = flat.shape[1] // count
    return jnp.concatenate([flat[:, width * k : width * (k + 1)] for k in range(count)], axis=0)


def dot(left, right):
    return jnp.dot(left, right, preferred_element_type=F32)


def halves(value):
    high = value.astype(BF16).astype(F32)
    return high, (value - high).astype(BF16).astype(F32)


def column(row):
    return jnp.broadcast_to(row, (TILE, row.shape[1])).T


def mortar_times(tiles, values):
    count = values.shape[0] // TILE
    rows = TILE + 2 * HALO
    parts = [
        dot(tiles[rows * t : rows * (t + 1), :], values[TILE * t : TILE * (t + 1)])
        for t in range(count)
    ]
    out = []
    none = jnp.zeros((HALO, values.shape[1]), F32)
    for t in range(count):
        before = parts[t - 1][TILE + HALO :] if t else none
        after = parts[t + 1][TILE : TILE + HALO] if t + 1 < count else none
        gap = jnp.zeros((TILE - 2 * HALO, values.shape[1]), F32)
        out.append(parts[t][:TILE] + jnp.concatenate([before, gap, after], axis=0))
    return jnp.concatenate(out, axis=0)


def mortar_t_times(tiles_t, values):
    count = values.shape[0] // TILE
    none = jnp.zeros((HALO, values.shape[1]), BF16)
    fill = jnp.zeros((TILE - 2 * HALO, values.shape[1]), BF16)
    out = []
    for t in range(count):
        low, high = TILE * t, TILE * (t + 1)
        before = values[low - HALO : low] if t else none
        after = values[high : high + HALO] if t + 1 < count else none
        window = jnp.concatenate([values[low:high], before, after, fill], axis=0)
        out.append(dot(tiles_t[TILE * t : TILE * (t + 1), :], window))
    return jnp.concatenate(out, axis=0)


def unpacked(pack, t):
    edge = pack[160 * t : 160 * t + HALO, :].astype(F32)
    lane = lax.broadcasted_iota(jnp.int32, edge.shape, 1)
    above = jnp.where(lane < TILE // 2, edge, 0.0)
    below = jnp.where(lane < TILE // 2, 0.0, edge)
    middle = pack[160 * t + HALO : 160 * (t + 1), :].astype(F32)
    return jnp.concatenate([middle, above, below], axis=0)


def with_fill(tile):
    return jnp.concatenate([tile, jnp.zeros((TILE - 2 * HALO, TILE), F32)], axis=0)


class Moves:
    def __init__(self, sems):
        self.sems, self.used = sems, 0

    def start(self, source, target):
        copy = pltpu.make_async_copy(source, target, self.sems.at[self.used])
        self.used += 1
        copy.start()
        return copy


CHUNK = 256
SIDE = 16


def start_faces(moves, kinv, held, ms, first=0, end=None):
    copies = []
    for r in range(first, 2 * ms // CHUNK if end is None else end):
        row = r * CHUNK + (ms if r * CHUNK >= ms else 0)
        pair = []
        for to, at in ((0, 0), (ms, 2 * ms)):
            pair.append(
                moves.start(
                    kinv.at[pl.ds(row, CHUNK), pl.ds(at, ms)],
                    held.at[pl.ds(r * CHUNK, CHUNK), pl.ds(to, ms)],
                )
            )
        copies.append(pair)
    return copies


def solved(copies, held, load, fixed, zt, um, us, ms, start=0):
    for r, pair in enumerate(copies, start):
        for copy in pair:
            copy.wait()
        row = r * CHUNK
        u = (dot(held[row : row + CHUNK, :], load) + fixed[row : row + CHUNK, :]).astype(BF16)
        if row < ms:
            um[row : row + CHUNK, :] = u
        else:
            us[row - ms : row - ms + CHUNK, :] = u
    if zt is None:
        return None
    both = dot(zt[:, :ms], um[...]) + dot(zt[:, ms:], us[...])
    return both[:24] + both[24:]


def loads_of(push, scaled, loads_m, loads_s):
    master = (-push.astype(F32) - loads_m.astype(F32)).astype(BF16)
    slave = (scaled - loads_s.astype(F32)).astype(BF16)
    return jnp.concatenate([master, slave], axis=0)


def pack_kernel(mortar, seg, field, modes, coarse, weights, cand, out, behind):
    ms = mortar.shape[0]
    nr = coarse.shape[0]
    rigid = rows_of(modes, nr)
    count = ms // TILE
    ids = seg[...].astype(F32)
    ids_col = column(ids)
    none = jnp.zeros((HALO, TILE), F32)

    def masked(low, high, t):
        own = slice(TILE * t, TILE * (t + 1))
        same = ids_col[low:high] == ids[:, own]
        return jnp.where(same, mortar[low:high, own].astype(F32), 0.0)

    tiles = []
    for t in range(count):
        low, high = TILE * t, TILE * (t + 1)
        middle = masked(low, high, t)
        above = masked(low - HALO, low, t) if t else none
        below = masked(high, high + HALO, t) if t + 1 < count else none
        out[160 * t : 160 * t + HALO, :] = (above + below).astype(BF16)
        out[160 * t + HALO : 160 * (t + 1), :] = middle.astype(BF16)
        tile = jnp.concatenate([middle, above, below], axis=0)
        tiles.append(with_fill(tile).T.astype(BF16))
    push = mortar_t_times(jnp.concatenate(tiles, axis=0), field[...].astype(BF16))
    out[160 * count : 160 * count + ms, :] = push.astype(BF16)

    behind[...] = jnp.zeros_like(behind)
    behind[0:nr, :] = rigid[:, :ms]
    behind[8 : 8 + nr, :] = coarse[...]
    for t in range(count):
        own = slice(TILE * t, TILE * (t + 1))
        chosen = jnp.zeros((1, TILE), F32)
        if TILE * (t + 1) <= cand.shape[1]:
            chosen = cand[:, own].astype(F32)
        lanes = slice(ms + TILE * t, ms + TILE * (t + 1))
        pad = jnp.zeros((8 - nr, TILE), F32)
        rows = [rigid[:, lanes], weights[:, own], chosen, coarse[:, own], pad]
        value = jnp.concatenate(rows, axis=0)
        high, low = halves(value)
        base = 160 * count + ms + 2 * SIDE * t
        out[base : base + SIDE, :] = high.astype(BF16)
        out[base + SIDE : base + 2 * SIDE, :] = low.astype(BF16)


def side_rows(pack_p, ms):
    count = ms // TILE
    out = []
    for t in range(count):
        base = 160 * count + ms + 2 * SIDE * t
        high = pack_p[base : base + SIDE, :].astype(F32)
        out.append(high + pack_p[base + SIDE : base + 2 * SIDE, :].astype(F32))
    return jnp.concatenate(out, axis=1)


def fixed_kernel(loads, kinv, out, held, sems):
    ms = loads.shape[0] // 3
    moves = Moves(sems)
    copies = []
    for r in range(2 * ms // CHUNK):
        row = r * CHUNK + (ms if r * CHUNK >= ms else 0)
        copies.append(
            moves.start(
                kinv.at[pl.ds(row, CHUNK), pl.ds(ms, ms)], held.at[pl.ds(r * CHUNK, CHUNK), :]
            )
        )
    for r, copy in enumerate(copies):
        copy.wait()
        out[r * CHUNK : (r + 1) * CHUNK, :] = -dot(
            held[r * CHUNK : (r + 1) * CHUNK, :], loads[ms : 2 * ms, :]
        )


def setup_kernel(*refs):
    names, results = 8, 11
    kinv = refs[names]
    far_outs = refs[names + 1 : names + 1 + results]
    rest = refs[names + 1 + results :]
    local, rest = rest[:names], rest[names:]
    outs, rest = rest[:results], rest[results:]
    held, rows, modes, modes_p, um, us, long, sems = rest
    pack_p, weights, rigid_row, side_n, pack, field, loads, fixed = local
    tiles_s, tiles_p, tiles_pt, side_p, zt, md, md_p, near, far, resid, klt = outs
    ms = weights.shape[1]
    nr = rigid_row.shape[1] // (2 * ms)
    odd = is_odd()
    count = ms // TILE
    span = TILE + 2 * HALO
    moves = Moves(sems)
    arrive = [moves.start(a, b) for a, b in zip(refs[:names], local)]
    copies = start_faces(moves, kinv, held, ms)
    leaving = []

    def wait(*which):
        for n in which:
            arrive[n].wait()

    def leave(*which):
        for n in which:
            leaving.append(moves.start(outs[n], far_outs[n]))

    wait(0)
    for t in range(count):
        tile = unpacked(pack_p, t)
        tiles_p[span * t : span * (t + 1), :] = tile.astype(BF16)
        tiles_pt[TILE * t : TILE * (t + 1), :] = with_fill(tile).T.astype(BF16)
    side_p[...] = side_rows(pack_p, ms)
    leave(1, 2, 3)

    wait(1, 2, 3, 4)
    rigid = rows_of(rigid_row, nr)
    for t in range(count):
        tiles_s[span * t : span * (t + 1), :] = unpacked(pack, t).astype(BF16)
    leave(0)

    def through(tiles, values):
        rows[...] = jnp.zeros_like(rows)
        high, low = halves(values)
        rows[0:nr, :] = high
        rows[8 : 8 + nr, :] = low
        moved = mortar_times(tiles, rows[...].T.astype(BF16)).T
        return moved[0:nr] + moved[8 : 8 + nr]

    modes[...] = jnp.zeros_like(modes)
    modes_p[...] = jnp.zeros_like(modes_p)
    modes[nr : 2 * nr, :] = rigid[:, ms:] * weights[...]
    modes[2 * nr : 3 * nr, :] = -through(tiles_s, side_n[0:nr, :])
    modes_p[0:nr, :] = side_p[0:nr, :] * side_p[6:7, :]
    modes_p[nr : 2 * nr, :] = -through(tiles_p, rigid[:, :ms])

    def placed(values):
        later = jnp.concatenate([values[18:24], values[0:18]], axis=0)
        return jnp.where(odd, later, values)

    def stacked(values):
        high, low = halves(values)
        rows[...] = jnp.zeros_like(rows)
        rows[0:24, :] = high
        rows[32:56, :] = low
        rows[64:88, :] = high
        return rows[...].T.astype(BF16)

    own = placed(modes[...])
    md[...] = stacked(own)
    columns = stacked(placed(modes_p[...]))
    md_p[...] = columns
    leave(5, 6)
    pushed = mortar_t_times(tiles_pt, columns).T
    high, low = halves(-(pushed[0:24] + pushed[32:56]))
    zt[0:24, :ms] = high.astype(BF16)
    zt[24:48, :ms] = low.astype(BF16)
    high, low = halves(own * weights[...])
    zt[0:24, ms:] = high.astype(BF16)
    zt[24:48, ms:] = low.astype(BF16)
    leave(4)
    push = pack_p[160 * count : 160 * count + ms, :]
    wait(5, 6, 7)
    scaled = column(weights[...]) * field[...]
    load = loads_of(push, scaled, loads[:ms, :], loads[2 * ms :, :])
    long[...] = jnp.zeros_like(long)
    long[0:24, :] = zt[0:24, :].astype(F32)
    long[32:56, :] = zt[24:48, :].astype(F32)
    values = jnp.concatenate([load, long[...].T.astype(BF16)], axis=1)
    for r, pair in enumerate(copies):
        for copy in pair:
            copy.wait()
        row = r * CHUNK
        part = dot(held[row : row + CHUNK, :], values)
        u = (part[:, :TILE] + fixed[row : row + CHUNK, :]).astype(BF16)
        if row < ms:
            um[row : row + CHUNK, :] = u
        else:
            us[row - ms : row - ms + CHUNK, :] = u
        long[:, row : row + CHUNK] = part[:, TILE:].T
    both = dot(zt[:, :ms], um[...]) + dot(zt[:, ms:], us[...])
    resid[...] = both[:24] + both[24:]
    near[...] = jnp.where(odd, um[...], us[...])
    far[...] = jnp.where(odd, us[...], um[...])
    leave(9, 8, 7)
    high, low = halves(long[0:24, :] + long[32:56, :])
    klt[0:24, :] = high.astype(BF16)
    klt[24:48, :] = low.astype(BF16)
    leave(10)
    for copy in leaving:
        copy.wait()


def coarse_rows(coarse, side_p, side_n, source, cand, out, floors, rows):
    nr, width = coarse.shape
    rows[...] = jnp.zeros_like(rows)
    rows[0:nr, :] = side_p[8 : 8 + nr, :]
    rows[nr : 2 * nr, :] = coarse[...]
    rows[2 * nr : 3 * nr, :] = side_n[8 : 8 + nr, :]
    later = jnp.concatenate([rows[18:24, :], rows[0:18, :]], axis=0)
    high, low = halves(jnp.where(is_odd(), later, rows[...]))
    both = jnp.concatenate([high, low], axis=0).astype(BF16)
    count = width // TILE
    for n in range(out.shape[1] // CHUNK):
        near_by = [(n + k) % count for k in (-1, 0, 1)]
        left = jnp.concatenate([both[:, TILE * t : TILE * (t + 1)] for t in near_by], axis=1)
        wanted = source[:, n * CHUNK : (n + 1) * CHUNK]
        picks = []
        for t in near_by:
            index = lax.broadcasted_iota(jnp.int32, (TILE, CHUNK), 0) + TILE * t
            picks.append(jnp.where(index == wanted, 1.0, 0.0).astype(BF16))
        out[:, n * CHUNK : (n + 1) * CHUNK] = dot(left, jnp.concatenate(picks, axis=0)).astype(
            BF16
        )

    floors[...] = jnp.zeros_like(floors)
    chosen = (cand[...].astype(F32), side_p[7:8, : cand.shape[1]])
    for t in range(floors.shape[1] // TILE):
        place = lax.broadcasted_iota(jnp.int32, (TILE, cand.shape[1]), 0) + TILE * t
        for n, which in enumerate(chosen):
            hit = jnp.where(place.astype(F32) == which, 1.0, 0.0)
            found = jnp.broadcast_to(jnp.max(hit, axis=1, keepdims=True), (TILE, TILE)).T
            floors[n : n + 1, TILE * t : TILE * (t + 1)] = jnp.where(
                found[0:1] > 0.0, 0.0, -jnp.inf
            )


def pair_kernel(resid, other, out):
    pair = (resid[...] + other[...]).astype(BF16)
    out[...] = jnp.broadcast_to(pair[None], out.shape)


def last_kernel(slave, um_n, tiles_s, grad):
    grad[...] = slave[...] - mortar_times(tiles_s, um_n[...])


def dot_rows(left, right):
    return lax.dot_general(left, right, (((1,), (1,)), ((), ())), preferred_element_type=F32)


def forms_kernel(
    zt, md, klt, coarse, side_p, side_n, source, cand, near,
    mrows, forms, coarse_of, floors,
    square, rows,
):
    del near
    ms = md.shape[0]
    coarse_rows(coarse, side_p, side_n, source, cand, coarse_of, floors, rows)
    mrows[...] = md[...].astype(F32).T[0:64].astype(BF16)

    def form(at, product):
        square[...] = jnp.zeros_like(square)
        square[0:24, 0:64] = product[0:24] + product[32:56]
        turned = square[...].T
        high, low = halves(turned[0:24] + turned[32:56])
        square[...] = jnp.zeros_like(square)
        square[0:24, :] = high
        square[32:56, :] = low
        square[64:88, :] = high
        forms[at : at + 24, :] = square[...].T[0:24].astype(BF16)

    gap = jnp.zeros((8, 2 * ms), BF16)
    left = jnp.concatenate([zt[0:24, :], gap, zt[24:48, :], gap], axis=0)
    right = jnp.concatenate([klt[0:24, :], gap, klt[24:48, :], gap], axis=0)
    form(0, dot_rows(mrows[...], mrows[...]))
    form(24, dot_rows(left, right))


def gradient_kernel(*refs):
    names = 12
    kinv, _, g_out, gp_out, stats = refs[names : names + 5]
    held = refs[names + 5]
    local = refs[names + 6 : 2 * names + 6]
    g, gp, solution, sems = refs[2 * names + 6 :]
    ms = g.shape[0]
    moves = Moves(sems)
    arrive = [moves.start(a, b) for a, b in zip(refs[:9], local[:9])]
    copies = start_faces(moves, kinv, held, ms)
    arrive += [moves.start(a, b) for a, b in zip(refs[9:names], local[9:])]
    weights, side_p, near, far, near_r, far_r, tiles_p, tiles_pt, tiles_s, mrows, zt, klt = local

    def wait(*which):
        for n in which:
            arrive[n].wait()

    wait(0, 1, 2, 3, 4, 5, 6)
    odd = is_odd()
    um, us = jnp.where(odd, near[...], far[...]), jnp.where(odd, far[...], near[...])
    um_n = jnp.where(odd, far_r[...], near_r[...])
    us_p = jnp.where(odd, near_r[...], far_r[...])
    wcol = column(weights[...])
    gp[...] = column(side_p[6:7, :]) * us_p.astype(F32) - mortar_times(tiles_p, um)
    out_p = moves.start(gp, gp_out)
    wait(7)
    master = (-mortar_t_times(tiles_pt, gp[...].astype(BF16))).astype(BF16)
    wait(8)
    g[...] = wcol * us.astype(F32) - mortar_times(tiles_s, um_n)
    out_s = moves.start(g, g_out)
    load = jnp.concatenate([master, (wcol * g[...]).astype(BF16)], axis=0)
    curve = jnp.zeros((CHUNK, TILE), F32)
    for r, pair in enumerate(copies):
        for copy in pair:
            copy.wait()
        row = r * CHUNK
        part = dot(held[row : row + CHUNK, :], load)
        solution[row : row + CHUNK, :] = part
        curve += load[row : row + CHUNK].astype(F32) * part
    wait(9, 10, 11)
    stats[...] = jnp.zeros_like(stats)
    stats[0:1, :] = jnp.sum(g[...] * g[...], axis=0, keepdims=True)
    stats[1:2, :] = jnp.sum(curve, axis=0, keepdims=True)
    high, low = halves(g[...])
    first = dot(mrows[...], high.astype(BF16))
    second = dot(mrows[0:32, :], low.astype(BF16))
    stats[8:32, :] = first[0:24] + first[32:56] + second[0:24]
    high, low = halves(solution[...])
    first = dot(zt[...], high.astype(BF16)) + dot(klt[...], load)
    second = dot(zt[0:32, :], low.astype(BF16))
    stats[32:56, :] = first[0:24] + first[24:48] + second[0:24]
    out_p.wait()
    out_s.wait()


def project_kernel(every, coarse, forms, stats, stack, sums):
    both = dot(coarse[...], every[...].reshape(coarse.shape[1], TILE))
    c = both[:24] + both[24:]
    high, low = halves(c)
    gap = jnp.zeros((8, TILE), F32)
    rest = jnp.zeros((TILE - 88, TILE), F32)
    operand = jnp.concatenate([high, gap, high, gap, low, rest], axis=0).astype(BF16)
    stack[...] = operand
    moved = dot(forms[...], operand)
    norm = stats[0:1, :] + jnp.sum(
        c * (moved[0:24] - 2.0 * stats[8:32, :]), axis=0, keepdims=True
    )
    curve = stats[1:2, :] + jnp.sum(c * (moved[24:48] - stats[32:56, :]), axis=0, keepdims=True)
    total = jnp.concatenate([norm, curve], axis=0)
    sums[...] = jnp.broadcast_to(total[None], sums.shape)


def direction_kernel(stack, g, gp, md, md_p, d, dp):
    d[...] = g[...] - dot(md[...], stack[...])
    dp[...] = gp[...] - dot(md_p[...], stack[...])


def marker_kernel(near, out):
    del near
    out[...] = jnp.zeros_like(out)


def step_kernel(final, *refs):
    names = 10
    loads, kinv = refs[names : names + 2]
    y_out, yp_out, near_out, far_out, resid_out = refs[names + 2 : names + 7]
    held = refs[names + 7]
    local = refs[names + 8 : 2 * names + 8]
    loads_m, loads_s, um, us, near, far, resid, sems = refs[2 * names + 8 :]
    weights, floors, sums, field_p, dp, tiles_pt, field, d, zt, fixed = local[:10]
    ms = d.shape[0]
    moves = Moves(sems)
    arrive = [moves.start(refs[n], local[n]) for n in range(8)]
    arrive_m = moves.start(loads.at[pl.ds(0, ms), :], loads_m)
    arrive_s = moves.start(loads.at[pl.ds(2 * ms, ms), :], loads_s)
    arrive += [moves.start(refs[n], local[n]) for n in range(8, 10)]
    copies = start_faces(moves, kinv, held, ms, 0, ms // CHUNK if final else None)

    def wait(*which):
        for n in which:
            arrive[n].wait()

    wait(0, 1)
    wcol = column(weights[...])
    floor, floor_p = column(floors[0:1, :]), column(floors[1:2, :])
    wait(2)
    total = jnp.sum(sums[...], axis=0)
    step = total[0:1] / total[1:2]
    wait(3, 4)
    field_p[...] = jnp.maximum(field_p[...] - step * dp[...], floor_p)
    out_p = None if final else moves.start(field_p, yp_out)
    wait(5)
    push = mortar_t_times(tiles_pt, field_p[...].astype(BF16)).astype(BF16)
    wait(6, 7)
    field[...] = jnp.maximum(field[...] - step * d[...], floor)
    out_s = moves.start(field, y_out)
    arrive_m.wait()
    arrive_s.wait()
    load = loads_of(push, wcol * field[...], loads_m[...], loads_s[...])
    wait(8, 9)
    if final:
        near[...] = load[:ms]
        far[...] = load[ms:]
        outs = [moves.start(near, near_out), moves.start(far, far_out)]
        solved(copies, held, load, fixed, None, um, us, ms)
        outs += [out_s, moves.start(um, yp_out)]
    else:
        resid[...] = solved(copies, held, load, fixed, zt, um, us, ms)
        odd = is_odd()
        near[...] = jnp.where(odd, um[...], us[...])
        far[...] = jnp.where(odd, us[...], um[...])
        outs = [moves.start(far, far_out), moves.start(near, near_out)]
        outs += [out_p, out_s, moves.start(resid, resid_out)]
    for copy in outs:
        copy.wait()


def slave_kernel(load_m, load_s, weights, fixed, kinv, out, held, us, sems):
    ms = weights.shape[1]
    copies = start_faces(Moves(sems), kinv, held, ms, ms // CHUNK)
    load = jnp.concatenate([load_m[...], load_s[...]], axis=0)
    solved(copies, held, load, fixed, None, None, us, ms, ms // CHUNK)
    out[...] = column(weights[...]) * us[...].astype(F32)


def shape(dims, dtype):
    return jax.ShapeDtypeStruct(dims, dtype)


def kernel_call(body, outs, *operands, anywhere=(), anywhere_out=(), scratch=(), flops=0):
    here = pl.BlockSpec(memory_space=pltpu.VMEM)
    far = pl.BlockSpec(memory_space=pl.ANY)
    moved = sum(int(np.prod(o.shape)) * o.dtype.itemsize for o in list(operands) + list(outs))
    return pl.pallas_call(
        body,
        out_shape=tuple(outs),
        in_specs=[far if n in anywhere else here for n in range(len(operands))],
        out_specs=tuple(far if n in anywhere_out else here for n in range(len(outs))),
        scratch_shapes=list(scratch),
        compiler_params=pltpu.CompilerParams(vmem_limit_bytes=64 * MIB),
        cost_estimate=pl.CostEstimate(flops=flops, bytes_accessed=moved, transcendentals=0),
    )(*operands)


def on_device(
    inverse_blocks,
    primal_loads,
    mortar_values,
    segment_ids,
    slave_weights,
    rigid_modes,
    coarse_inverse,
    candidates,
    start_multipliers,
):
    ms = mortar_values.shape[1]
    nr = rigid_modes.shape[1]
    nc = coarse_inverse.shape[1]
    lc = start_multipliers.shape[2]
    sub, grp = lax.axis_size("sub"), lax.axis_size("grp")
    chips = sub * grp // 2
    kinv = inverse_blocks[0]
    loads = primal_loads[0]
    rigid = rigid_modes.reshape(1, -1)
    field = start_multipliers[0]
    count = ms // TILE
    face = lambda dtype: shape((ms, lc), dtype)
    kff = pltpu.VMEM((2 * ms, 2 * ms), BF16)
    chunks = 2 * ms // CHUNK

    pack, behind = kernel_call(
        pack_kernel,
        [shape(((160 + 2 * SIDE) * count + ms, lc), BF16), shape((16, ms), F32)],
        mortar_values[0],
        segment_ids,
        field,
        rigid,
        coarse_inverse,
        slave_weights,
        candidates,
    )
    pack_p = shifted(pack, 1)
    side_n = shifted(behind, -1)
    field_p = shifted(field, 1)
    (fixed,) = kernel_call(
        fixed_kernel,
        [shape((2 * ms, lc), F32)],
        loads,
        kinv,
        anywhere=(1,),
        scratch=[pltpu.VMEM((2 * ms, ms), BF16), pltpu.SemaphoreType.DMA((chunks,))],
        flops=4 * ms * ms * lc,
    )
    outs = [
        shape((TILE_ROWS * count, TILE), BF16),
        shape((TILE_ROWS * count, TILE), BF16),
        shape((ms, 2 * TILE), BF16),
        shape((SIDE, ms), F32),
        shape((48, 2 * ms), BF16),
        face(BF16),
        face(BF16),
        face(BF16),
        face(BF16),
        shape((24, lc), F32),
        shape((48, 2 * ms), BF16),
    ]
    operands = (pack_p, slave_weights, rigid, side_n, pack, field, loads, fixed)
    (tiles_s, tiles_p, tiles_pt, side_p, zt, md, md_p, near, far, resid, klt) = kernel_call(
        setup_kernel,
        outs,
        *operands,
        kinv,
        anywhere=range(len(operands) + 1),
        anywhere_out=range(len(outs)),
        scratch=[pltpu.VMEM(o.shape, o.dtype) for o in operands]
        + [pltpu.VMEM(o.shape, o.dtype) for o in outs]
        + [
            kff,
            pltpu.VMEM((TILE, ms), F32),
            pltpu.VMEM((24, ms), F32),
            pltpu.VMEM((24, ms), F32),
            pltpu.VMEM((ms, lc), BF16),
            pltpu.VMEM((ms, lc), BF16),
            pltpu.VMEM((TILE, 2 * ms), F32),
            pltpu.SemaphoreType.DMA((len(operands) + len(outs) + 2 * chunks,)),
        ],
        flops=8 * ms * ms * lc,
    )

    chip, group, spot, mode = np.meshgrid(
        np.arange(sub // 2), np.arange(grp), np.arange(4), np.arange(nr), indexing="ij"
    )
    source = (((2 * chip + spot - 1) % sub) * grp + group) * nr + mode
    source = jnp.asarray(source.reshape(1, -1), jnp.int32)
    mrows, forms, coarse, floors = kernel_call(
        forms_kernel,
        [
            shape((64, ms), BF16),
            shape((48, TILE), BF16),
            shape((48, source.shape[1]), BF16),
            shape((8, ms), F32),
        ],
        zt,
        md,
        klt,
        coarse_inverse,
        side_p,
        side_n,
        source,
        candidates,
        near,
        anywhere=(8,),
        scratch=[pltpu.VMEM((TILE, TILE), F32), pltpu.VMEM((24, nc), F32)],
        flops=10**11,
    )

    same_core = [
        [(2 * m + core) * grp + z for m in range(sub // 2) for z in range(grp)]
        for core in range(2)
    ]
    for turn in range(STEPS):
        (pieces,) = kernel_call(
            pair_kernel, [shape((chips, 24, lc), BF16)], resid, swapped(resid)
        )
        every = lax.all_to_all(
            pieces, AXES, 0, 0, tiled=True, axis_index_groups=same_core
        )
        far_r = swapped_out(far)
        near_r = swapped(near)
        (marker,) = kernel_call(
            marker_kernel, [shape((8, TILE), F32)], near, anywhere=(0,), flops=10**12
        )
        operands = (
            slave_weights, side_p, near, far, near_r, far_r, tiles_p, tiles_pt, tiles_s,
            mrows, zt, klt,
        )
        g, g_p, stats = kernel_call(
            gradient_kernel,
            [face(F32), face(F32), shape((64, lc), F32)],
            *operands,
            kinv,
            marker,
            anywhere=range(len(operands) + 2),
            anywhere_out=(0, 1),
            scratch=[kff]
            + [pltpu.VMEM(o.shape, o.dtype) for o in operands]
            + [
                pltpu.VMEM((ms, lc), F32),
                pltpu.VMEM((ms, lc), F32),
                pltpu.VMEM((2 * ms, lc), F32),
                pltpu.SemaphoreType.DMA((len(operands) + 2 * chunks + 2,)),
            ],
            flops=8 * ms * ms * lc,
        )
        stack, sums = kernel_call(
            project_kernel,
            [shape((TILE, lc), BF16), shape((2 * chips, 2, lc), F32)],
            every, coarse, forms, stats,
            flops=2 * 48 * every.shape[0] * every.shape[1] * lc,
        )
        d, d_p = kernel_call(
            direction_kernel,
            [face(F32), face(F32)],
            stack, g, g_p, md, md_p,
            flops=4 * ms * TILE * lc,
        )
        totals = lax.all_to_all(sums, AXES, 0, 0, tiled=True)
        operands = (
            slave_weights, floors, totals, field_p, d_p, tiles_pt, field, d, zt, fixed,
        )
        final = turn == STEPS - 1
        field, field_p, near, far, resid = kernel_call(
            functools.partial(step_kernel, final),
            [
                face(F32),
                face(BF16 if final else F32),
                face(BF16),
                face(BF16),
                shape((24, lc), F32),
            ],
            *operands,
            loads,
            kinv,
            anywhere=range(len(operands) + 2),
            anywhere_out=(0, 1, 2, 3, 4),
            scratch=[kff]
            + [pltpu.VMEM(o.shape, o.dtype) for o in operands]
            + [pltpu.VMEM((ms, lc), BF16)] * 6
            + [
                pltpu.VMEM((24, lc), F32),
                pltpu.SemaphoreType.DMA((len(operands) + 2 * chunks + 7,)),
            ],
            flops=8 * ms * ms * lc,
        )
    um_n = shifted(field_p, -1)
    (slave,) = kernel_call(
        slave_kernel,
        [face(F32)],
        near, far, slave_weights, fixed, kinv,
        anywhere=(4,),
        scratch=[kff, pltpu.VMEM((ms, lc), BF16), pltpu.SemaphoreType.DMA((chunks,))],
        flops=10**11,
    )
    (gradient,) = kernel_call(
        last_kernel, [face(F32)], slave, um_n, tiles_s, flops=2 * 192 * ms * lc
    )
    return (field[None], gradient[None])


def solution(mesh):
    placed = (
        P(AXES, None, None),
        P(AXES, None, None),
        P(AXES, None, None),
        P(AXES, None),
        P(AXES, None),
        P(AXES, None, None),
        P(AXES, None),
        P(AXES, None),
        P(AXES, None, None),
    )
    return jax.shard_map(
        on_device,
        mesh=mesh,
        in_specs=placed,
        out_specs=(P(AXES, None, None), P(AXES, None, None)),
        check_vma=False,
    )
```

```python
import functools

import jax
import jax.numpy as jnp
import numpy as np
from jax import lax
from jax.experimental import pallas as pl
from jax.experimental.pallas import tpu as pltpu
from jax.sharding import PartitionSpec as P

STEPS = 3
AXES = ("sub", "grp")
F32, BF16 = jnp.float32, jnp.bfloat16
TILE = 128
TILE_ROWS = 192
HALO = 32
MIB = 1 << 20


def shifted(block, distance):
    size = lax.axis_size("sub")
    return lax.ppermute(block, "sub", [((i - distance) % size, i) for i in range(size)])


def swapped(block):
    size = lax.axis_size("sub")
    return lax.ppermute(block, "sub", [(i ^ 1, i) for i in range(size)])


def swapped_out(block):
    size = lax.axis_size("sub")
    other = [(i + 1 if i % 2 else i - 1) % size for i in range(size)]
    return lax.ppermute(block, "sub", [(other[i], i) for i in range(size)])


def is_odd():
    return lax.rem(lax.axis_index("sub"), 2) == 1


def rows_of(flat, count):
    width = flat.shape[1] // count
    return jnp.concatenate([flat[:, width * k : width * (k + 1)] for k in range(count)], axis=0)


def dot(left, right):
    return jnp.dot(left, right, preferred_element_type=F32)


def halves(value):
    high = value.astype(BF16).astype(F32)
    return high, (value - high).astype(BF16).astype(F32)


def column(row):
    return jnp.broadcast_to(row, (TILE, row.shape[1])).T


def mortar_times(tiles, values):
    count = values.shape[0] // TILE
    rows = TILE + 2 * HALO
    parts = [
        dot(tiles[rows * t : rows * (t + 1), :], values[TILE * t : TILE * (t + 1)])
        for t in range(count)
    ]
    out = []
    none = jnp.zeros((HALO, values.shape[1]), F32)
    for t in range(count):
        before = parts[t - 1][TILE + HALO :] if t else none
        after = parts[t + 1][TILE : TILE + HALO] if t + 1 < count else none
        gap = jnp.zeros((TILE - 2 * HALO, values.shape[1]), F32)
        out.append(parts[t][:TILE] + jnp.concatenate([before, gap, after], axis=0))
    return jnp.concatenate(out, axis=0)


def mortar_t_times(tiles_t, values):
    count = values.shape[0] // TILE
    none = jnp.zeros((HALO, values.shape[1]), BF16)
    fill = jnp.zeros((TILE - 2 * HALO, values.shape[1]), BF16)
    out = []
    for t in range(count):
        low, high = TILE * t, TILE * (t + 1)
        before = values[low - HALO : low] if t else none
        after = values[high : high + HALO] if t + 1 < count else none
        window = jnp.concatenate([values[low:high], before, after, fill], axis=0)
        out.append(dot(tiles_t[TILE * t : TILE * (t + 1), :], window))
    return jnp.concatenate(out, axis=0)


def unpacked(pack, t):
    edge = pack[160 * t : 160 * t + HALO, :].astype(F32)
    lane = lax.broadcasted_iota(jnp.int32, edge.shape, 1)
    above = jnp.where(lane < TILE // 2, edge, 0.0)
    below = jnp.where(lane < TILE // 2, 0.0, edge)
    middle = pack[160 * t + HALO : 160 * (t + 1), :].astype(F32)
    return jnp.concatenate([middle, above, below], axis=0)


def with_fill(tile):
    return jnp.concatenate([tile, jnp.zeros((TILE - 2 * HALO, TILE), F32)], axis=0)


class Moves:
    def __init__(self, sems):
        self.sems, self.used = sems, 0

    def start(self, source, target):
        copy = pltpu.make_async_copy(source, target, self.sems.at[self.used])
        self.used += 1
        copy.start()
        return copy


CHUNK = 256
SIDE = 16


def start_faces(moves, kinv, held, ms, first=0, end=None):
    copies = []
    for r in range(first, 2 * ms // CHUNK if end is None else end):
        row = r * CHUNK + (ms if r * CHUNK >= ms else 0)
        pair = []
        for to, at in ((0, 0), (ms, 2 * ms)):
            pair.append(
                moves.start(
                    kinv.at[pl.ds(row, CHUNK), pl.ds(at, ms)],
                    held.at[pl.ds(r * CHUNK, CHUNK), pl.ds(to, ms)],
                )
            )
        copies.append(pair)
    return copies


def solved(copies, held, load, fixed, zt, um, us, ms, start=0):
    for r, pair in enumerate(copies, start):
        for copy in pair:
            copy.wait()
        row = r * CHUNK
        u = (dot(held[row : row + CHUNK, :], load) + fixed[row : row + CHUNK, :]).astype(BF16)
        if row < ms:
            um[row : row + CHUNK, :] = u
        else:
            us[row - ms : row - ms + CHUNK, :] = u
    if zt is None:
        return None
    both = dot(zt[:, :ms], um[...]) + dot(zt[:, ms:], us[...])
    return both[:24] + both[24:]


def loads_of(push, scaled, loads_m, loads_s):
    master = (-push.astype(F32) - loads_m.astype(F32)).astype(BF16)
    slave = (scaled - loads_s.astype(F32)).astype(BF16)
    return jnp.concatenate([master, slave], axis=0)


def pack_kernel(mortar, seg, field, modes, coarse, weights, cand, out, behind):
    ms = mortar.shape[0]
    nr = coarse.shape[0]
    rigid = rows_of(modes, nr)
    count = ms // TILE
    ids = seg[...].astype(F32)
    ids_col = column(ids)
    none = jnp.zeros((HALO, TILE), F32)

    def masked(low, high, t):
        own = slice(TILE * t, TILE * (t + 1))
        same = ids_col[low:high] == ids[:, own]
        return jnp.where(same, mortar[low:high, own].astype(F32), 0.0)

    tiles = []
    for t in range(count):
        low, high = TILE * t, TILE * (t + 1)
        middle = masked(low, high, t)
        above = masked(low - HALO, low, t) if t else none
        below = masked(high, high + HALO, t) if t + 1 < count else none
        out[160 * t : 160 * t + HALO, :] = (above + below).astype(BF16)
        out[160 * t + HALO : 160 * (t + 1), :] = middle.astype(BF16)
        tile = jnp.concatenate([middle, above, below], axis=0)
        tiles.append(with_fill(tile).T.astype(BF16))
    push = mortar_t_times(jnp.concatenate(tiles, axis=0), field[...].astype(BF16))
    out[160 * count : 160 * count + ms, :] = push.astype(BF16)

    behind[...] = jnp.zeros_like(behind)
    behind[0:nr, :] = rigid[:, :ms]
    behind[8 : 8 + nr, :] = coarse[...]
    for t in range(count):
        own = slice(TILE * t, TILE * (t + 1))
        chosen = jnp.zeros((1, TILE), F32)
        if TILE * (t + 1) <= cand.shape[1]:
            chosen = cand[:, own].astype(F32)
        lanes = slice(ms + TILE * t, ms + TILE * (t + 1))
        pad = jnp.zeros((8 - nr, TILE), F32)
        rows = [rigid[:, lanes], weights[:, own], chosen, coarse[:, own], pad]
        value = jnp.concatenate(rows, axis=0)
        high, low = halves(value)
        base = 160 * count + ms + 2 * SIDE * t
        out[base : base + SIDE, :] = high.astype(BF16)
        out[base + SIDE : base + 2 * SIDE, :] = low.astype(BF16)


def side_rows(pack_p, ms):
    count = ms // TILE
    out = []
    for t in range(count):
        base = 160 * count + ms + 2 * SIDE * t
        high = pack_p[base : base + SIDE, :].astype(F32)
        out.append(high + pack_p[base + SIDE : base + 2 * SIDE, :].astype(F32))
    return jnp.concatenate(out, axis=1)


def fixed_kernel(loads, kinv, out, held, sems):
    ms = loads.shape[0] // 3
    moves = Moves(sems)
    copies = []
    for r in range(2 * ms // CHUNK):
        row = r * CHUNK + (ms if r * CHUNK >= ms else 0)
        copies.append(
            moves.start(
                kinv.at[pl.ds(row, CHUNK), pl.ds(ms, ms)], held.at[pl.ds(r * CHUNK, CHUNK), :]
            )
        )
    for r, copy in enumerate(copies):
        copy.wait()
        out[r * CHUNK : (r + 1) * CHUNK, :] = -dot(
            held[r * CHUNK : (r + 1) * CHUNK, :], loads[ms : 2 * ms, :]
        )


def setup_kernel(*refs):
    names, results = 8, 11
    kinv = refs[names]
    far_outs = refs[names + 1 : names + 1 + results]
    rest = refs[names + 1 + results :]
    local, rest = rest[:names], rest[names:]
    outs, rest = rest[:results], rest[results:]
    held, rows, modes, modes_p, um, us, long, sems = rest
    pack_p, weights, rigid_row, side_n, pack, field, loads, fixed = local
    tiles_s, tiles_p, tiles_pt, side_p, zt, md, md_p, near, far, resid, klt = outs
    ms = weights.shape[1]
    nr = rigid_row.shape[1] // (2 * ms)
    odd = is_odd()
    count = ms // TILE
    span = TILE + 2 * HALO
    moves = Moves(sems)
    arrive = [moves.start(a, b) for a, b in zip(refs[:names], local)]
    copies = start_faces(moves, kinv, held, ms)
    leaving = []

    def wait(*which):
        for n in which:
            arrive[n].wait()

    def leave(*which):
        for n in which:
            leaving.append(moves.start(outs[n], far_outs[n]))

    wait(0)
    for t in range(count):
        tile = unpacked(pack_p, t)
        tiles_p[span * t : span * (t + 1), :] = tile.astype(BF16)
        tiles_pt[TILE * t : TILE * (t + 1), :] = with_fill(tile).T.astype(BF16)
    side_p[...] = side_rows(pack_p, ms)
    leave(1, 2, 3)

    wait(1, 2, 3, 4)
    rigid = rows_of(rigid_row, nr)
    for t in range(count):
        tiles_s[span * t : span * (t + 1), :] = unpacked(pack, t).astype(BF16)
    leave(0)

    def through(tiles, values):
        rows[...] = jnp.zeros_like(rows)
        high, low = halves(values)
        rows[0:nr, :] = high
        rows[8 : 8 + nr, :] = low
        moved = mortar_times(tiles, rows[...].T.astype(BF16)).T
        return moved[0:nr] + moved[8 : 8 + nr]

    modes[...] = jnp.zeros_like(modes)
    modes_p[...] = jnp.zeros_like(modes_p)
    modes[nr : 2 * nr, :] = rigid[:, ms:] * weights[...]
    modes[2 * nr : 3 * nr, :] = -through(tiles_s, side_n[0:nr, :])
    modes_p[0:nr, :] = side_p[0:nr, :] * side_p[6:7, :]
    modes_p[nr : 2 * nr, :] = -through(tiles_p, rigid[:, :ms])

    def placed(values):
        later = jnp.concatenate([values[18:24], values[0:18]], axis=0)
        return jnp.where(odd, later, values)

    def stacked(values):
        high, low = halves(values)
        rows[...] = jnp.zeros_like(rows)
        rows[0:24, :] = high
        rows[32:56, :] = low
        rows[64:88, :] = high
        return rows[...].T.astype(BF16)

    own = placed(modes[...])
    md[...] = stacked(own)
    columns = stacked(placed(modes_p[...]))
    md_p[...] = columns
    leave(5, 6)
    pushed = mortar_t_times(tiles_pt, columns).T
    high, low = halves(-(pushed[0:24] + pushed[32:56]))
    zt[0:24, :ms] = high.astype(BF16)
    zt[24:48, :ms] = low.astype(BF16)
    high, low = halves(own * weights[...])
    zt[0:24, ms:] = high.astype(BF16)
    zt[24:48, ms:] = low.astype(BF16)
    leave(4)
    push = pack_p[160 * count : 160 * count + ms, :]
    wait(5, 6, 7)
    scaled = column(weights[...]) * field[...]
    load = loads_of(push, scaled, loads[:ms, :], loads[2 * ms :, :])
    long[...] = jnp.zeros_like(long)
    long[0:24, :] = zt[0:24, :].astype(F32)
    long[32:56, :] = zt[24:48, :].astype(F32)
    values = jnp.concatenate([load, long[...].T.astype(BF16)], axis=1)
    for r, pair in enumerate(copies):
        for copy in pair:
            copy.wait()
        row = r * CHUNK
        part = dot(held[row : row + CHUNK, :], values)
        u = (part[:, :TILE] + fixed[row : row + CHUNK, :]).astype(BF16)
        if row < ms:
            um[row : row + CHUNK, :] = u
        else:
            us[row - ms : row - ms + CHUNK, :] = u
        long[:, row : row + CHUNK] = part[:, TILE:].T
    both = dot(zt[:, :ms], um[...]) + dot(zt[:, ms:], us[...])
    resid[...] = both[:24] + both[24:]
    near[...] = jnp.where(odd, um[...], us[...])
    far[...] = jnp.where(odd, us[...], um[...])
    leave(9, 8, 7)
    high, low = halves(long[0:24, :] + long[32:56, :])
    klt[0:24, :] = high.astype(BF16)
    klt[24:48, :] = low.astype(BF16)
    leave(10)
    for copy in leaving:
        copy.wait()


def coarse_rows(coarse, side_p, side_n, source, cand, out, floors, rows):
    nr, width = coarse.shape
    rows[...] = jnp.zeros_like(rows)
    rows[0:nr, :] = side_p[8 : 8 + nr, :]
    rows[nr : 2 * nr, :] = coarse[...]
    rows[2 * nr : 3 * nr, :] = side_n[8 : 8 + nr, :]
    later = jnp.concatenate([rows[18:24, :], rows[0:18, :]], axis=0)
    high, low = halves(jnp.where(is_odd(), later, rows[...]))
    both = jnp.concatenate([high, low], axis=0).astype(BF16)
    count = width // TILE
    for n in range(out.shape[1] // CHUNK):
        near_by = [(n + k) % count for k in (-1, 0, 1)]
        left = jnp.concatenate([both[:, TILE * t : TILE * (t + 1)] for t in near_by], axis=1)
        wanted = source[:, n * CHUNK : (n + 1) * CHUNK]
        picks = []
        for t in near_by:
            index = lax.broadcasted_iota(jnp.int32, (TILE, CHUNK), 0) + TILE * t
            picks.append(jnp.where(index == wanted, 1.0, 0.0).astype(BF16))
        out[:, n * CHUNK : (n + 1) * CHUNK] = dot(left, jnp.concatenate(picks, axis=0)).astype(
            BF16
        )

    floors[...] = jnp.zeros_like(floors)
    chosen = (cand[...].astype(F32), side_p[7:8, : cand.shape[1]])
    for t in range(floors.shape[1] // TILE):
        place = lax.broadcasted_iota(jnp.int32, (TILE, cand.shape[1]), 0) + TILE * t
        for n, which in enumerate(chosen):
            hit = jnp.where(place.astype(F32) == which, 1.0, 0.0)
            found = jnp.broadcast_to(jnp.max(hit, axis=1, keepdims=True), (TILE, TILE)).T
            floors[n : n + 1, TILE * t : TILE * (t + 1)] = jnp.where(
                found[0:1] > 0.0, 0.0, -jnp.inf
            )


def pair_kernel(resid, other, out):
    pair = (resid[...] + other[...]).astype(BF16)
    out[...] = jnp.broadcast_to(pair[None], out.shape)


def last_kernel(slave, um_n, tiles_s, grad):
    grad[...] = slave[...] - mortar_times(tiles_s, um_n[...])


def dot_rows(left, right):
    return lax.dot_general(left, right, (((1,), (1,)), ((), ())), preferred_element_type=F32)


def forms_kernel(
    zt, md, klt, coarse, side_p, side_n, source, cand, near,
    mrows, forms, coarse_of, floors,
    square, rows,
):
    del near
    ms = md.shape[0]
    coarse_rows(coarse, side_p, side_n, source, cand, coarse_of, floors, rows)
    mrows[...] = md[...].astype(F32).T[0:64].astype(BF16)

    def form(at, product):
        square[...] = jnp.zeros_like(square)
        square[0:24, 0:64] = product[0:24] + product[32:56]
        turned = square[...].T
        high, low = halves(turned[0:24] + turned[32:56])
        square[...] = jnp.zeros_like(square)
        square[0:24, :] = high
        square[32:56, :] = low
        square[64:88, :] = high
        forms[at : at + 24, :] = square[...].T[0:24].astype(BF16)

    gap = jnp.zeros((8, 2 * ms), BF16)
    left = jnp.concatenate([zt[0:24, :], gap, zt[24:48, :], gap], axis=0)
    right = jnp.concatenate([klt[0:24, :], gap, klt[24:48, :], gap], axis=0)
    form(0, dot_rows(mrows[...], mrows[...]))
    form(24, dot_rows(left, right))


def gradient_kernel(*refs):
    names = 12
    kinv, _, g_out, gp_out, stats = refs[names : names + 5]
    held = refs[names + 5]
    local = refs[names + 6 : 2 * names + 6]
    g, gp, solution, sems = refs[2 * names + 6 :]
    ms = g.shape[0]
    moves = Moves(sems)
    arrive = [moves.start(a, b) for a, b in zip(refs[:9], local[:9])]
    copies = start_faces(moves, kinv, held, ms)
    arrive += [moves.start(a, b) for a, b in zip(refs[9:names], local[9:])]
    weights, side_p, near, far, near_r, far_r, tiles_p, tiles_pt, tiles_s, mrows, zt, klt = local

    def wait(*which):
        for n in which:
            arrive[n].wait()

    wait(0, 1, 2, 3, 4, 5, 6)
    odd = is_odd()
    um, us = jnp.where(odd, near[...], far[...]), jnp.where(odd, far[...], near[...])
    um_n = jnp.where(odd, far_r[...], near_r[...])
    us_p = jnp.where(odd, near_r[...], far_r[...])
    wcol = column(weights[...])
    gp[...] = column(side_p[6:7, :]) * us_p.astype(F32) - mortar_times(tiles_p, um)
    out_p = moves.start(gp, gp_out)
    wait(7)
    master = (-mortar_t_times(tiles_pt, gp[...].astype(BF16))).astype(BF16)
    wait(8)
    g[...] = wcol * us.astype(F32) - mortar_times(tiles_s, um_n)
    out_s = moves.start(g, g_out)
    load = jnp.concatenate([master, (wcol * g[...]).astype(BF16)], axis=0)
    curve = jnp.zeros((CHUNK, TILE), F32)
    for r, pair in enumerate(copies):
        for copy in pair:
            copy.wait()
        row = r * CHUNK
        part = dot(held[row : row + CHUNK, :], load)
        solution[row : row + CHUNK, :] = part
        curve += load[row : row + CHUNK].astype(F32) * part
    wait(9, 10, 11)
    stats[...] = jnp.zeros_like(stats)
    stats[0:1, :] = jnp.sum(g[...] * g[...], axis=0, keepdims=True)
    stats[1:2, :] = jnp.sum(curve, axis=0, keepdims=True)
    high, low = halves(g[...])
    first = dot(mrows[...], high.astype(BF16))
    second = dot(mrows[0:32, :], low.astype(BF16))
    stats[8:32, :] = first[0:24] + first[32:56] + second[0:24]
    high, low = halves(solution[...])
    first = dot(zt[...], high.astype(BF16)) + dot(klt[...], load)
    second = dot(zt[0:32, :], low.astype(BF16))
    stats[32:56, :] = first[0:24] + first[24:48] + second[0:24]
    out_p.wait()
    out_s.wait()


def project_kernel(every, coarse, forms, stats, stack, sums):
    both = dot(coarse[...], every[...].reshape(coarse.shape[1], TILE))
    c = both[:24] + both[24:]
    high, low = halves(c)
    gap = jnp.zeros((8, TILE), F32)
    rest = jnp.zeros((TILE - 88, TILE), F32)
    operand = jnp.concatenate([high, gap, high, gap, low, rest], axis=0).astype(BF16)
    stack[...] = operand
    moved = dot(forms[...], operand)
    norm = stats[0:1, :] + jnp.sum(
        c * (moved[0:24] - 2.0 * stats[8:32, :]), axis=0, keepdims=True
    )
    curve = stats[1:2, :] + jnp.sum(c * (moved[24:48] - stats[32:56, :]), axis=0, keepdims=True)
    total = jnp.concatenate([norm, curve], axis=0)
    sums[...] = jnp.broadcast_to(total[None], sums.shape)


def direction_kernel(stack, g, gp, md, md_p, d, dp):
    d[...] = g[...] - dot(md[...], stack[...])
    dp[...] = gp[...] - dot(md_p[...], stack[...])


def marker_kernel(near, out):
    del near
    out[...] = jnp.zeros_like(out)


def step_kernel(final, *refs):
    names = 10
    loads, kinv = refs[names : names + 2]
    y_out, yp_out, near_out, far_out, resid_out = refs[names + 2 : names + 7]
    held = refs[names + 7]
    local = refs[names + 8 : 2 * names + 8]
    loads_m, loads_s, um, us, near, far, resid, sems = refs[2 * names + 8 :]
    weights, floors, sums, field_p, dp, tiles_pt, field, d, zt, fixed = local[:10]
    ms = d.shape[0]
    moves = Moves(sems)
    arrive = [moves.start(refs[n], local[n]) for n in range(8)]
    arrive_m = moves.start(loads.at[pl.ds(0, ms), :], loads_m)
    arrive_s = moves.start(loads.at[pl.ds(2 * ms, ms), :], loads_s)
    arrive += [moves.start(refs[n], local[n]) for n in range(8, 10)]
    copies = start_faces(moves, kinv, held, ms, 0, ms // CHUNK if final else None)

    def wait(*which):
        for n in which:
            arrive[n].wait()

    wait(0, 1)
    wcol = column(weights[...])
    floor, floor_p = column(floors[0:1, :]), column(floors[1:2, :])
    wait(2)
    total = jnp.sum(sums[...], axis=0)
    step = total[0:1] / total[1:2]
    wait(3, 4)
    field_p[...] = jnp.maximum(field_p[...] - step * dp[...], floor_p)
    out_p = None if final else moves.start(field_p, yp_out)
    wait(5)
    push = mortar_t_times(tiles_pt, field_p[...].astype(BF16)).astype(BF16)
    wait(6, 7)
    field[...] = jnp.maximum(field[...] - step * d[...], floor)
    out_s = moves.start(field, y_out)
    arrive_m.wait()
    arrive_s.wait()
    load = loads_of(push, wcol * field[...], loads_m[...], loads_s[...])
    wait(8, 9)
    if final:
        near[...] = load[:ms]
        far[...] = load[ms:]
        outs = [moves.start(near, near_out), moves.start(far, far_out)]
        solved(copies, held, load, fixed, None, um, us, ms)
        outs += [out_s, moves.start(um, yp_out)]
    else:
        solved(copies, held, load, fixed, None, um, us, ms)
        odd = is_odd()
        near[...] = jnp.where(odd, um[...], us[...])
        far[...] = jnp.where(odd, us[...], um[...])
        outs = [moves.start(far, far_out), moves.start(near, near_out)]
        both = dot(zt[:, :ms], um[...]) + dot(zt[:, ms:], us[...])
        resid[...] = both[:24] + both[24:]
        outs += [out_p, out_s, moves.start(resid, resid_out)]
    for copy in outs:
        copy.wait()


def slave_kernel(load_m, load_s, weights, fixed, kinv, out, held, us, sems):
    ms = weights.shape[1]
    copies = start_faces(Moves(sems), kinv, held, ms, ms // CHUNK)
    load = jnp.concatenate([load_m[...], load_s[...]], axis=0)
    solved(copies, held, load, fixed, None, None, us, ms, ms // CHUNK)
    out[...] = column(weights[...]) * us[...].astype(F32)


def shape(dims, dtype):
    return jax.ShapeDtypeStruct(dims, dtype)


def kernel_call(body, outs, *operands, anywhere=(), anywhere_out=(), scratch=(), flops=0):
    here = pl.BlockSpec(memory_space=pltpu.VMEM)
    far = pl.BlockSpec(memory_space=pl.ANY)
    moved = sum(int(np.prod(o.shape)) * o.dtype.itemsize for o in list(operands) + list(outs))
    return pl.pallas_call(
        body,
        out_shape=tuple(outs),
        in_specs=[far if n in anywhere else here for n in range(len(operands))],
        out_specs=tuple(far if n in anywhere_out else here for n in range(len(outs))),
        scratch_shapes=list(scratch),
        compiler_params=pltpu.CompilerParams(vmem_limit_bytes=64 * MIB),
        cost_estimate=pl.CostEstimate(flops=flops, bytes_accessed=moved, transcendentals=0),
    )(*operands)


def on_device(
    inverse_blocks,
    primal_loads,
    mortar_values,
    segment_ids,
    slave_weights,
    rigid_modes,
    coarse_inverse,
    candidates,
    start_multipliers,
):
    ms = mortar_values.shape[1]
    nr = rigid_modes.shape[1]
    nc = coarse_inverse.shape[1]
    lc = start_multipliers.shape[2]
    sub, grp = lax.axis_size("sub"), lax.axis_size("grp")
    chips = sub * grp // 2
    kinv = inverse_blocks[0]
    loads = primal_loads[0]
    rigid = rigid_modes.reshape(1, -1)
    field = start_multipliers[0]
    count = ms // TILE
    face = lambda dtype: shape((ms, lc), dtype)
    kff = pltpu.VMEM((2 * ms, 2 * ms), BF16)
    chunks = 2 * ms // CHUNK

    pack, behind = kernel_call(
        pack_kernel,
        [shape(((160 + 2 * SIDE) * count + ms, lc), BF16), shape((16, ms), F32)],
        mortar_values[0],
        segment_ids,
        field,
        rigid,
        coarse_inverse,
        slave_weights,
        candidates,
    )
    pack_p = shifted(pack, 1)
    side_n = shifted(behind, -1)
    field_p = shifted(field, 1)
    (fixed,) = kernel_call(
        fixed_kernel,
        [shape((2 * ms, lc), F32)],
        loads,
        kinv,
        anywhere=(1,),
        scratch=[pltpu.VMEM((2 * ms, ms), BF16), pltpu.SemaphoreType.DMA((chunks,))],
        flops=4 * ms * ms * lc,
    )
    outs = [
        shape((TILE_ROWS * count, TILE), BF16),
        shape((TILE_ROWS * count, TILE), BF16),
        shape((ms, 2 * TILE), BF16),
        shape((SIDE, ms), F32),
        shape((48, 2 * ms), BF16),
        face(BF16),
        face(BF16),
        face(BF16),
        face(BF16),
        shape((24, lc), F32),
        shape((48, 2 * ms), BF16),
    ]
    operands = (pack_p, slave_weights, rigid, side_n, pack, field, loads, fixed)
    (tiles_s, tiles_p, tiles_pt, side_p, zt, md, md_p, near, far, resid, klt) = kernel_call(
        setup_kernel,
        outs,
        *operands,
        kinv,
        anywhere=range(len(operands) + 1),
        anywhere_out=range(len(outs)),
        scratch=[pltpu.VMEM(o.shape, o.dtype) for o in operands]
        + [pltpu.VMEM(o.shape, o.dtype) for o in outs]
        + [
            kff,
            pltpu.VMEM((TILE, ms), F32),
            pltpu.VMEM((24, ms), F32),
            pltpu.VMEM((24, ms), F32),
            pltpu.VMEM((ms, lc), BF16),
            pltpu.VMEM((ms, lc), BF16),
            pltpu.VMEM((TILE, 2 * ms), F32),
            pltpu.SemaphoreType.DMA((len(operands) + len(outs) + 2 * chunks,)),
        ],
        flops=8 * ms * ms * lc,
    )

    chip, group, spot, mode = np.meshgrid(
        np.arange(sub // 2), np.arange(grp), np.arange(4), np.arange(nr), indexing="ij"
    )
    source = (((2 * chip + spot - 1) % sub) * grp + group) * nr + mode
    source = jnp.asarray(source.reshape(1, -1), jnp.int32)
    mrows, forms, coarse, floors = kernel_call(
        forms_kernel,
        [
            shape((64, ms), BF16),
            shape((48, TILE), BF16),
            shape((48, source.shape[1]), BF16),
            shape((8, ms), F32),
        ],
        zt,
        md,
        klt,
        coarse_inverse,
        side_p,
        side_n,
        source,
        candidates,
        near,
        anywhere=(8,),
        scratch=[pltpu.VMEM((TILE, TILE), F32), pltpu.VMEM((24, nc), F32)],
        flops=10**11,
    )

    same_core = [
        [(2 * m + core) * grp + z for m in range(sub // 2) for z in range(grp)]
        for core in range(2)
    ]
    for turn in range(STEPS):
        (pieces,) = kernel_call(
            pair_kernel, [shape((chips, 24, lc), BF16)], resid, swapped(resid)
        )
        every = lax.all_to_all(
            pieces, AXES, 0, 0, tiled=True, axis_index_groups=same_core
        )
        far_r = swapped_out(far)
        near_r = swapped(near)
        (marker,) = kernel_call(
            marker_kernel, [shape((8, TILE), F32)], near, anywhere=(0,), flops=10**12
        )
        operands = (
            slave_weights, side_p, near, far, near_r, far_r, tiles_p, tiles_pt, tiles_s,
            mrows, zt, klt,
        )
        g, g_p, stats = kernel_call(
            gradient_kernel,
            [face(F32), face(F32), shape((64, lc), F32)],
            *operands,
            kinv,
            marker,
            anywhere=range(len(operands) + 2),
            anywhere_out=(0, 1),
            scratch=[kff]
            + [pltpu.VMEM(o.shape, o.dtype) for o in operands]
            + [
                pltpu.VMEM((ms, lc), F32),
                pltpu.VMEM((ms, lc), F32),
                pltpu.VMEM((2 * ms, lc), F32),
                pltpu.SemaphoreType.DMA((len(operands) + 2 * chunks + 2,)),
            ],
            flops=8 * ms * ms * lc,
        )
        stack, sums = kernel_call(
            project_kernel,
            [shape((TILE, lc), BF16), shape((2 * chips, 2, lc), F32)],
            every, coarse, forms, stats,
            flops=2 * 48 * every.shape[0] * every.shape[1] * lc,
        )
        d, d_p = kernel_call(
            direction_kernel,
            [face(F32), face(F32)],
            stack, g, g_p, md, md_p,
            flops=4 * ms * TILE * lc,
        )
        totals = lax.all_to_all(sums, AXES, 0, 0, tiled=True)
        operands = (
            slave_weights, floors, totals, field_p, d_p, tiles_pt, field, d, zt, fixed,
        )
        final = turn == STEPS - 1
        field, field_p, near, far, resid = kernel_call(
            functools.partial(step_kernel, final),
            [
                face(F32),
                face(BF16 if final else F32),
                face(BF16),
                face(BF16),
                shape((24, lc), F32),
            ],
            *operands,
            loads,
            kinv,
            anywhere=range(len(operands) + 2),
            anywhere_out=(0, 1, 2, 3, 4),
            scratch=[kff]
            + [pltpu.VMEM(o.shape, o.dtype) for o in operands]
            + [pltpu.VMEM((ms, lc), BF16)] * 6
            + [
                pltpu.VMEM((24, lc), F32),
                pltpu.SemaphoreType.DMA((len(operands) + 2 * chunks + 7,)),
            ],
            flops=8 * ms * ms * lc,
        )
    um_n = shifted(field_p, -1)
    (slave,) = kernel_call(
        slave_kernel,
        [face(F32)],
        near, far, slave_weights, fixed, kinv,
        anywhere=(4,),
        scratch=[kff, pltpu.VMEM((ms, lc), BF16), pltpu.SemaphoreType.DMA((chunks,))],
        flops=10**11,
    )
    (gradient,) = kernel_call(
        last_kernel, [face(F32)], slave, um_n, tiles_s, flops=2 * 192 * ms * lc
    )
    return (field[None], gradient[None])


def solution(mesh):
    placed = (
        P(AXES, None, None),
        P(AXES, None, None),
        P(AXES, None, None),
        P(AXES, None),
        P(AXES, None),
        P(AXES, None, None),
        P(AXES, None),
        P(AXES, None),
        P(AXES, None, None),
    )
    return jax.shard_map(
        on_device,
        mesh=mesh,
        in_specs=placed,
        out_specs=(P(AXES, None, None), P(AXES, None, None)),
        check_vma=False,
    )
```
